32 devices in a mesh: seq: 16 (over z, y, x), exp: 2 (over core).
Axes of the slice: x: 2, y: 2, z: 4, core: 2. Of those that a mesh axis runs over, the one named last changes fastest.
Arguments:
- queries: bfloat16 [4096, 1024], P('seq', 'exp'), may hold values from -170 to 170
- keys: bfloat16 [4096, 1024], P('seq', 'exp'), may hold values from -5 to 5
- values: bfloat16 [4096, 1024], P('seq', 'exp'), may hold values from -6 to 6
- resid: bfloat16 [4096, 2048], P(('seq', 'exp')), may hold values from -6 to 6
- pair_ids: int32 [4096], replicated, may hold values from 0 to 15, never falling along the last dimension, each value on 1 to 512 neighbouring positions
- out_weight: bfloat16 [1024, 2048], P('exp'), may hold values from -0.1875 to 0.1875
- norm_gain: float32 [2048], replicated, may hold values from 0.5 to 1.5
- experts: int32 [4096, 6], P(('seq', 'exp')), may hold values from 0 to 15, all different within a row; in each aligned block of 128 rows (0 to 127, 128 to 255, ...) at most 96 rows name the same one
- gates: float32 [4096, 6], P(('seq', 'exp')), may hold values from 0.05 to 0.5
- w_gate: bfloat16 [16, 2048, 704], P('seq', None, 'exp'), may hold values from -0.125 to 0.125
- w_up: bfloat16 [16, 2048, 704], P('seq', None, 'exp'), may hold values from -0.125 to 0.125
- w_down: bfloat16 [16, 704, 2048], P('seq', 'exp'), may hold values from -0.21875 to 0.21875
Outputs:
- mixed: bfloat16 [4096, 2048], P(('seq', 'exp'))
The draws below stay inside these ranges and needn't reach their ends.
Inputs may be any that keep to these rules, and one draw needn't show every extreme that they name: In the aligned blocks of 128 rows no expert is named more than 96 times, a bound that some block reaches; each row names 6 different experts. `pair_ids`: pair numbers never fall along the sequence; each pair has 1 to 512 tokens, one exactly that many.
All inputs are finite; a program needn't handle non-finite values.
Results may differ from the reference program's by a relative error of at most 0.012.
Values may be sent and summed in bfloat16 or wider, within the bound.
No kernel may reach another device: no remote copies, remote signals or barrier semaphores. Data moves between devices by JAX's collectives and lax.ppermute only.
A program may use at most 128 MiB of HBM per device.

```python
import math
import jax
import jax.numpy as jnp
import numpy as np
from jax import lax

D = 2048
HEADS = 8
HD = 128
FF = 704
TOP = 6
TOK_DEV = 256
EXPERTS = 16
TOKENS = 4096
WIN = 256
MOE_ROWS = 128
CAP = 96


def query_key_pair(key):
    base = jax.random.fold_in(key, 7101)
    width = HEADS * HD
    key_draw = jnp.clip(jax.random.normal(jax.random.fold_in(base, 1), (TOKENS, width), jnp.float32), -4.0, 4.0)
    query_draw = jnp.clip(jax.random.normal(jax.random.fold_in(base, 2), (TOKENS, width), jnp.float32), -4.0, 4.0)
    return (query_draw, key_draw)


def draw_queries(key, part):
    return query_key_pair(key)[0].astype(jnp.bfloat16)


def draw_keys(key, part):
    return query_key_pair(key)[1].astype(jnp.bfloat16)


def block_levels(stream_key, shape, pieces, low, high):
    factor_of, own = 1.0, jax.random.fold_in(stream_key, 6)
    for dim, blocks in pieces:
        heights = jnp.exp(jax.random.uniform(jax.random.fold_in(own, dim), (blocks,), jnp.float32, low / len(pieces), high / len(pieces)))
        factor_of = factor_of * jnp.repeat(heights, shape[dim] // blocks).reshape([-1 if axis == dim else 1 for axis in range(len(shape))])
    return factor_of


def split_up(number_of, total, reach, slope):
    loads = [(1 << 20) // math.isqrt(rank ** slope) + 1 for rank in range(2, number_of + 1)]
    rest, given = total - reach - (number_of - 1), [1] * (number_of - 1)
    while rest > 0:
        candidates = [i for i in range(number_of - 1) if given[i] < reach]
        mass, remaining = sum([loads[i] for i in candidates]), rest
        for i in candidates:
            extra = min(reach - given[i], max(1, remaining * loads[i] // mass), rest)
            given[i] = given[i] + extra
            rest = rest - extra
    return np.array([reach] + given)


def uneven(stream_key, amount, total, reach, lean):
    if amount == 2:
        one = jax.random.randint(stream_key, (), max(1, total - reach), min(reach, total - 1) + 1)
        return jnp.stack([one, total - one])
    lengths = jnp.asarray(split_up(amount, total, reach, lean), jnp.int32)
    pairs = (amount - 1) // 2
    giver, sink = lengths[1:1 + 2 * pairs:2], lengths[2:2 + 2 * pairs:2]
    margin = jnp.minimum(giver - 1, reach - sink)
    moved = jax.random.randint(jax.random.fold_in(stream_key, 1), (pairs,), 0, 1 << 20) % (margin + 1)
    lengths = lengths.at[1:1 + 2 * pairs:2].set(giver - moved).at[2:2 + 2 * pairs:2].set(sink + moved)
    return lengths[jax.random.permutation(jax.random.fold_in(stream_key, 2), amount)]


def assign_block(key, own, number, rows, count, top, limit, skew):
    sequence = jax.random.permutation(key, count)
    heavy_load, usual = portions_of(count, rows * top, limit, skew, True), portions_of(count, rows * top, limit, skew, False)
    places = jnp.arange(count)

    def named(sizes, rotation):
        used = int((sizes > 0).sum())
        fixed = max(1, used // 4)
        shifted = fixed + (places - fixed + rotation * (used - fixed)) % max(1, count - fixed)
        return jnp.zeros((count,), jnp.int32).at[sequence[jnp.where(places < fixed, places, shifted)]].set(jnp.asarray(sizes, jnp.int32))

    sizes = jnp.where(number % 4 == 0, named(heavy_load, number // 4), named(usual, number - number // 4 - 1))
    mixed = jax.random.permutation(jax.random.fold_in(own, 3), count)
    donor, receiver = mixed[0:count // 2 * 2:2], mixed[1:count // 2 * 2:2]
    room = jnp.minimum(sizes[donor] - 1, limit - sizes[receiver]) // 2
    room = jnp.where((donor == sequence[0]) | (receiver == sequence[0]) | (sizes[receiver] == 0), 0, jnp.maximum(room, 0))
    shifted = jax.random.randint(jax.random.fold_in(own, 4), (count // 2,), 0, 1 << 20) % (room + 1)
    sizes = sizes.at[donor].add(-shifted).at[receiver].add(shifted)
    labels = jnp.searchsorted(jnp.cumsum(sizes), jnp.arange(rows * top), side="right").astype(jnp.int32)
    grid = labels.reshape(top, rows).T
    grid = grid[jax.random.permutation(jax.random.fold_in(own, 1), rows)]
    rotation = jax.random.randint(jax.random.fold_in(own, 2), (rows, 1), 0, top)
    return jnp.take_along_axis(grid, (jnp.arange(top)[None, :] + rotation) % top, axis=1)


def portions_of(count, total, limit, lean, full):
    loads = [(1 << 20) // math.isqrt(grade ** lean) + 1 for grade in range(1, count + 1)]
    largest = limit if full else min(limit, max(-(-total // count), total * loads[0] // sum(loads)))
    least = 1 if total - largest >= count - 1 else 0
    given, surplus = [largest] + [least] * (count - 1), total - largest - least * (count - 1)
    while surplus > 0:
        free = [i for i in range(1, count) if given[i] < largest] or [i for i in range(1, count) if given[i] < limit]
        mass, budget = sum([loads[i] for i in free]), surplus
        for i in free:
            extra = min(limit - given[i], max(1, budget * loads[i] // mass), surplus)
            given[i] = given[i] + extra
            surplus = surplus - extra
    return np.array(given)


def gaussian(stream_key, dims, spread, limit, split=(), kind=jnp.bfloat16):
    values = spread * jax.random.normal(stream_key, dims, jnp.float32)
    if split:
        values = values * block_levels(stream_key, dims, split, -0.22, 0.18)
    return jnp.clip(values, -limit, limit).astype(kind)


def setup_inputs(seed: int = 0) -> dict:
    splits = jax.random.split(jax.random.key(seed), 13)
    queries = draw_queries(jax.random.fold_in(splits[12], 71), 0)
    keys = draw_keys(jax.random.fold_in(splits[12], 71), 0)
    values = gaussian(splits[2], (TOKENS, HEADS * HD), 1.0, 6.0, ((0, 16), (1, 2)))
    resid = gaussian(splits[3], (TOKENS, D), 1.0, 6.0, ((0, 32),))
    pair_ids = jnp.searchsorted(jnp.cumsum(uneven(splits[4], TOKENS // TOK_DEV, TOKENS, 2 * TOK_DEV, 2)), jnp.arange(TOKENS), side="right").astype(jnp.int32)
    out_weight = gaussian(splits[5], (HEADS * HD, D), (HEADS * HD) ** -0.5, 0.1875, ((0, 2),))
    norm_gain = jnp.clip(1.0 + 0.1 * jax.random.normal(splits[6], (D,), jnp.float32), 0.5, 1.5)
    experts_keys = jax.random.split(jax.random.fold_in(splits[7], 1), TOKENS // MOE_ROWS)
    experts_turns = jax.random.permutation(jax.random.fold_in(splits[7], 3), TOKENS // MOE_ROWS)
    experts = jax.vmap(lambda own, number: assign_block(jax.random.fold_in(splits[7], 2), own, number, MOE_ROWS, EXPERTS, TOP, CAP, 2))(experts_keys, experts_turns).reshape((TOKENS, TOP))
    gates = jnp.clip(0.05 + 0.45 * jax.random.uniform(splits[8], (TOKENS, TOP), jnp.float32) ** block_levels(splits[8], (TOKENS, TOP), ((0, 32),), -0.2, 0.2), 0.05, 0.5)
    w_gate = gaussian(splits[9], (EXPERTS, D, FF), D ** -0.5, 0.125, ((0, 16), (2, 2)))
    w_up = gaussian(splits[10], (EXPERTS, D, FF), D ** -0.5, 0.125, ((0, 16), (2, 2)))
    w_down = gaussian(splits[11], (EXPERTS, FF, D), FF ** -0.5, 0.21875, ((0, 16), (1, 2)))
    return {"queries": queries, "keys": keys, "values": values, "resid": resid, "pair_ids": pair_ids, "out_weight": out_weight, "norm_gain": norm_gain, "experts": experts, "gates": gates, "w_gate": w_gate, "w_up": w_up, "w_down": w_down}


def attend(query_block, key_block, value_block, query_ids, key_ids, query_pos, key_pos):
    rows = query_block.shape[0]
    span = key_block.shape[0]
    qh = query_block.astype(jnp.float32).reshape(rows, HEADS, HD)
    kh = key_block.astype(jnp.float32).reshape(span, HEADS, HD)
    vh = value_block.astype(jnp.float32).reshape(span, HEADS, HD)
    score = jnp.einsum('qhd,khd->hqk', qh, kh) / math.sqrt(HD)
    allowed = (query_ids[:, None] == key_ids[None, :]) & (jnp.abs(query_pos[:, None] - key_pos[None, :]) < WIN)
    score = jnp.where(allowed[None], score, -jnp.inf)
    top = lax.optimization_barrier(jnp.max(score, axis=-1, keepdims=True))
    weights = jnp.exp(score - top)
    probs = (weights / lax.optimization_barrier(jnp.sum(weights, axis=-1, keepdims=True))).astype(jnp.bfloat16)
    outcome = jnp.einsum('hqk,khd->qhd', probs.astype(jnp.float32), vh)
    return outcome.reshape(rows, HEADS * HD).astype(jnp.bfloat16)

def reference(queries, keys, values, resid, pair_ids, out_weight, norm_gain, experts, gates, w_gate, w_up, w_down):
    key_pad = jnp.pad(keys, ((WIN, WIN), (0, 0)))
    value_pad = jnp.pad(values, ((WIN, WIN), (0, 0)))
    id_pad = jnp.pad(pair_ids, (WIN, WIN), constant_values=-1)

    def block(index):
        start = index * TOK_DEV
        query_block = lax.dynamic_slice_in_dim(queries, start, TOK_DEV, 0)
        key_block = lax.dynamic_slice_in_dim(key_pad, start, TOK_DEV + 2 * WIN, 0)
        value_block = lax.dynamic_slice_in_dim(value_pad, start, TOK_DEV + 2 * WIN, 0)
        query_ids = lax.dynamic_slice_in_dim(pair_ids, start, TOK_DEV, 0)
        key_ids = lax.dynamic_slice_in_dim(id_pad, start, TOK_DEV + 2 * WIN, 0)
        query_pos = jnp.arange(TOK_DEV, dtype=jnp.int32) + WIN
        key_pos = jnp.arange(TOK_DEV + 2 * WIN, dtype=jnp.int32)
        return attend(query_block, key_block, value_block, query_ids, key_ids, query_pos, key_pos)
    attended = lax.map(block, jnp.arange(TOKENS // TOK_DEV, dtype=jnp.int32)).reshape(TOKENS, HEADS * HD)
    stream = resid.astype(jnp.float32) + jnp.dot(attended, out_weight, preferred_element_type=jnp.float32)
    meansq = lax.optimization_barrier(jnp.mean(stream * stream, axis=-1, keepdims=True))
    normed = (stream * lax.rsqrt(meansq + 1e-05) * norm_gain).astype(jnp.bfloat16)
    flat_experts = experts.reshape(-1).astype(jnp.int32)
    flat_gates = gates.reshape(-1)
    order = jnp.argsort(flat_experts, stable=True).astype(jnp.int32)
    counts = lax.optimization_barrier(jnp.sum((flat_experts[:, None] == jnp.arange(EXPERTS, dtype=jnp.int32)[None, :]).astype(jnp.int32), axis=0))
    starts = (jnp.cumsum(counts) - counts).astype(jnp.int32)
    bound = TOKENS // MOE_ROWS * CAP
    order_pad = jnp.concatenate([order, jnp.zeros((bound,), jnp.int32)])

    def per_expert(total, expert):
        picks = lax.dynamic_slice_in_dim(order_pad, starts[expert], bound, 0)
        valid = jnp.arange(bound, dtype=jnp.int32) < counts[expert]
        token_rows = picks // TOP
        inputs = normed[token_rows]
        gate_part = jnp.dot(inputs, w_gate[expert], preferred_element_type=jnp.float32)
        up_part = jnp.dot(inputs, w_up[expert], preferred_element_type=jnp.float32)
        act = (jax.nn.silu(gate_part) * up_part).astype(jnp.bfloat16)
        result = jnp.dot(act, w_down[expert], preferred_element_type=jnp.float32).astype(jnp.bfloat16)
        weight = jnp.where(valid, flat_gates[picks], jnp.zeros((), flat_gates.dtype))
        total = total.at[token_rows].add(result.astype(jnp.float32) * weight[:, None])
        return (total, None)
    mixture, unused = lax.scan(per_expert, jnp.zeros((TOKENS, D), jnp.float32), jnp.arange(EXPERTS, dtype=jnp.int32))
    return (stream + mixture).astype(jnp.bfloat16)
```

```python
import math

import jax
import jax.numpy as jnp
from jax import lax
from jax.sharding import PartitionSpec as P

HD = 128
TOP = 6
SWAP = [(0, 1), (1, 0)]


def with_halo(cells, width):
    count = lax.axis_size("seq")
    ends = count - 1
    before = lax.ppermute(cells, "seq", [(i, i + 1) for i in range(ends)])
    after = lax.ppermute(cells, "seq", [(i + 1, i) for i in range(ends)])
    return jnp.concatenate([before, cells, after], axis=1)


def both_halves(part, core, axis):
    other = lax.ppermute(part, "exp", SWAP)
    low = jnp.where(core == 0, part, other)
    high = jnp.where(core == 0, other, part)
    return jnp.concatenate([low, high], axis=axis)


def shards(
    queries,
    keys,
    values,
    resid,
    pair_ids,
    out_weight,
    norm_gain,
    experts,
    gates,
    w_gate,
    w_up,
    w_down,
):
    tok_rows = queries.shape[0]
    local_width = queries.shape[1]
    local_heads = local_width // HD
    moe_rows = resid.shape[0]
    shard = lax.axis_index("seq")
    core = lax.axis_index("exp")
    widened = with_halo(jnp.stack([keys, values]), tok_rows)
    n_experts = lax.axis_size("seq")
    per_expert = jnp.sum(
        jnp.where(
            experts[:, :, None] == jnp.arange(n_experts, dtype=jnp.int32)[None, None, :],
            gates[:, :, None],
            0.0,
        ),
        axis=1,
    )
    all_gates = lax.all_gather(per_expert, "seq", axis=0, tiled=True)
    my_gate = lax.dynamic_slice_in_dim(all_gates, shard, 1, 1)
    out_other = lax.ppermute(out_weight, "exp", SWAP)
    gate_w = both_halves(w_gate[0], core, 1)
    up_w = both_halves(w_up[0], core, 1)
    down_w = both_halves(w_down[0], core, 0)

    id_pad = jnp.pad(pair_ids, (tok_rows, tok_rows), constant_values=-1)
    key_ids = lax.dynamic_slice_in_dim(id_pad, shard * tok_rows, 3 * tok_rows, 0)
    query_ids = lax.dynamic_slice_in_dim(id_pad, shard * tok_rows + tok_rows, tok_rows, 0)
    query_pos = jnp.arange(tok_rows, dtype=jnp.int32) + tok_rows
    key_pos = jnp.arange(3 * tok_rows, dtype=jnp.int32)
    allowed = (query_ids[:, None] == key_ids[None, :]) & (
        jnp.abs(query_pos[:, None] - key_pos[None, :]) < tok_rows
    )
    query_heads = queries.reshape(tok_rows, local_heads, HD)
    key_heads = widened[0].reshape(3 * tok_rows, local_heads, HD)
    value_heads = widened[1].reshape(3 * tok_rows, local_heads, HD)
    score = jnp.einsum(
        "qhd,khd->hqk", query_heads, key_heads, preferred_element_type=jnp.float32
    ) / math.sqrt(HD)
    score = jnp.where(allowed[None], score, -jnp.inf)
    top = jnp.max(score, axis=-1, keepdims=True)
    weights = jnp.exp(score - top)
    probs = (weights / jnp.sum(weights, axis=-1, keepdims=True)).astype(jnp.bfloat16)
    attended = jnp.einsum("hqk,khd->qhd", probs, value_heads, preferred_element_type=jnp.float32)
    attended = attended.reshape(tok_rows, local_width).astype(jnp.bfloat16)
    mine = lax.dynamic_slice_in_dim(attended, core * moe_rows, moe_rows, 0)
    theirs = lax.dynamic_slice_in_dim(attended, (1 - core) * moe_rows, moe_rows, 0)
    received = lax.ppermute(theirs, "exp", SWAP)
    projected = jnp.dot(mine, out_weight, preferred_element_type=jnp.float32) + jnp.dot(
        received, out_other, preferred_element_type=jnp.float32
    )
    stream = resid.astype(jnp.float32) + projected
    meansq = jnp.mean(stream * stream, axis=-1, keepdims=True)
    normed = (stream * lax.rsqrt(meansq + 1e-05) * norm_gain).astype(jnp.bfloat16)

    group = lax.all_gather(normed, "seq", axis=0, tiled=True)
    gate_part = jnp.dot(group, gate_w, preferred_element_type=jnp.float32)
    up_part = jnp.dot(group, up_w, preferred_element_type=jnp.float32)
    act = (jax.nn.silu(gate_part) * up_part).astype(jnp.bfloat16)
    result = jnp.dot(act, down_w, preferred_element_type=jnp.float32) * my_gate
    mixture = lax.psum_scatter(
        result.astype(jnp.bfloat16), "seq", scatter_dimension=0, tiled=True
    )
    return (stream + mixture.astype(jnp.float32)).astype(jnp.bfloat16)


def solution(mesh):
    in_specs = (
        P("seq", "exp"),
        P("seq", "exp"),
        P("seq", "exp"),
        P(("seq", "exp"), None),
        P(),
        P("exp", None),
        P(),
        P(("seq", "exp"), None),
        P(("seq", "exp"), None),
        P("seq", None, "exp"),
        P("seq", None, "exp"),
        P("seq", "exp", None),
    )
    out_specs = P(("seq", "exp"), None)
    return jax.shard_map(shards, mesh=mesh, in_specs=in_specs, out_specs=out_specs, check_vma=False)
```

```python
import math

import jax
import jax.numpy as jnp
from jax import lax
from jax.sharding import PartitionSpec as P

HD = 128
TOP = 6
SWAP = [(0, 1), (1, 0)]


def with_halo(cells, width):
    count = lax.axis_size("seq")
    ends = count - 1
    before = lax.ppermute(cells, "seq", [(i, i + 1) for i in range(ends)])
    after = lax.ppermute(cells, "seq", [(i + 1, i) for i in range(ends)])
    return jnp.concatenate([before, cells, after], axis=1)


def flip(block, mask):
    count = lax.axis_size("seq")
    return lax.ppermute(block, "seq", [(i, i ^ mask) for i in range(count)])


def gather_small(block):
    mask = 1
    while mask < lax.axis_size("seq"):
        block = jnp.concatenate([block, flip(block, mask)], axis=0)
        mask *= 2
    return block


def expert(tokens, weight, gate_up, down):
    hidden = lax.dot_general(
        tokens, gate_up, (((1,), (1,)), ((), ())), preferred_element_type=jnp.float32
    )
    units = down.shape[0]
    act = (jax.nn.silu(hidden[:, :units]) * hidden[:, units:]).astype(jnp.bfloat16)
    result = jnp.dot(act, down, preferred_element_type=jnp.float32)
    return (result * weight).astype(jnp.bfloat16)


def plane_gather(block):
    half = block.shape[1] // 2
    beside_x = flip(block, 1)
    beside_y = flip(block, 2)
    left = flip(beside_x[:, :half], 2)
    right = flip(beside_y[:, half:], 1)
    return [block, beside_x, beside_y, jnp.concatenate([left, right], axis=1)]


def add(*terms):
    total = terms[0].astype(jnp.float32)
    for term in terms[1:]:
        total = total + term.astype(jnp.float32)
    return total


def plane_scatter(own, for_x, for_y, for_both):
    half = own.shape[1] // 2
    left = flip(for_both[:, :half], 2)
    right = flip(for_both[:, half:], 1)
    for_x = jnp.concatenate([add(for_x[:, :half], left).astype(jnp.bfloat16), for_x[:, half:]], axis=1)
    for_y = jnp.concatenate([for_y[:, :half], add(for_y[:, half:], right).astype(jnp.bfloat16)], axis=1)
    return add(own, flip(for_x, 1), flip(for_y, 2))


def expert_layer(normed, weights, gate_up, down):
    count = lax.axis_size("seq")
    rows = normed.shape[0]

    def run(blocks, first):
        tokens = jnp.concatenate(blocks, axis=0)
        part = weights[first * rows : first * rows + tokens.shape[0]]
        result = expert(tokens, part, gate_up, down)
        return [result[i * rows : (i + 1) * rows] for i in range(len(blocks))]

    if count == 16:
        layers = [normed] + [flip(normed, 4 * k) for k in range(1, 4)]
        gathered = [plane_gather(layer) for layer in layers]
        results = [run(blocks, 4 * k) for k, blocks in enumerate(gathered)]
        sums = [plane_scatter(*result) for result in results]
        return add(sums[0], *[flip(sums[k].astype(jnp.bfloat16), 4 * k) for k in range(1, 4)])
    blocks, mask = [normed], 1
    while mask < count:
        blocks = blocks + [flip(block, mask) for block in blocks]
        mask *= 2
    step = 8
    parts = []
    for first in range(0, count, step):
        parts += run(blocks[first : first + step], first)
    while mask > 1:
        mask //= 2
        parts = [add(parts[i], flip(parts[i + mask], mask)).astype(jnp.bfloat16) for i in range(mask)]
    return add(parts[0])


def shards(
    queries,
    keys,
    values,
    resid,
    pair_ids,
    out_weight,
    norm_gain,
    experts,
    gates,
    w_gate,
    w_up,
    w_down,
):
    tok_rows = queries.shape[0]
    local_width = queries.shape[1]
    local_heads = local_width // HD
    moe_rows = resid.shape[0]
    shard = lax.axis_index("seq")
    core = lax.axis_index("exp")
    widened = with_halo(jnp.stack([keys, values]), tok_rows)
    n_experts = lax.axis_size("seq")
    per_expert = jnp.sum(
        jnp.where(
            experts[:, :, None] == jnp.arange(n_experts, dtype=jnp.int32)[None, None, :],
            gates[:, :, None],
            0.0,
        ),
        axis=1,
    )
    all_gates = gather_small(per_expert)
    my_gate = lax.dynamic_slice_in_dim(all_gates, shard, 1, 1)
    out_other = lax.ppermute(out_weight, "exp", SWAP)
    own_up = jnp.swapaxes(w_up[0], 0, 1)
    own_gate = jnp.swapaxes(w_gate[0], 0, 1)
    units = own_gate.shape[0]
    own = jnp.concatenate([own_gate, own_up, w_down[0]], axis=0)
    other = lax.ppermute(own, "exp", SWAP)
    gate_up = jnp.concatenate(
        [own_gate, other[:units], own_up, other[units : 2 * units]], axis=0
    )
    down = jnp.concatenate([w_down[0], other[2 * units :]], axis=0)

    id_pad = jnp.pad(pair_ids, (tok_rows, tok_rows), constant_values=-1)
    key_ids = lax.dynamic_slice_in_dim(id_pad, shard * tok_rows, 3 * tok_rows, 0)
    query_ids = lax.dynamic_slice_in_dim(id_pad, shard * tok_rows + tok_rows, tok_rows, 0)
    query_pos = jnp.arange(tok_rows, dtype=jnp.int32) + tok_rows
    key_pos = jnp.arange(3 * tok_rows, dtype=jnp.int32)
    allowed = (query_ids[:, None] == key_ids[None, :]) & (
        jnp.abs(query_pos[:, None] - key_pos[None, :]) < tok_rows
    )
    query_heads = queries.reshape(tok_rows, local_heads, HD)
    key_heads = widened[0].reshape(3 * tok_rows, local_heads, HD)
    value_heads = widened[1].reshape(3 * tok_rows, local_heads, HD)
    score = jnp.einsum(
        "qhd,khd->hqk", query_heads, key_heads, preferred_element_type=jnp.float32
    ) / math.sqrt(HD)
    score = jnp.where(allowed[None], score, -jnp.inf)
    top = jnp.max(score, axis=-1, keepdims=True)
    weights = jnp.exp(score - top)
    probs = (weights / jnp.sum(weights, axis=-1, keepdims=True)).astype(jnp.bfloat16)
    attended = jnp.einsum("hqk,khd->qhd", probs, value_heads, preferred_element_type=jnp.float32)
    attended = attended.reshape(tok_rows, local_width).astype(jnp.bfloat16)
    mine = lax.dynamic_slice_in_dim(attended, core * moe_rows, moe_rows, 0)
    theirs = lax.dynamic_slice_in_dim(attended, (1 - core) * moe_rows, moe_rows, 0)
    received = lax.ppermute(theirs, "exp", SWAP)
    projected = jnp.dot(mine, out_weight, preferred_element_type=jnp.float32) + jnp.dot(
        received, out_other, preferred_element_type=jnp.float32
    )
    stream = resid.astype(jnp.float32) + projected
    meansq = jnp.mean(stream * stream, axis=-1, keepdims=True)
    normed = (stream * lax.rsqrt(meansq + 1e-05) * norm_gain).astype(jnp.bfloat16)

    mixture = expert_layer(normed, my_gate, gate_up, down)
    return (stream + mixture).astype(jnp.bfloat16)


def solution(mesh):
    in_specs = (
        P("seq", "exp"),
        P("seq", "exp"),
        P("seq", "exp"),
        P(("seq", "exp"), None),
        P(),
        P("exp", None),
        P(),
        P(("seq", "exp"), None),
        P(("seq", "exp"), None),
        P("seq", None, "exp"),
        P("seq", None, "exp"),
        P("seq", "exp", None),
    )
    out_specs = P(("seq", "exp"), None)
    return jax.shard_map(shards, mesh=mesh, in_specs=in_specs, out_specs=out_specs, check_vma=False)
```

```python
import functools
import math

import jax
import jax.numpy as jnp
from jax import lax
from jax.experimental import pallas as pl
from jax.experimental.pallas import tpu as pltpu
from jax.sharding import PartitionSpec as P

HD = 128
SWAP = [(0, 1), (1, 0)]
VMEM = pl.BlockSpec(memory_space=pltpu.VMEM)
ANY = pl.BlockSpec(memory_space=pl.ANY)
NT = (((1,), (1,)), ((), ()))


def flip(block, mask):
    count = lax.axis_size("seq")
    return lax.ppermute(block, "seq", [(i, i ^ mask) for i in range(count)])


def gather_small(block):
    mask = 1
    while mask < lax.axis_size("seq"):
        block = jnp.concatenate([block, flip(block, mask)], axis=0)
        mask *= 2
    return block


def attention_kernel(q_ref, own_ref, before_ref, after_ref, qid_ref, kid_ref, _0, _1, _2, _3, out_ref):
    rows = q_ref.shape[0]
    query_pos = lax.broadcasted_iota(jnp.int32, (rows, 3 * rows), 0) + rows
    key_pos = lax.broadcasted_iota(jnp.int32, (rows, 3 * rows), 1)
    allowed = (qid_ref[...] == kid_ref[...]) & (jnp.abs(query_pos - key_pos) < rows)
    for head in range(q_ref.shape[1] // HD):
        cols = slice(head * HD, (head + 1) * HD)
        query = q_ref[:, cols]
        score = jnp.concatenate(
            [
                lax.dot_general(query, ref[:rows, cols], NT, preferred_element_type=jnp.float32)
                for ref in (before_ref, own_ref, after_ref)
            ],
            axis=1,
        ) / math.sqrt(HD)
        score = jnp.where(allowed, score, -jnp.inf)
        weights = jnp.exp(score - jnp.max(score, axis=-1, keepdims=True))
        probs = (weights / jnp.sum(weights, axis=-1, keepdims=True)).astype(jnp.bfloat16)
        total = jnp.zeros((rows, HD), jnp.float32)
        for place, ref in enumerate((before_ref, own_ref, after_ref)):
            total += jnp.dot(
                probs[:, place * rows : (place + 1) * rows],
                ref[rows:, cols],
                preferred_element_type=jnp.float32,
            )
        out_ref[:, cols] = total.astype(jnp.bfloat16)


def attention(queries, own, before, after, query_ids, key_ids, *ahead):
    rows, width = queries.shape
    return pl.pallas_call(
        attention_kernel,
        out_shape=jax.ShapeDtypeStruct(queries.shape, jnp.bfloat16),
        in_specs=[VMEM] * 6 + [ANY] * len(ahead),
        out_specs=VMEM,
        cost_estimate=pl.CostEstimate(
            flops=12 * rows * rows * width, bytes_accessed=5 * 1024 * 1024, transcendentals=0
        ),
        name="window_attention",
    )(queries, own, before, after, query_ids, key_ids, *ahead)


def norm_kernel(mine_ref, theirs_ref, own_w, other_w, resid_ref, gain_ref, stream_ref, normed_ref):
    stream = resid_ref[...].astype(jnp.float32)
    stream += jnp.dot(mine_ref[...], own_w[...], preferred_element_type=jnp.float32)
    stream += jnp.dot(theirs_ref[...], other_w[...], preferred_element_type=jnp.float32)
    meansq = jnp.mean(stream * stream, axis=-1, keepdims=True)
    stream_ref[...] = stream
    normed_ref[...] = (stream * lax.rsqrt(meansq + 1e-05) * gain_ref[...]).astype(jnp.bfloat16)


def project_and_norm(mine, theirs, own_w, other_w, resid, gain):
    rows, width = resid.shape
    return pl.pallas_call(
        norm_kernel,
        out_shape=(
            jax.ShapeDtypeStruct((rows, width), jnp.float32),
            jax.ShapeDtypeStruct((rows, width), jnp.bfloat16),
        ),
        in_specs=[VMEM] * 6,
        out_specs=(VMEM, VMEM),
        cost_estimate=pl.CostEstimate(
            flops=4 * rows * width * mine.shape[1], bytes_accessed=8 * 1024 * 1024, transcendentals=0
        ),
        compiler_params=pltpu.CompilerParams(vmem_limit_bytes=24 * 1024 * 1024),
        name="project_and_norm",
    )(mine, theirs, own_w, other_w, resid, gain)


def expert_kernel(count, *refs):
    blocks, (weight_ref, gate_up, down), outs = refs[:count], refs[count : count + 3], refs[count + 3 :]
    units = down.shape[0]
    for half in range(0, count, 2):
        part = min(2, count - half)
        rows = blocks[0].shape[0]
        tokens = jnp.concatenate([ref[...] for ref in blocks[half : half + part]], axis=0)
        gate = lax.dot_general(tokens, gate_up[:units, :], NT, preferred_element_type=jnp.float32)
        up = lax.dot_general(tokens, gate_up[units:, :], NT, preferred_element_type=jnp.float32)
        act = (gate / (1.0 + jnp.exp(-gate)) * up).astype(jnp.bfloat16)
        result = jnp.dot(act, down[...], preferred_element_type=jnp.float32)
        result = result * weight_ref[half * rows : (half + part) * rows, :]
        for i in range(part):
            outs[half + i][...] = result[i * rows : (i + 1) * rows].astype(jnp.bfloat16)


def expert(blocks, weight, gate_up, down):
    rows, width = blocks[0].shape
    count = len(blocks)
    return pl.pallas_call(
        functools.partial(expert_kernel, count),
        out_shape=[jax.ShapeDtypeStruct((rows, width), jnp.bfloat16)] * count,
        in_specs=[VMEM] * (count + 3),
        out_specs=[VMEM] * count,
        cost_estimate=pl.CostEstimate(
            flops=6 * count * rows * width * down.shape[0],
            bytes_accessed=13 * 1024 * 1024,
            transcendentals=0,
        ),
        compiler_params=pltpu.CompilerParams(vmem_limit_bytes=40 * 1024 * 1024),
        name="expert_rows",
    )(*blocks, weight, gate_up, down)


def add(*terms):
    total = terms[0].astype(jnp.float32)
    for term in terms[1:]:
        total = total + term.astype(jnp.float32)
    return total


def add_small(*terms):
    return add(*terms).astype(jnp.bfloat16)


def expert_layer(normed, stream, weights, gate_up, down):
    count = lax.axis_size("seq")
    rows = normed.shape[0]

    def run(blocks, first):
        part = weights[first * rows : (first + len(blocks)) * rows]
        return expert(blocks, part, gate_up, down)

    if count == 16:
        o0 = normed
        o2, x0, y0, o1, o3 = flip(o0, 8), flip(o0, 1), flip(o0, 2), flip(o0, 4), flip(o0, 12)
        d0 = flip(y0, 1)
        x1 = flip(x0, 4)
        y1 = flip(o1, 2)
        x2, y2 = flip(o2, 1), flip(o2, 2)
        d1 = flip(d0, 4)
        d2 = flip(x2, 2)
        x3, y3 = flip(o3, 1), flip(o3, 2)
        d3 = flip(y3, 1)
        o0, x0, y0, d0 = run([o0, x0, y0, d0], 0)
        o1, x1, y1, d1 = run([o1, x1, y1, d1], 4)
        o2, x2, y2, d2 = run([o2, x2, y2, d2], 8)
        o3, x3, y3, d3 = run([o3, x3, y3, d3], 12)
        d0 = add_small(d0, flip(d1, 4))
        x0 = add_small(x0, flip(x1, 4))
        o1 = add_small(o1, flip(y1, 2))
        x2 = add_small(x2, flip(d2, 2))
        o2 = add_small(o2, flip(x2, 1), flip(y2, 2))
        y3 = add_small(y3, flip(d3, 1))
        o3 = add_small(o3, flip(x3, 1), flip(y3, 2))
        y0 = add_small(y0, flip(d0, 1))
        return add(
            stream, o0, flip(x0, 1), flip(y0, 2), flip(o1, 4), flip(o2, 8), flip(o3, 12)
        )
    blocks, mask = [normed], 1
    while mask < count:
        blocks = blocks + [flip(block, mask) for block in blocks]
        mask *= 2
    parts = []
    for first in range(0, count, 4):
        parts += run(blocks[first : first + 4], first)
    while mask > 1:
        mask //= 2
        parts = [add_small(parts[i], flip(parts[i + mask], mask)) for i in range(mask)]
    return add(stream, parts[0])


def shards(
    queries,
    keys,
    values,
    resid,
    pair_ids,
    out_weight,
    norm_gain,
    experts,
    gates,
    w_gate,
    w_up,
    w_down,
):
    tok_rows = queries.shape[0]
    moe_rows = resid.shape[0]
    shard = lax.axis_index("seq")
    core = lax.axis_index("exp")
    count = lax.axis_size("seq")

    own = jnp.concatenate([keys, values], axis=0)
    before = lax.ppermute(own, "seq", [(i, i + 1) for i in range(count - 1)])
    after = lax.ppermute(own, "seq", [(i + 1, i) for i in range(count - 1)])
    per_expert = jnp.sum(
        jnp.where(
            experts[:, :, None] == jnp.arange(count, dtype=jnp.int32)[None, None, :],
            gates[:, :, None],
            0.0,
        ),
        axis=1,
    )
    my_gate = lax.dynamic_slice_in_dim(gather_small(per_expert), shard, 1, 1)
    out_other = lax.ppermute(out_weight, "exp", SWAP)
    own_up = jnp.swapaxes(w_up[0], 0, 1)
    own_gate = jnp.swapaxes(w_gate[0], 0, 1)
    units = own_gate.shape[0]
    own_w = jnp.concatenate([own_gate, own_up, w_down[0]], axis=0)
    other_w = lax.ppermute(own_w, "exp", SWAP)
    gate_up = jnp.concatenate(
        [own_gate, other_w[:units], own_up, other_w[units : 2 * units]], axis=0
    )
    down = jnp.concatenate([w_down[0], other_w[2 * units :]], axis=0)

    id_pad = jnp.pad(pair_ids, (tok_rows, tok_rows), constant_values=-1)
    key_ids = lax.dynamic_slice_in_dim(id_pad, shard * tok_rows, 3 * tok_rows, 0)
    query_ids = lax.dynamic_slice_in_dim(pair_ids, shard * tok_rows, tok_rows, 0)
    attended = attention(
        queries,
        own,
        before,
        after,
        query_ids[:, None],
        key_ids[None, :],
        my_gate,
        out_other,
        gate_up,
        down,
    )
    mine = lax.dynamic_slice_in_dim(attended, core * moe_rows, moe_rows, 0)
    theirs = lax.dynamic_slice_in_dim(attended, (1 - core) * moe_rows, moe_rows, 0)
    received = lax.ppermute(theirs, "exp", SWAP)
    stream, normed = project_and_norm(
        mine, received, out_weight, out_other, resid, norm_gain[None, :]
    )
    return expert_layer(normed, stream, my_gate, gate_up, down).astype(jnp.bfloat16)


def solution(mesh):
    in_specs = (
        P("seq", "exp"),
        P("seq", "exp"),
        P("seq", "exp"),
        P(("seq", "exp"), None),
        P(),
        P("exp", None),
        P(),
        P(("seq", "exp"), None),
        P(("seq", "exp"), None),
        P("seq", None, "exp"),
        P("seq", None, "exp"),
        P("seq", "exp", None),
    )
    out_specs = P(("seq", "exp"), None)
    return jax.shard_map(shards, mesh=mesh, in_specs=in_specs, out_specs=out_specs, check_vma=False)
```

```python
import functools
import math

import jax
import jax.numpy as jnp
from jax import lax
from jax.experimental import pallas as pl
from jax.experimental.pallas import tpu as pltpu
from jax.sharding import PartitionSpec as P

HD = 128
SWAP = [(0, 1), (1, 0)]
VMEM = pl.BlockSpec(memory_space=pltpu.VMEM)
ANY = pl.BlockSpec(memory_space=pl.ANY)
NT = (((1,), (1,)), ((), ()))


def flip(block, mask):
    count = lax.axis_size("seq")
    return lax.ppermute(block, "seq", [(i, i ^ mask) for i in range(count)])


def after(block, *arrays):
    return lax.optimization_barrier((block, *arrays))[0]


def gate_order(count):
    masks = [1 << bit for bit in range(count.bit_length() - 1)]
    return masks[2:] + masks[1::-1]


def gather_gates(block):
    for mask in gate_order(lax.axis_size("seq")):
        block = jnp.concatenate([block, flip(block, mask)], axis=0)
    return block


def place_of(j):
    return sum(1 << bit for bit, mask in enumerate(gate_order(lax.axis_size("seq"))) if j & mask)


def attention_kernel(start_ref, q_ref, own_ref, before_ref, after_ref, qid_ref, kid_ref, *refs):
    out_ref = refs[-1]
    rows, some = q_ref.shape[0], out_ref.shape[0]
    start = pl.multiple_of(start_ref[0], some)
    query_pos = lax.broadcasted_iota(jnp.int32, (some, 3 * rows), 0) + (start + rows)
    key_pos = lax.broadcasted_iota(jnp.int32, (some, 3 * rows), 1)
    allowed = (qid_ref[pl.ds(start, some), :] == kid_ref[...]) & (
        jnp.abs(query_pos - key_pos) < rows
    )
    for head in range(q_ref.shape[1] // HD):
        cols = slice(head * HD, (head + 1) * HD)
        query = q_ref[pl.ds(start, some), cols]
        score = jnp.concatenate(
            [
                lax.dot_general(query, ref[:rows, cols], NT, preferred_element_type=jnp.float32)
                for ref in (before_ref, own_ref, after_ref)
            ],
            axis=1,
        ) / math.sqrt(HD)
        score = jnp.where(allowed, score, -jnp.inf)
        weights = jnp.exp(score - jnp.max(score, axis=-1, keepdims=True))
        probs = (weights / jnp.sum(weights, axis=-1, keepdims=True)).astype(jnp.bfloat16)
        total = jnp.zeros((some, HD), jnp.float32)
        for place, ref in enumerate((before_ref, own_ref, after_ref)):
            total += jnp.dot(
                probs[:, place * rows : (place + 1) * rows],
                ref[rows:, cols],
                preferred_element_type=jnp.float32,
            )
        out_ref[:, cols] = total.astype(jnp.bfloat16)


def attention(start, some, queries, own, before, after_own, query_ids, key_ids, ahead):
    rows, width = queries.shape
    return pl.pallas_call(
        attention_kernel,
        out_shape=jax.ShapeDtypeStruct((some, width), jnp.bfloat16),
        in_specs=[pl.BlockSpec(memory_space=pltpu.SMEM)] + [VMEM] * 6 + [ANY] * len(ahead),
        out_specs=VMEM,
        cost_estimate=pl.CostEstimate(
            flops=12 * some * rows * width, bytes_accessed=4 * 1024 * 1024, transcendentals=0
        ),
        name="window_attention",
    )(start, queries, own, before, after_own, query_ids, key_ids, *ahead)


def norm_kernel(mine_ref, theirs_ref, own_w, other_w, resid_ref, gain_ref, *refs):
    stream_ref, normed_ref = refs[-2:]
    stream = resid_ref[...].astype(jnp.float32)
    stream += jnp.dot(mine_ref[...], own_w[...], preferred_element_type=jnp.float32)
    stream += jnp.dot(theirs_ref[...], other_w[...], preferred_element_type=jnp.float32)
    meansq = jnp.mean(stream * stream, axis=-1, keepdims=True)
    stream_ref[...] = stream
    normed_ref[...] = (stream * lax.rsqrt(meansq + 1e-05) * gain_ref[...]).astype(jnp.bfloat16)


def project_and_norm(mine, theirs, own_w, other_w, resid, gain, *ahead):
    rows, width = resid.shape
    return pl.pallas_call(
        norm_kernel,
        out_shape=(
            jax.ShapeDtypeStruct((rows, width), jnp.float32),
            jax.ShapeDtypeStruct((rows, width), jnp.bfloat16),
        ),
        in_specs=[VMEM] * 6 + [ANY] * len(ahead),
        out_specs=(VMEM, VMEM),
        cost_estimate=pl.CostEstimate(
            flops=4 * rows * width * mine.shape[1], bytes_accessed=8 * 1024 * 1024, transcendentals=0
        ),
        compiler_params=pltpu.CompilerParams(vmem_limit_bytes=24 * 1024 * 1024),
        name="project_and_norm",
    )(mine, theirs, own_w, other_w, resid, gain, *ahead)


def expert_kernel(places, shard_ref, *refs):
    count = len(places)
    blocks, gates_ref, halves = refs[:count], refs[count], refs[count + 1 : count + 7]
    outs, (gate_w, up_w, down_w, sems) = refs[count + 7 : -4], refs[-4:]
    units = halves[0].shape[0]
    copies = []
    for i, half in enumerate(halves):
        target = (gate_w, up_w, down_w)[i // 2].at[pl.ds(i % 2 * units, units), :]
        copies.append(pltpu.make_async_copy(half, target, sems.at[i]))
        copies[-1].start()
    rows = blocks[0].shape[0]
    tokens = jnp.concatenate([ref[...] for ref in blocks], axis=0)
    copies[0].wait()
    copies[1].wait()
    gate = lax.dot_general(tokens, gate_w[...], NT, preferred_element_type=jnp.float32)
    copies[2].wait()
    copies[3].wait()
    up = lax.dot_general(tokens, up_w[...], NT, preferred_element_type=jnp.float32)
    act = (gate / (1.0 + jnp.exp(-gate)) * up).astype(jnp.bfloat16)
    copies[4].wait()
    copies[5].wait()
    for i, place in enumerate(places):
        gates = gates_ref[place * rows : (place + 1) * rows, :]
        expert = lax.broadcasted_iota(jnp.int32, gates.shape, 1)
        chosen = jnp.sum(jnp.where(expert == shard_ref[0], gates, 0.0), axis=1, keepdims=True)
        result = jnp.dot(
            act[i * rows : (i + 1) * rows], down_w[...], preferred_element_type=jnp.float32
        )
        outs[i][...] = (result * chosen).astype(jnp.bfloat16)


def expert(blocks, places, shard, gates, halves):
    rows, width = blocks[0].shape
    units = halves[0].shape[0]
    count = len(blocks)
    return pl.pallas_call(
        functools.partial(expert_kernel, places),
        out_shape=[jax.ShapeDtypeStruct((rows, width), jnp.bfloat16)] * count,
        in_specs=[pl.BlockSpec(memory_space=pltpu.SMEM)] + [VMEM] * (count + 1) + [ANY] * 6,
        out_specs=[VMEM] * count,
        scratch_shapes=[pltpu.VMEM((2 * units, width), jnp.bfloat16)] * 3
        + [pltpu.SemaphoreType.DMA((6,))],
        cost_estimate=pl.CostEstimate(
            flops=12 * count * rows * width * units,
            bytes_accessed=13 * 1024 * 1024,
            transcendentals=0,
        ),
        compiler_params=pltpu.CompilerParams(vmem_limit_bytes=40 * 1024 * 1024),
        name="expert_rows",
    )(shard, *blocks, gates, *halves)


def add(*terms):
    total = terms[0].astype(jnp.float32)
    for term in terms[1:]:
        total = total + term.astype(jnp.float32)
    return total


def add_small(*terms):
    return add(*terms).astype(jnp.bfloat16)


def expert_layer(normed, stream, shard, gates, halves):
    count = lax.axis_size("seq")

    def run(blocks, first):
        places = tuple(place_of(first + i) for i in range(len(blocks)))
        return expert(blocks, places, shard, gates, halves)

    if count == 16:
        o0 = normed
        o2, x0, y0, o1 = flip(o0, 8), flip(o0, 1), flip(o0, 2), flip(o0, 4)
        d0, x1, y1 = flip(y0, 1), flip(x0, 4), flip(o1, 2)
        o3 = flip(after(o0, o2), 12)
        x2, y2 = flip(o2, 1), flip(after(o2, y1), 2)
        d1 = flip(d0, 4)
        d2 = flip(x2, 2)
        x3, y3 = flip(o3, 1), flip(o3, 2)
        d3 = flip(y3, 1)
        o0, x0, y0, d0 = run([o0, x0, y0, d0], 0)
        o1, x1, y1, d1 = run([o1, x1, y1, d1], 4)
        o2, x2, y2, d2 = run([o2, x2, y2, d2], 8)
        o3, x3, y3, d3 = run([o3, x3, y3, d3], 12)
        d0 = add_small(d0, flip(d1, 4))
        x0 = add_small(x0, flip(x1, 4))
        o1 = add_small(o1, flip(y1, 2))
        x2 = add_small(x2, flip(d2, 2))
        o2 = add_small(o2, flip(x2, 1), flip(y2, 2))
        o2 = flip(o2, 8)
        y3 = add_small(y3, flip(d3, 1))
        o3 = add_small(o3, flip(x3, 1), flip(y3, 2))
        o3 = flip(o3, 12)
        y0 = add_small(y0, flip(d0, 1))
        return add(stream, o0, flip(x0, 1), flip(y0, 2), flip(o1, 4), o2, o3)
    blocks, mask = [normed], 1
    while mask < count:
        blocks = blocks + [flip(block, mask) for block in blocks]
        mask *= 2
    parts = []
    for first in range(0, count, 4):
        parts += run(blocks[first : first + 4], first)
    while mask > 1:
        mask //= 2
        parts = [add_small(parts[i], flip(parts[i + mask], mask)) for i in range(mask)]
    return add(stream, parts[0])


def shards(
    queries,
    keys,
    values,
    resid,
    pair_ids,
    out_weight,
    norm_gain,
    experts,
    gates,
    w_gate,
    w_up,
    w_down,
):
    tok_rows = queries.shape[0]
    moe_rows = resid.shape[0]
    shard = lax.axis_index("seq")
    core = lax.axis_index("exp")
    count = lax.axis_size("seq")

    own = jnp.concatenate([keys, values], axis=0)
    before = lax.ppermute(own, "seq", [(i, i + 1) for i in range(count - 1)])
    after_own = lax.ppermute(own, "seq", [(i + 1, i) for i in range(count - 1)])
    per_expert = jnp.sum(
        jnp.where(
            experts[:, :, None] == jnp.arange(count, dtype=jnp.int32)[None, None, :],
            gates[:, :, None],
            0.0,
        ),
        axis=1,
    )
    all_gates = gather_gates(per_expert)
    out_other = lax.ppermute(out_weight, "exp", SWAP)
    gate_w, up_w = jnp.swapaxes(w_gate[0], 0, 1), jnp.swapaxes(w_up[0], 0, 1)
    gate_other = lax.ppermute(gate_w, "exp", SWAP)
    id_pad = jnp.pad(pair_ids, (tok_rows, tok_rows), constant_values=-1)
    key_ids = lax.dynamic_slice_in_dim(id_pad, shard * tok_rows, 3 * tok_rows, 0)
    query_ids = lax.dynamic_slice_in_dim(pair_ids, shard * tok_rows, tok_rows, 0)
    ids = (query_ids[:, None], key_ids[None, :])
    ready = (before, after_own, all_gates, *ids)
    up_other = lax.ppermute(after(up_w, *ready), "exp", SWAP)
    down_other = lax.ppermute(after(w_down[0], *ready), "exp", SWAP)
    halves = [gate_w, gate_other, up_w, up_other, w_down[0], down_other]

    def attend(half, ahead):
        start = (half * moe_rows).reshape(1)
        return attention(start, moe_rows, queries, own, before, after_own, *ids, ahead)

    theirs = attend(1 - core, [out_other, gate_other])
    received = lax.ppermute(theirs, "exp", SWAP)
    mine = attend(core, [theirs])
    stream, normed = project_and_norm(
        mine, received, out_weight, out_other, resid, norm_gain[None, :], up_other, down_other
    )
    mixed = expert_layer(normed, stream, shard.reshape(1), all_gates, halves)
    return mixed.astype(jnp.bfloat16)


def solution(mesh):
    in_specs = (
        P("seq", "exp"),
        P("seq", "exp"),
        P("seq", "exp"),
        P(("seq", "exp"), None),
        P(),
        P("exp", None),
        P(),
        P(("seq", "exp"), None),
        P(("seq", "exp"), None),
        P("seq", None, "exp"),
        P("seq", None, "exp"),
        P("seq", "exp", None),
    )
    out_specs = P(("seq", "exp"), None)
    return jax.shard_map(shards, mesh=mesh, in_specs=in_specs, out_specs=out_specs, check_vma=False)
```

```python
import functools
import math

import jax
import jax.numpy as jnp
from jax import lax
from jax.experimental import pallas as pl
from jax.experimental.pallas import tpu as pltpu
from jax.sharding import PartitionSpec as P

HD = 128
SWAP = [(0, 1), (1, 0)]
VMEM = pl.BlockSpec(memory_space=pltpu.VMEM)
ANY = pl.BlockSpec(memory_space=pl.ANY)
NT = (((1,), (1,)), ((), ()))


def flip(block, mask):
    count = lax.axis_size("seq")
    return lax.ppermute(block, "seq", [(i, i ^ mask) for i in range(count)])


def after(block, *arrays):
    return lax.optimization_barrier((block, *arrays))[0]


def gate_order(count):
    masks = [1 << bit for bit in range(count.bit_length() - 1)]
    return masks[2:] + masks[1::-1]


def gather_gates(block):
    for mask in gate_order(lax.axis_size("seq")):
        half = block
        block = jnp.concatenate([half, flip(half, mask)], axis=0)
    return half, block


def place_of(j):
    return sum(1 << bit for bit, mask in enumerate(gate_order(lax.axis_size("seq"))) if j & mask)


def stack_kernel(keys_ref, values_ref, out_ref, sems):
    rows = keys_ref.shape[0]
    copies = [
        pltpu.make_async_copy(ref, out_ref.at[pl.ds(i * rows, rows), :], sems.at[i])
        for i, ref in enumerate((keys_ref, values_ref))
    ]
    for copy in copies:
        copy.start()
    for copy in copies:
        copy.wait()


def stack(keys, values):
    rows, width = keys.shape
    return pl.pallas_call(
        stack_kernel,
        out_shape=jax.ShapeDtypeStruct((2 * rows, width), keys.dtype),
        in_specs=[ANY, ANY],
        out_specs=ANY,
        scratch_shapes=[pltpu.SemaphoreType.DMA((2,))],
        name="stack_keys_values",
    )(keys, values)


def attention_kernel(core_ref, q_ref, before_ref, own_ref, after_ref, ids_ref, *refs):
    theirs_ref, mine_ref = refs[-2:]
    rows = q_ref.shape[0]
    some = rows // 2
    scale = 1.0 / math.sqrt(HD)
    column = jnp.transpose(jnp.broadcast_to(ids_ref[:, rows : 2 * rows], (HD, rows)))[:, :1]
    for half in range(2):
        first = half * some
        spans = [
            (before_ref, half * some, rows),
            (own_ref, 0, rows),
            (after_ref, 0, some + half * some),
        ]
        keys = 2 * rows + some
        query_pos = lax.broadcasted_iota(jnp.int32, (some, keys), 0) + (first + rows)
        key_pos = lax.broadcasted_iota(jnp.int32, (some, keys), 1) + first
        allowed = (column[first : first + some] == ids_ref[:, first : first + keys]) & (
            jnp.abs(query_pos - key_pos) < rows
        )
        for head in range(q_ref.shape[1] // HD):
            cols = slice(head * HD, (head + 1) * HD)
            query = q_ref[first : first + some, cols]
            score = jnp.concatenate(
                [
                    lax.dot_general(query, ref[lo:hi, cols], NT, preferred_element_type=jnp.float32)
                    for ref, lo, hi in spans
                ],
                axis=1,
            )
            score = jnp.where(allowed, score * scale, -jnp.inf)
            weights = jnp.exp(score - jnp.max(score, axis=-1, keepdims=True))
            share = 1.0 / jnp.sum(weights, axis=-1, keepdims=True)
            probs = (weights * share).astype(jnp.bfloat16)
            total, at = jnp.zeros((some, HD), jnp.float32), 0
            for ref, lo, hi in spans:
                total += jnp.dot(
                    probs[:, at : at + hi - lo],
                    ref[rows + lo : rows + hi, cols],
                    preferred_element_type=jnp.float32,
                )
                at += hi - lo
            total = total.astype(jnp.bfloat16)

            @pl.when(core_ref[0] == half)
            def _():
                mine_ref[:, cols] = total

            @pl.when(core_ref[0] != half)
            def _():
                theirs_ref[:, cols] = total


def attention(core, queries, near, ids, *ahead):
    rows, width = queries.shape
    half = jax.ShapeDtypeStruct((rows // 2, width), jnp.bfloat16)
    return pl.pallas_call(
        attention_kernel,
        out_shape=(half, half),
        in_specs=[pl.BlockSpec(memory_space=pltpu.SMEM)] + [VMEM] * 5 + [ANY] * len(ahead),
        out_specs=(VMEM, VMEM),
        compiler_params=pltpu.CompilerParams(vmem_limit_bytes=16 * 1024 * 1024),
        name="window_attention",
    )(core, queries, *near, ids, *ahead)


def norm_kernel(mine_ref, theirs_ref, own_w, other_w, resid_ref, gain_ref, *refs):
    stream_ref, normed_ref = refs[-2:]
    stream = resid_ref[...].astype(jnp.float32)
    stream += jnp.dot(mine_ref[...], own_w[...], preferred_element_type=jnp.float32)
    stream += jnp.dot(theirs_ref[...], other_w[...], preferred_element_type=jnp.float32)
    meansq = jnp.mean(stream * stream, axis=-1, keepdims=True)
    stream_ref[...] = stream
    normed_ref[...] = (stream * lax.rsqrt(meansq + 1e-05) * gain_ref[...]).astype(jnp.bfloat16)


def project_and_norm(mine, theirs, own_w, other_w, resid, gain, *ahead):
    rows, width = resid.shape
    return pl.pallas_call(
        norm_kernel,
        out_shape=(
            jax.ShapeDtypeStruct((rows, width), jnp.float32),
            jax.ShapeDtypeStruct((rows, width), jnp.bfloat16),
        ),
        in_specs=[VMEM] * 6 + [ANY] * len(ahead),
        out_specs=(VMEM, VMEM),
        compiler_params=pltpu.CompilerParams(vmem_limit_bytes=16 * 1024 * 1024),
        name="project_and_norm",
    )(mine, theirs, own_w, other_w, resid, gain, *ahead)


def expert_kernel(places, shard_ref, *refs):
    count = len(places)
    blocks, gates_ref, halves = refs[:count], refs[count], refs[count + 1 : count + 7]
    outs, (gate_w, up_w, down_w, sems) = refs[count + 7 : -4], refs[-4:]
    units = halves[0].shape[0]
    copies = []
    for i, half in enumerate(halves):
        target = (gate_w, up_w, down_w)[i // 2].at[pl.ds(i % 2 * units, units), :]
        copies.append(pltpu.make_async_copy(half, target, sems.at[i]))
        copies[-1].start()
    rows = blocks[0].shape[0]
    tokens = jnp.concatenate([ref[...] for ref in blocks], axis=0)
    copies[0].wait()
    copies[1].wait()
    gate = lax.dot_general(tokens, gate_w[...], NT, preferred_element_type=jnp.float32)
    copies[2].wait()
    copies[3].wait()
    up = lax.dot_general(tokens, up_w[...], NT, preferred_element_type=jnp.float32)
    act = (gate / (1.0 + jnp.exp(-gate)) * up).astype(jnp.bfloat16)
    copies[4].wait()
    copies[5].wait()
    result = jnp.dot(act, down_w[...], preferred_element_type=jnp.float32)
    for i, place in enumerate(places):
        gates = gates_ref[place * rows : (place + 1) * rows, :]
        expert = lax.broadcasted_iota(jnp.int32, gates.shape, 1)
        chosen = jnp.sum(jnp.where(expert == shard_ref[0], gates, 0.0), axis=1, keepdims=True)
        outs[i][...] = (result[i * rows : (i + 1) * rows] * chosen).astype(jnp.bfloat16)


def expert(blocks, places, shard, gates, halves):
    rows, width = blocks[0].shape
    units = halves[0].shape[0]
    count = len(blocks)
    return pl.pallas_call(
        functools.partial(expert_kernel, places),
        out_shape=[jax.ShapeDtypeStruct((rows, width), jnp.bfloat16)] * count,
        in_specs=[pl.BlockSpec(memory_space=pltpu.SMEM)] + [VMEM] * (count + 1) + [ANY] * 6,
        out_specs=[VMEM] * count,
        scratch_shapes=[pltpu.VMEM((2 * units, width), jnp.bfloat16)] * 3
        + [pltpu.SemaphoreType.DMA((6,))],
        compiler_params=pltpu.CompilerParams(vmem_limit_bytes=40 * 1024 * 1024),
        name="expert_rows",
    )(shard, *blocks, gates, *halves)


def add(*terms):
    total = terms[0].astype(jnp.float32)
    for term in terms[1:]:
        total = total + term.astype(jnp.float32)
    return total


def add_small(*terms):
    return add(*terms).astype(jnp.bfloat16)


def shift(block, pairs):
    return lax.ppermute(block, "seq", [(4 * a + i, 4 * b + i) for a, b in pairs for i in range(4)])


OUTWARD, INWARD, MIDDLE = [(1, 0), (2, 3)], [(0, 1), (3, 2)], [(1, 2), (2, 1)]


def step_layer(normed, stream, run):
    z = lax.axis_index("seq") // 4
    inner = (z == 1) | (z == 2)

    def step(arrays, *waits):
        return lax.optimization_barrier((*arrays, *waits))[: len(arrays)]

    o0 = normed
    x0, y0, o1, near3 = flip(o0, 1), flip(o0, 2), flip(o0, 4), shift(o0, MIDDLE)

    x0, y0, o1, near3 = step([x0, y0, o1, near3])
    d0, y1 = flip(y0, 1), flip(o1, 2)
    ends2, near2 = shift(near3, OUTWARD), shift(o1, MIDDLE)

    d0, y1, ends2, near2 = step([d0, y1, ends2, near2])
    o2 = jnp.where(inner, near2, ends2)
    ends3, x2, y2 = shift(near2, OUTWARD), flip(o2, 1), flip(o2, 2)
    p0, px0, py0, pd0 = run([o0, x0, y0, d0], (0, 1, 2, 3))

    ends3, x2, y2, x0, near3 = step([ends3, x2, y2, x0, near3], p0)
    o3 = jnp.where(inner, near3, ends3)
    x3, y3, x1 = flip(o3, 1), flip(o3, 2), flip(x0, 4)
    p1, py1, p2, px2, py2, p3 = run([o1, y1, o2, x2, y2, o3], (4, 6, 8, 9, 10, 12))

    x3, y3, x1, y2, d0 = step([x3, y3, x1, y2, d0], p1)
    d2, d3, d1 = flip(y2, 1), flip(x3, 2), flip(d0, 4)
    px3, py3, px1 = run([x3, y3, x1], (13, 14, 5))

    d2, d3, d1 = step([d2, d3, d1], px3)
    pd2, pd3, pd1 = run([d2, d3, d1], (11, 15, 7))
    to_y2, to_x3, to_d0 = flip(pd2, 1), flip(pd3, 2), flip(pd1, 4)

    px3, py2, pd0 = add_small(px3, to_x3), add_small(py2, to_y2), add_small(pd0, to_d0)
    px3, py3, px1, py2, pd0 = step([px3, py3, px1, py2, pd0])
    by_x, by_y, to_x0 = flip(px3, 1), flip(py3, 2), flip(px1, 4)

    p3, px0 = add_small(p3, by_x, by_y), add_small(px0, to_x0)
    p3, px0, px2, py2 = step([p3, px0, px2, py2])
    to_2, by_x, by_y = shift(p3, INWARD), flip(px2, 1), flip(py2, 2)

    p2 = add_small(p2, by_x, by_y, to_2)
    p2, pd0, py1 = step([p2, pd0, py1])
    to_3, to_1, to_y0, by_y = shift(p2, INWARD), shift(p2, MIDDLE), flip(pd0, 1), flip(py1, 2)

    p3, p1, py0 = add_small(p3, to_3), add_small(p1, by_y, to_1), add_small(py0, to_y0)
    p3, p1, py0, px0 = step([p3, p1, py0, px0])
    by_z, by_middle, by_x, by_y = flip(p1, 4), shift(p3, MIDDLE), flip(px0, 1), flip(py0, 2)
    return add(stream, p0, by_z, by_middle, by_x, by_y)


def expert_layer(normed, stream, shard, gates, halves):
    count = lax.axis_size("seq")

    def run(blocks, masks):
        places = tuple(place_of(mask) for mask in masks)
        return expert(blocks, places, shard, gates, halves)

    if count == 16:
        return step_layer(normed, stream, run)
    blocks, mask = [normed], 1
    while mask < count:
        blocks = blocks + [flip(block, mask) for block in blocks]
        mask *= 2
    parts = []
    for first in range(0, count, 4):
        parts += run(blocks[first : first + 4], range(first, first + 4))
    while mask > 1:
        mask //= 2
        parts = [add_small(parts[i], flip(parts[i + mask], mask)) for i in range(mask)]
    return add(stream, parts[0])


def shards(
    queries,
    keys,
    values,
    resid,
    pair_ids,
    out_weight,
    norm_gain,
    experts,
    gates,
    w_gate,
    w_up,
    w_down,
):
    tok_rows = queries.shape[0]
    moe_rows = resid.shape[0]
    shard = lax.axis_index("seq")
    core = lax.axis_index("exp")
    count = lax.axis_size("seq")

    own = stack(keys, values)
    before = lax.ppermute(own, "seq", [(i, i + 1) for i in range(count - 1)])
    after_own = lax.ppermute(own, "seq", [(i + 1, i) for i in range(count - 1)])
    per_expert = jnp.sum(
        jnp.where(
            experts[:, :, None] == jnp.arange(count, dtype=jnp.int32)[None, None, :],
            gates[:, :, None],
            0.0,
        ),
        axis=1,
    )
    some_gates, all_gates = gather_gates(per_expert)
    id_pad = jnp.pad(pair_ids, (tok_rows, tok_rows), constant_values=-1)
    ids = lax.dynamic_slice_in_dim(id_pad, shard * tok_rows, 3 * tok_rows, 0)[None, :]
    out_other = lax.ppermute(out_weight, "exp", SWAP)
    gate_w, up_w = jnp.swapaxes(w_gate[0], 0, 1), jnp.swapaxes(w_up[0], 0, 1)
    gate_other = lax.ppermute(gate_w, "exp", SWAP)
    ready = (before, after_own, some_gates, ids)
    up_other = lax.ppermute(after(up_w, *ready), "exp", SWAP)
    down_other = lax.ppermute(after(w_down[0], *ready), "exp", SWAP)
    halves = [gate_w, gate_other, up_w, up_other, w_down[0], down_other]

    theirs, mine = attention(
        core.reshape(1), queries, (before, own, after_own), ids, out_other, gate_other
    )
    received = lax.ppermute(theirs, "exp", SWAP)
    ahead = (up_other, down_other, all_gates)
    stream, normed = project_and_norm(
        mine, received, out_weight, out_other, resid, norm_gain[None, :], *ahead
    )
    mixed = expert_layer(normed, stream, shard.reshape(1), all_gates, halves)
    return mixed.astype(jnp.bfloat16)


def solution(mesh):
    in_specs = (
        P("seq", "exp"),
        P("seq", "exp"),
        P("seq", "exp"),
        P(("seq", "exp"), None),
        P(),
        P("exp", None),
        P(),
        P(("seq", "exp"), None),
        P(("seq", "exp"), None),
        P("seq", None, "exp"),
        P("seq", None, "exp"),
        P("seq", "exp", None),
    )
    out_specs = P(("seq", "exp"), None)
    return jax.shard_map(shards, mesh=mesh, in_specs=in_specs, out_specs=out_specs, check_vma=False)
```

```python
import functools
import math

import jax
import jax.numpy as jnp
from jax import lax
from jax.experimental import pallas as pl
from jax.experimental.pallas import tpu as pltpu
from jax.sharding import PartitionSpec as P

HD = 128
SWAP = [(0, 1), (1, 0)]
VMEM = pl.BlockSpec(memory_space=pltpu.VMEM)
ANY = pl.BlockSpec(memory_space=pl.ANY)
NT = (((1,), (1,)), ((), ()))


def flip(block, mask):
    count = lax.axis_size("seq")
    return lax.ppermute(block, "seq", [(i, i ^ mask) for i in range(count)])


def after(block, *arrays):
    return lax.optimization_barrier((block, *arrays))[0]


def gate_order(count):
    masks = [1 << bit for bit in range(count.bit_length() - 1)]
    return masks[2:] + masks[1::-1]


def gather_gates(block):
    pieces = [block]
    for mask in gate_order(lax.axis_size("seq")):
        pieces.append(flip(block, mask))
        block = jnp.concatenate([block, pieces[-1]], axis=1)
    return pieces


def place_of(j):
    return sum(1 << bit for bit, mask in enumerate(gate_order(lax.axis_size("seq"))) if j & mask)


def stack_kernel(keys_ref, values_ref, out_ref):
    rows = keys_ref.shape[0]
    out_ref[:rows] = keys_ref[...]
    out_ref[rows:] = values_ref[...]


def stack(keys, values):
    rows, width = keys.shape
    return pl.pallas_call(
        stack_kernel,
        out_shape=jax.ShapeDtypeStruct((2 * rows, width), keys.dtype),
        in_specs=[VMEM, VMEM],
        out_specs=VMEM,
        compiler_params=pltpu.CompilerParams(vmem_limit_bytes=63 * 1024 * 1024),
        name="stack_keys_values",
    )(keys, values)


def attention_kernel(core_ref, q_ref, before_ref, own_ref, after_ref, ids_ref, *refs):
    theirs_ref, mine_ref, both = refs[-3:]
    rows = q_ref.shape[0]
    some = rows // 2
    scale = 1.0 / math.sqrt(HD)
    column = jnp.transpose(jnp.broadcast_to(ids_ref[:, rows : 2 * rows], (HD, rows)))[:, :1]
    for half in range(2):
        first = half * some
        spans = [
            (before_ref, half * some, rows),
            (own_ref, 0, rows),
            (after_ref, 0, some + half * some),
        ]
        keys = 2 * rows + some
        query_pos = lax.broadcasted_iota(jnp.int32, (some, keys), 0) + (first + rows)
        key_pos = lax.broadcasted_iota(jnp.int32, (some, keys), 1) + first
        allowed = (column[first : first + some] == ids_ref[:, first : first + keys]) & (
            jnp.abs(query_pos - key_pos) < rows
        )
        for head in range(q_ref.shape[1] // HD):
            cols = slice(head * HD, (head + 1) * HD)
            query = q_ref[first : first + some, cols]
            score = jnp.concatenate(
                [
                    lax.dot_general(query, ref[lo:hi, cols], NT, preferred_element_type=jnp.float32)
                    for ref, lo, hi in spans
                ],
                axis=1,
            )
            score = jnp.where(allowed, score * scale, -jnp.inf)
            weights = jnp.exp(score - jnp.max(score, axis=-1, keepdims=True))
            share = 1.0 / jnp.sum(weights, axis=-1, keepdims=True)
            probs = (weights * share).astype(jnp.bfloat16)
            total, at = jnp.zeros((some, HD), jnp.float32), 0
            for ref, lo, hi in spans:
                total += jnp.dot(
                    probs[:, at : at + hi - lo],
                    ref[rows + lo : rows + hi, cols],
                    preferred_element_type=jnp.float32,
                )
                at += hi - lo
            both[first : first + some, cols] = total.astype(jnp.bfloat16)
    at = pl.multiple_of(core_ref[0] * some, some)
    mine_ref[...] = both[pl.ds(at, some), :]
    theirs_ref[...] = both[pl.ds(some - at, some), :]


def attention(core, queries, near, ids, *ahead):
    rows, width = queries.shape
    half = jax.ShapeDtypeStruct((rows // 2, width), jnp.bfloat16)
    return pl.pallas_call(
        attention_kernel,
        out_shape=(half, half),
        in_specs=[pl.BlockSpec(memory_space=pltpu.SMEM)] + [VMEM] * 5 + [ANY] * len(ahead),
        out_specs=(VMEM, VMEM),
        scratch_shapes=[pltpu.VMEM((rows, width), jnp.bfloat16)],
        compiler_params=pltpu.CompilerParams(vmem_limit_bytes=63 * 1024 * 1024),
        name="window_attention",
    )(core, queries, *near, ids, *ahead)


def norm_kernel(mine_ref, theirs_ref, own_w, other_w, resid_ref, gain_ref, *refs):
    stream_ref, normed_ref = refs[-2:]
    stream = resid_ref[...].astype(jnp.float32)
    stream += jnp.dot(mine_ref[...], own_w[...], preferred_element_type=jnp.float32)
    stream += jnp.dot(theirs_ref[...], other_w[...], preferred_element_type=jnp.float32)
    meansq = jnp.mean(stream * stream, axis=-1, keepdims=True)
    stream_ref[...] = stream
    normed_ref[...] = (stream * lax.rsqrt(meansq + 1e-05) * gain_ref[...]).astype(jnp.bfloat16)


def project_and_norm(mine, theirs, own_w, other_w, resid, gain, *ahead):
    rows, width = resid.shape
    return pl.pallas_call(
        norm_kernel,
        out_shape=(
            jax.ShapeDtypeStruct((rows, width), jnp.float32),
            jax.ShapeDtypeStruct((rows, width), jnp.bfloat16),
        ),
        in_specs=[VMEM] * 6 + [ANY] * len(ahead),
        out_specs=(VMEM, VMEM),
        compiler_params=pltpu.CompilerParams(vmem_limit_bytes=63 * 1024 * 1024),
        name="project_and_norm",
    )(mine, theirs, own_w, other_w, resid, gain, *ahead)


def assemble_kernel(*refs):
    halves, (gate_up, down, sems) = refs[:6], refs[6:]
    units = halves[0].shape[0]
    copies = []
    for i, half in enumerate(halves):
        target, at = (gate_up, i * units) if i < 4 else (down, (i - 4) * units)
        copies.append(pltpu.make_async_copy(half, target.at[pl.ds(at, units), :], sems.at[i]))
    for copy in copies:
        copy.start()
    for copy in copies:
        copy.wait()


def assemble(halves):
    units, width = halves[0].shape
    return pl.pallas_call(
        assemble_kernel,
        out_shape=(
            jax.ShapeDtypeStruct((4 * units, width), jnp.bfloat16),
            jax.ShapeDtypeStruct((2 * units, width), jnp.bfloat16),
        ),
        in_specs=[ANY] * 6,
        out_specs=(VMEM, VMEM),
        scratch_shapes=[pltpu.SemaphoreType.DMA((6,))],
        compiler_params=pltpu.CompilerParams(vmem_limit_bytes=36 * 1024 * 1024),
        name="assemble_weights",
    )(*halves)


def expert_kernel(places, pieces, shard_ref, *refs):
    count = len(places)
    blocks, gates, (gate_up, down) = refs[:count], refs[count : count + pieces], refs[count + pieces :][:2]
    outs = refs[count + pieces + 2 :]
    units = down.shape[0]
    rows = blocks[0].shape[0]
    for first in range(0, count, 2):
        group = range(first, min(first + 2, count))
        tokens = jnp.concatenate([blocks[i][...] for i in group], axis=0)
        gate = lax.dot_general(tokens, gate_up[:units, :], NT, preferred_element_type=jnp.float32)
        up = lax.dot_general(tokens, gate_up[units:, :], NT, preferred_element_type=jnp.float32)
        act = (gate / (1.0 + jnp.exp(-gate)) * up).astype(jnp.bfloat16)
        result = jnp.dot(act, down[...], preferred_element_type=jnp.float32)
        for i in group:
            piece = places[i].bit_length()
            at = (places[i] - (1 << piece >> 1)) * rows
            here = gates[piece][:, at : at + rows]
            expert = lax.broadcasted_iota(jnp.int32, here.shape, 0)
            chosen = jnp.sum(jnp.where(expert == shard_ref[0], here, 0.0), axis=0, keepdims=True)
            chosen = jnp.transpose(jnp.broadcast_to(chosen, (rows, rows)))[:, :1]
            part = result[(i - first) * rows : (i - first + 1) * rows]
            outs[i][...] = (part * chosen).astype(jnp.bfloat16)


def expert(blocks, places, shard, gates, weights):
    rows, width = blocks[0].shape
    count = len(blocks)
    return pl.pallas_call(
        functools.partial(expert_kernel, places, len(gates)),
        out_shape=[jax.ShapeDtypeStruct((rows, width), jnp.bfloat16)] * count,
        in_specs=[pl.BlockSpec(memory_space=pltpu.SMEM)] + [VMEM] * (count + len(gates) + 2),
        out_specs=[VMEM] * count,
        compiler_params=pltpu.CompilerParams(vmem_limit_bytes=36 * 1024 * 1024),
        name="expert_rows",
    )(shard, *blocks, *gates, *weights)


def add(*terms):
    total = terms[0].astype(jnp.float32)
    for term in terms[1:]:
        total = total + term.astype(jnp.float32)
    return total


def add_small(*terms):
    return add(*terms).astype(jnp.bfloat16)


def shift(block, pairs):
    return lax.ppermute(block, "seq", [(4 * a + i, 4 * b + i) for a, b in pairs for i in range(4)])


OUTWARD, INWARD, MIDDLE = [(1, 0), (2, 3)], [(0, 1), (3, 2)], [(1, 2), (2, 1)]


def step_layer(normed, stream, run, weights):
    z = lax.axis_index("seq") // 4
    inner = (z == 1) | (z == 2)

    o0 = normed
    o1, near3, x0, y0 = flip(o0, 4), shift(o0, MIDDLE), flip(o0, 1), flip(o0, 2)

    ends2, near2 = shift(after(near3, o1), OUTWARD), shift(after(o1, near3), MIDDLE)
    d0, y1 = flip(after(y0, x0), 1), flip(after(o1, y0), 2)

    ends3 = shift(after(near2, ends2), OUTWARD)
    o2 = jnp.where(inner, near2, ends2)
    x2, y2 = flip(after(o2, d0, weights[0]), 1), flip(after(o2, y1, weights[0]), 2)
    p0, px0, py0, pd0 = run([after(o0, o2), x0, y0, d0], (0, 1, 2, 3))

    x1 = flip(after(x0, ends3, p0), 4)
    o3 = jnp.where(inner, near3, ends3)
    x3, y3 = flip(after(o3, x2, p0), 1), flip(after(o3, y2, p0), 2)
    p1, py1, p2, px2, py2, p3 = run([after(o1, p0), y1, o2, x2, y2, o3], (4, 6, 8, 9, 10, 12))

    d1 = flip(after(d0, x1, p1), 4)
    d2, d3 = flip(after(y2, x3, p1), 1), flip(after(x3, y3, p1), 2)
    px3, py3, px1 = run([after(x3, p1), y3, x1], (13, 14, 5))

    pd2, pd3 = run([after(d2, px3), d3], (11, 15))
    (pd1,) = run([after(d1, pd2)], (7,))
    to_x3, to_y2, to_d0 = flip(pd3, 2), flip(pd2, 1), flip(pd1, 4)

    px3, py2, pd0 = add_small(px3, to_x3), add_small(py2, to_y2), add_small(pd0, to_d0)
    by_x, by_y = flip(after(px3, to_y2), 1), flip(after(py3, to_x3), 2)
    to_x0 = flip(after(px1, to_d0), 4)

    p3, px0 = add_small(p3, by_x, by_y), add_small(px0, to_x0)
    to_2 = shift(after(p3, to_x0), INWARD)
    by_x, by_y = flip(after(px2, by_x), 1), flip(after(py2, by_y), 2)

    p2 = add_small(p2, by_x, by_y, to_2)
    to_3, to_1 = shift(after(p2, to_2), INWARD), shift(p2, MIDDLE)
    to_y0, by_y = flip(after(pd0, by_x), 1), flip(after(py1, by_y), 2)

    p3, p1, py0 = add_small(p3, to_3), add_small(p1, by_y, to_1), add_small(py0, to_y0)
    by_z, by_middle = flip(after(p1, to_3), 4), shift(after(p3, to_1), MIDDLE)
    by_x, by_y = flip(after(px0, to_y0), 1), flip(after(py0, by_y), 2)
    return add(stream, p0, by_z, by_middle, by_x, by_y)


def expert_layer(normed, stream, shard, gates, weights):
    count = lax.axis_size("seq")

    def run(blocks, masks):
        places = tuple(place_of(mask) for mask in masks)
        return expert(blocks, places, shard, gates, weights)

    if count == 16:
        return step_layer(normed, stream, run, weights)
    blocks, mask = [normed], 1
    while mask < count:
        blocks = blocks + [flip(block, mask) for block in blocks]
        mask *= 2
    parts = []
    for first in range(0, count, 4):
        parts += run(blocks[first : first + 4], range(first, first + 4))
    while mask > 1:
        mask //= 2
        parts = [add_small(parts[i], flip(parts[i + mask], mask)) for i in range(mask)]
    return add(stream, parts[0])


def shards(
    queries,
    keys,
    values,
    resid,
    pair_ids,
    out_weight,
    norm_gain,
    experts,
    gates,
    w_gate,
    w_up,
    w_down,
):
    tok_rows = queries.shape[0]
    moe_rows = resid.shape[0]
    shard = lax.axis_index("seq")
    core = lax.axis_index("exp")
    count = lax.axis_size("seq")

    own = stack(keys, values)
    before = lax.ppermute(own, "seq", [(i, i + 1) for i in range(count - 1)])
    after_own = lax.ppermute(own, "seq", [(i + 1, i) for i in range(count - 1)])
    chosen = experts.T[:, None, :] == jnp.arange(count, dtype=jnp.int32)[None, :, None]
    all_gates = gather_gates(jnp.sum(jnp.where(chosen, gates.T[:, None, :], 0.0), axis=0))
    some_gates = all_gates[-2]
    id_pad = jnp.pad(pair_ids, (tok_rows, tok_rows), constant_values=-1)
    ids = lax.dynamic_slice_in_dim(id_pad, shard * tok_rows, 3 * tok_rows, 0)[None, :]
    out_other = lax.ppermute(out_weight, "exp", SWAP)
    gate_w, up_w = jnp.swapaxes(w_gate[0], 0, 1), jnp.swapaxes(w_up[0], 0, 1)
    gate_other = lax.ppermute(gate_w, "exp", SWAP)
    ready = (before, after_own, some_gates, ids)
    up_other = lax.ppermute(after(up_w, *ready), "exp", SWAP)
    down_other = lax.ppermute(after(w_down[0], *ready), "exp", SWAP)
    halves = [gate_w, gate_other, up_w, up_other, w_down[0], down_other]

    theirs, mine = attention(
        core.reshape(1), queries, (before, own, after_own), ids, out_other, gate_other
    )
    received = lax.ppermute(theirs, "exp", SWAP)
    ahead = (up_other, down_other, all_gates[-1])
    stream, normed = project_and_norm(
        mine, received, out_weight, out_other, resid, norm_gain[None, :], *ahead
    )
    mixed = expert_layer(normed, stream, shard.reshape(1), all_gates, assemble(halves))
    return mixed.astype(jnp.bfloat16)


def solution(mesh):
    in_specs = (
        P("seq", "exp"),
        P("seq", "exp"),
        P("seq", "exp"),
        P(("seq", "exp"), None),
        P(),
        P("exp", None),
        P(),
        P(("seq", "exp"), None),
        P(("seq", "exp"), None),
        P("seq", None, "exp"),
        P("seq", None, "exp"),
        P("seq", "exp", None),
    )
    out_specs = P(("seq", "exp"), None)
    return jax.shard_map(shards, mesh=mesh, in_specs=in_specs, out_specs=out_specs, check_vma=False)
```

```python
import functools
import math

import jax
import jax.numpy as jnp
from jax import lax
from jax.experimental import pallas as pl
from jax.experimental.pallas import tpu as pltpu
from jax.sharding import PartitionSpec as P

HD = 128
SWAP = [(0, 1), (1, 0)]
VMEM = pl.BlockSpec(memory_space=pltpu.VMEM)
ANY = pl.BlockSpec(memory_space=pl.ANY)
NT = (((1,), (1,)), ((), ()))


def flip(block, mask):
    count = lax.axis_size("seq")
    return lax.ppermute(block, "seq", [(i, i ^ mask) for i in range(count)])


def after(block, *arrays):
    return lax.optimization_barrier((block, *arrays))[0]


def gate_order(count):
    masks = [1 << bit for bit in range(count.bit_length() - 1)]
    return masks[2:] + masks[1::-1]


def gather_gates(block):
    pieces = [block]
    for mask in gate_order(lax.axis_size("seq")):
        pieces.append(flip(block, mask))
        block = jnp.concatenate([block, pieces[-1]], axis=1)
    return pieces


def place_of(j):
    return sum(1 << bit for bit, mask in enumerate(gate_order(lax.axis_size("seq"))) if j & mask)


def fetch_kernel(own_ref, other_ref, resid_ref, *refs):
    outs, sems = refs[:-1], refs[-1]
    copies = [
        pltpu.make_async_copy(ref, out, sems.at[i])
        for i, (ref, out) in enumerate(zip((own_ref, other_ref, resid_ref), outs))
    ]
    for copy in copies:
        copy.start()
    for copy in copies:
        copy.wait()


def fetch(*arrays):
    return pl.pallas_call(
        fetch_kernel,
        out_shape=[jax.ShapeDtypeStruct(array.shape, array.dtype) for array in arrays],
        in_specs=[ANY] * len(arrays),
        out_specs=[VMEM] * len(arrays),
        scratch_shapes=[pltpu.SemaphoreType.DMA((len(arrays),))],
        compiler_params=pltpu.CompilerParams(vmem_limit_bytes=8 * 1024 * 1024),
        name="fetch_projection",
    )(*arrays)


def attention_kernel(where_ref, q_ref, ids_ref, *refs):
    blocks, (theirs_ref, mine_ref, keys, values, both, sems) = refs[:6], refs[-6:]
    rows = q_ref.shape[0]
    some = rows // 2
    core, odd = where_ref[0], where_ref[1]
    starts = (2 * rows * (1 - odd), rows, 2 * rows * odd)
    copies = []
    for i, block in enumerate(blocks):
        target = (keys, values)[i // 3].at[pl.ds(pl.multiple_of(starts[i % 3], rows), rows), :]
        copies.append(pltpu.make_async_copy(block, target, sems.at[i]))
        copies[-1].start()
    scale = 1.0 / math.sqrt(HD)
    column = jnp.transpose(jnp.broadcast_to(ids_ref[:, rows : 2 * rows], (HD, rows)))[:, :1]
    span = 2 * rows + some
    allowed = []
    for first in (0, some):
        query_pos = lax.broadcasted_iota(jnp.int32, (some, span), 0) + (first + rows)
        key_pos = lax.broadcasted_iota(jnp.int32, (some, span), 1) + first
        allowed.append(
            (column[first : first + some] == ids_ref[:, first : first + span])
            & (jnp.abs(query_pos - key_pos) < rows)
        )
    for copy in copies:
        copy.wait()
    for half, first in enumerate((0, some)):
        for head in range(q_ref.shape[1] // HD):
            cols = slice(head * HD, (head + 1) * HD)
            score = lax.dot_general(
                q_ref[first : first + some, cols],
                keys[first : first + span, cols],
                NT,
                preferred_element_type=jnp.float32,
            )
            score = jnp.where(allowed[half], score * scale, -jnp.inf)
            weights = jnp.exp(score - jnp.max(score, axis=-1, keepdims=True))
            share = 1.0 / jnp.sum(weights, axis=-1, keepdims=True)
            probs = (weights * share).astype(jnp.bfloat16)
            both[first : first + some, cols] = jnp.dot(
                probs, values[first : first + span, cols], preferred_element_type=jnp.float32
            ).astype(jnp.bfloat16)
    at = pl.multiple_of(core * some, some)
    mine_ref[...] = both[pl.ds(at, some), :]
    theirs_ref[...] = both[pl.ds(some - at, some), :]


def attention(where, queries, ids, near_keys, near_values, *ahead):
    rows, width = queries.shape
    half = jax.ShapeDtypeStruct((rows // 2, width), jnp.bfloat16)
    return pl.pallas_call(
        attention_kernel,
        out_shape=(half, half),
        in_specs=[pl.BlockSpec(memory_space=pltpu.SMEM), VMEM, VMEM] + [ANY] * (6 + len(ahead)),
        out_specs=(VMEM, VMEM),
        scratch_shapes=[pltpu.VMEM((3 * rows, width), jnp.bfloat16)] * 2
        + [pltpu.VMEM((rows, width), jnp.bfloat16), pltpu.SemaphoreType.DMA((6,))],
        compiler_params=pltpu.CompilerParams(vmem_limit_bytes=16 * 1024 * 1024),
        name="window_attention",
    )(where, queries, ids, *near_keys, *near_values, *ahead)


def norm_kernel(mine_ref, theirs_ref, own_w, other_w, resid_ref, gain_ref, *refs):
    stream_ref, normed_ref = refs[-2:]
    stream = resid_ref[...].astype(jnp.float32)
    stream += jnp.dot(mine_ref[...], own_w[...], preferred_element_type=jnp.float32)
    stream += jnp.dot(theirs_ref[...], other_w[...], preferred_element_type=jnp.float32)
    meansq = jnp.mean(stream * stream, axis=-1, keepdims=True)
    stream_ref[...] = stream
    normed_ref[...] = (stream * lax.rsqrt(meansq + 1e-05) * gain_ref[...]).astype(jnp.bfloat16)


def project_and_norm(mine, theirs, own_w, other_w, resid, gain, *ahead):
    rows, width = resid.shape
    return pl.pallas_call(
        norm_kernel,
        out_shape=(
            jax.ShapeDtypeStruct((rows, width), jnp.float32),
            jax.ShapeDtypeStruct((rows, width), jnp.bfloat16),
        ),
        in_specs=[VMEM] * 6 + [ANY] * len(ahead),
        out_specs=(VMEM, VMEM),
        compiler_params=pltpu.CompilerParams(vmem_limit_bytes=16 * 1024 * 1024),
        name="project_and_norm",
    )(mine, theirs, own_w, other_w, resid, gain, *ahead)


def assemble_kernel(*refs):
    halves, (gate_up, down, sems) = refs[:6], refs[6:]
    units = halves[0].shape[0]
    copies = []
    for i, half in enumerate(halves):
        target, at = (gate_up, i * units) if i < 4 else (down, (i - 4) * units)
        copies.append(pltpu.make_async_copy(half, target.at[pl.ds(at, units), :], sems.at[i]))
    for copy in copies:
        copy.start()
    for copy in copies:
        copy.wait()


def assemble(halves):
    units, width = halves[0].shape
    return pl.pallas_call(
        assemble_kernel,
        out_shape=(
            jax.ShapeDtypeStruct((4 * units, width), jnp.bfloat16),
            jax.ShapeDtypeStruct((2 * units, width), jnp.bfloat16),
        ),
        in_specs=[ANY] * 6,
        out_specs=(VMEM, VMEM),
        scratch_shapes=[pltpu.SemaphoreType.DMA((6,))],
        compiler_params=pltpu.CompilerParams(vmem_limit_bytes=12 * 1024 * 1024),
        name="assemble_weights",
    )(*halves)


def expert_kernel(places, pieces, shard_ref, *refs):
    count = len(places)
    blocks, gates, (gate_up, down) = refs[:count], refs[count : count + pieces], refs[count + pieces :][:2]
    outs = refs[count + pieces + 2 :]
    units = down.shape[0]
    rows = blocks[0].shape[0]
    for first in range(0, count, 2):
        group = range(first, min(first + 2, count))
        tokens = jnp.concatenate([blocks[i][...] for i in group], axis=0)
        gate = lax.dot_general(tokens, gate_up[:units, :], NT, preferred_element_type=jnp.float32)
        up = lax.dot_general(tokens, gate_up[units:, :], NT, preferred_element_type=jnp.float32)
        act = (gate / (1.0 + jnp.exp(-gate)) * up).astype(jnp.bfloat16)
        result = jnp.dot(act, down[...], preferred_element_type=jnp.float32)
        for i in group:
            piece = places[i].bit_length()
            at = (places[i] - (1 << piece >> 1)) * rows
            here = gates[piece][:, at : at + rows]
            expert = lax.broadcasted_iota(jnp.int32, here.shape, 0)
            chosen = jnp.sum(jnp.where(expert == shard_ref[0], here, 0.0), axis=0, keepdims=True)
            chosen = jnp.transpose(jnp.broadcast_to(chosen, (rows, rows)))[:, :1]
            part = result[(i - first) * rows : (i - first + 1) * rows]
            outs[i][...] = (part * chosen).astype(jnp.bfloat16)


def expert(blocks, places, shard, gates, weights):
    rows, width = blocks[0].shape
    count = len(blocks)
    return pl.pallas_call(
        functools.partial(expert_kernel, places, len(gates)),
        out_shape=[jax.ShapeDtypeStruct((rows, width), jnp.bfloat16)] * count,
        in_specs=[pl.BlockSpec(memory_space=pltpu.SMEM)] + [VMEM] * (count + len(gates) + 2),
        out_specs=[VMEM] * count,
        compiler_params=pltpu.CompilerParams(vmem_limit_bytes=24 * 1024 * 1024),
        name="expert_rows",
    )(shard, *blocks, *gates, *weights)


def add(*terms):
    total = terms[0].astype(jnp.float32)
    for term in terms[1:]:
        total = total + term.astype(jnp.float32)
    return total


def add_small(*terms):
    return add(*terms).astype(jnp.bfloat16)


def shift(block, pairs):
    return lax.ppermute(block, "seq", [(4 * a + i, 4 * b + i) for a, b in pairs for i in range(4)])


OUTWARD, INWARD, MIDDLE = [(1, 0), (2, 3)], [(0, 1), (3, 2)], [(1, 2), (2, 1)]


def step_layer(normed, stream, run, weights):
    z = lax.axis_index("seq") // 4
    inner = (z == 1) | (z == 2)

    o0 = normed
    o1, near3, x0, y0 = flip(o0, 4), shift(o0, MIDDLE), flip(o0, 1), flip(o0, 2)

    ends2, near2 = shift(after(near3, o1), OUTWARD), shift(after(o1, near3), MIDDLE)
    d0, y1 = flip(after(y0, x0), 1), flip(after(o1, y0), 2)

    ends3 = shift(after(near2, ends2), OUTWARD)
    o2 = jnp.where(inner, near2, ends2)
    x2, y2 = flip(after(o2, d0, weights[0]), 1), flip(after(o2, y1, weights[0]), 2)
    p0, px0, py0, pd0 = run([after(o0, o2), x0, y0, d0], (0, 1, 2, 3))

    x1 = flip(after(x0, ends3, p0), 4)
    o3 = jnp.where(inner, near3, ends3)
    x3, y3 = flip(after(o3, x2, p0), 1), flip(after(o3, y2, p0), 2)
    p1, py1, p2, px2, py2, p3 = run([after(o1, p0), y1, o2, x2, y2, o3], (4, 6, 8, 9, 10, 12))

    d1 = flip(after(d0, x1, p1), 4)
    d2, d3 = flip(after(y2, x3, p1), 1), flip(after(x3, y3, p1), 2)
    px3, py3, px1 = run([after(x3, p1), y3, x1], (13, 14, 5))

    pd2, pd3 = run([after(d2, px3, d1), d3], (11, 15))
    (pd1,) = run([after(d1, pd2)], (7,))
    to_x3, to_y2, to_d0 = flip(pd3, 2), flip(pd2, 1), flip(pd1, 4)

    px3, py2, pd0 = add_small(px3, to_x3), add_small(py2, to_y2), add_small(pd0, to_d0)
    by_x, by_y, to_x0 = flip(px3, 1), flip(py3, 2), flip(px1, 4)

    p3, px0 = add_small(p3, by_x, by_y), add_small(px0, to_x0)
    to_2, by_x, by_y = shift(p3, INWARD), flip(px2, 1), flip(py2, 2)

    p2 = add_small(p2, by_x, by_y, to_2)
    to_3, to_1 = shift(p2, INWARD), shift(p2, MIDDLE)
    to_y0, by_y = flip(pd0, 1), flip(py1, 2)

    p3, p1, py0 = add_small(p3, to_3), add_small(p1, by_y, to_1), add_small(py0, to_y0)
    by_z, by_middle, by_x, by_y = flip(p1, 4), shift(p3, MIDDLE), flip(px0, 1), flip(py0, 2)
    return add(stream, p0, by_z, by_middle, by_x, by_y)


def expert_layer(normed, stream, shard, gates, weights):
    count = lax.axis_size("seq")

    def run(blocks, masks):
        places = tuple(place_of(mask) for mask in masks)
        return expert(blocks, places, shard, gates, weights)

    if count == 16:
        return step_layer(normed, stream, run, weights)
    blocks, mask = [normed], 1
    while mask < count:
        blocks = blocks + [flip(block, mask) for block in blocks]
        mask *= 2
    parts = []
    for first in range(0, count, 4):
        parts += run(blocks[first : first + 4], range(first, first + 4))
    while mask > 1:
        mask //= 2
        parts = [add_small(parts[i], flip(parts[i + mask], mask)) for i in range(mask)]
    return add(stream, parts[0])


def shards(
    queries,
    keys,
    values,
    resid,
    pair_ids,
    out_weight,
    norm_gain,
    experts,
    gates,
    w_gate,
    w_up,
    w_down,
):
    tok_rows = queries.shape[0]
    moe_rows = resid.shape[0]
    shard = lax.axis_index("seq")
    core = lax.axis_index("exp")
    count = lax.axis_size("seq")

    def halo(part, *arrays):
        beside = after(flip(part, 1), *arrays)
        ahead = [(i, i + 2) for i in range(0, count - 2, 2)]
        back = [(i + 2, i) for i in range(1, count - 2, 2)]
        return beside, part, lax.ppermute(beside, "seq", ahead + back)

    out_other = lax.ppermute(out_weight, "exp", SWAP)
    out_own, out_other, stream = fetch(out_weight, out_other, resid)
    near_keys, near_values = halo(keys), halo(values, out_own)
    chosen = experts.T[:, None, :] == jnp.arange(count, dtype=jnp.int32)[None, :, None]
    all_gates = gather_gates(jnp.sum(jnp.where(chosen, gates.T[:, None, :], 0.0), axis=0))
    id_pad = jnp.pad(pair_ids, (tok_rows, tok_rows), constant_values=-1)
    ids = lax.dynamic_slice_in_dim(id_pad, shard * tok_rows, 3 * tok_rows, 0)[None, :]
    gate_w, up_w = jnp.swapaxes(w_gate[0], 0, 1), jnp.swapaxes(w_up[0], 0, 1)
    gate_other = lax.ppermute(gate_w, "exp", SWAP)
    ready = (*near_keys, *near_values, all_gates[-1], ids)
    up_other = lax.ppermute(after(up_w, *ready), "exp", SWAP)
    down_other = lax.ppermute(after(w_down[0], *ready), "exp", SWAP)
    halves = [gate_w, gate_other, up_w, up_other, w_down[0], down_other]

    where = jnp.stack([core, shard % 2])
    theirs, mine = attention(
        where, queries, ids, near_keys, near_values, gate_other
    )
    received = lax.ppermute(theirs, "exp", SWAP)
    stream, normed = project_and_norm(
        mine, received, out_own, out_other, stream, norm_gain[None, :], up_other, down_other
    )
    mixed = expert_layer(normed, stream, shard.reshape(1), all_gates, assemble(halves))
    return mixed.astype(jnp.bfloat16)


def solution(mesh):
    in_specs = (
        P("seq", "exp"),
        P("seq", "exp"),
        P("seq", "exp"),
        P(("seq", "exp"), None),
        P(),
        P("exp", None),
        P(),
        P(("seq", "exp"), None),
        P(("seq", "exp"), None),
        P("seq", None, "exp"),
        P("seq", None, "exp"),
        P("seq", "exp", None),
    )
    out_specs = P(("seq", "exp"), None)
    return jax.shard_map(shards, mesh=mesh, in_specs=in_specs, out_specs=out_specs, check_vma=False)
```

```python
import functools
import math

import jax
import jax.numpy as jnp
from jax import lax
from jax.experimental import pallas as pl
from jax.experimental.pallas import tpu as pltpu
from jax.sharding import PartitionSpec as P

HD = 128
SWAP = [(0, 1), (1, 0)]
VMEM = pl.BlockSpec(memory_space=pltpu.VMEM)
ANY = pl.BlockSpec(memory_space=pl.ANY)
NT = (((1,), (1,)), ((), ()))


def flip(block, mask):
    count = lax.axis_size("seq")
    return lax.ppermute(block, "seq", [(i, i ^ mask) for i in range(count)])


def after(block, *arrays):
    return lax.optimization_barrier((block, *arrays))[0]


def gate_order(count):
    masks = [1 << bit for bit in range(count.bit_length() - 1)]
    return masks[2:] + masks[1::-1]


def gather_gates(block):
    pieces = [block]
    for mask in gate_order(lax.axis_size("seq")):
        pieces.append(flip(block, mask))
        block = jnp.concatenate([block, pieces[-1]], axis=1)
    return pieces


def place_of(j):
    return sum(1 << bit for bit, mask in enumerate(gate_order(lax.axis_size("seq"))) if j & mask)


def attention_kernel(where_ref, q_ref, ids_ref, *refs):
    blocks, (theirs_ref, mine_ref, keys, values, both, sems) = refs[:6], refs[-6:]
    rows = q_ref.shape[0]
    some = rows // 2
    core, odd = where_ref[0], where_ref[1]
    starts = (2 * rows * (1 - odd), rows, 2 * rows * odd)
    copies = []
    for i, block in enumerate(blocks):
        target = (keys, values)[i // 3].at[pl.ds(pl.multiple_of(starts[i % 3], rows), rows), :]
        copies.append(pltpu.make_async_copy(block, target, sems.at[i]))
        copies[-1].start()
    scale = 1.0 / math.sqrt(HD)
    column = jnp.transpose(jnp.broadcast_to(ids_ref[:, rows : 2 * rows], (HD, rows)))[:, :1]
    span = 2 * rows + some
    allowed = []
    for first in (0, some):
        query_pos = lax.broadcasted_iota(jnp.int32, (some, span), 0) + (first + rows)
        key_pos = lax.broadcasted_iota(jnp.int32, (some, span), 1) + first
        allowed.append(
            (column[first : first + some] == ids_ref[:, first : first + span])
            & (jnp.abs(query_pos - key_pos) < rows)
        )
    for copy in copies:
        copy.wait()
    for half, first in enumerate((0, some)):
        for head in range(q_ref.shape[1] // HD):
            cols = slice(head * HD, (head + 1) * HD)
            score = lax.dot_general(
                q_ref[first : first + some, cols],
                keys[first : first + span, cols],
                NT,
                preferred_element_type=jnp.float32,
            )
            score = jnp.where(allowed[half], score * scale, -jnp.inf)
            weights = jnp.exp(score - jnp.max(score, axis=-1, keepdims=True))
            share = 1.0 / jnp.sum(weights, axis=-1, keepdims=True)
            probs = (weights * share).astype(jnp.bfloat16)
            both[first : first + some, cols] = jnp.dot(
                probs, values[first : first + span, cols], preferred_element_type=jnp.float32
            ).astype(jnp.bfloat16)
    at = pl.multiple_of(core * some, some)
    mine_ref[...] = both[pl.ds(at, some), :]
    theirs_ref[...] = both[pl.ds(some - at, some), :]


def attention(where, queries, ids, near_keys, near_values, *ahead):
    rows, width = queries.shape
    half = jax.ShapeDtypeStruct((rows // 2, width), jnp.bfloat16)
    return pl.pallas_call(
        attention_kernel,
        out_shape=(half, half),
        in_specs=[pl.BlockSpec(memory_space=pltpu.SMEM), VMEM, VMEM] + [ANY] * (6 + len(ahead)),
        out_specs=(VMEM, VMEM),
        scratch_shapes=[pltpu.VMEM((3 * rows, width), jnp.bfloat16)] * 2
        + [pltpu.VMEM((rows, width), jnp.bfloat16), pltpu.SemaphoreType.DMA((6,))],
        compiler_params=pltpu.CompilerParams(vmem_limit_bytes=63 * 1024 * 1024),
        name="window_attention",
    )(where, queries, ids, *near_keys, *near_values, *ahead)


def norm_kernel(mine_ref, theirs_ref, own_w, other_w, resid_ref, gain_ref, *refs):
    stream_ref, normed_ref = refs[-2:]
    stream = resid_ref[...].astype(jnp.float32)
    stream += jnp.dot(mine_ref[...], own_w[...], preferred_element_type=jnp.float32)
    stream += jnp.dot(theirs_ref[...], other_w[...], preferred_element_type=jnp.float32)
    meansq = jnp.mean(stream * stream, axis=-1, keepdims=True)
    stream_ref[...] = stream
    normed_ref[...] = (stream * lax.rsqrt(meansq + 1e-05) * gain_ref[...]).astype(jnp.bfloat16)


def project_and_norm(mine, theirs, own_w, other_w, resid, gain, *ahead):
    rows, width = resid.shape
    return pl.pallas_call(
        norm_kernel,
        out_shape=(
            jax.ShapeDtypeStruct((rows, width), jnp.float32),
            jax.ShapeDtypeStruct((rows, width), jnp.bfloat16),
        ),
        in_specs=[VMEM] * 6 + [ANY] * len(ahead),
        out_specs=(VMEM, VMEM),
        compiler_params=pltpu.CompilerParams(vmem_limit_bytes=63 * 1024 * 1024),
        name="project_and_norm",
    )(mine, theirs, own_w, other_w, resid, gain, *ahead)


def assemble_kernel(*refs):
    halves, (gate_up, down, sems) = refs[:6], refs[6:]
    units = halves[0].shape[0]
    copies = []
    for i, half in enumerate(halves):
        target, at = (gate_up, i * units) if i < 4 else (down, (i - 4) * units)
        copies.append(pltpu.make_async_copy(half, target.at[pl.ds(at, units), :], sems.at[i]))
    for copy in copies:
        copy.start()
    for copy in copies:
        copy.wait()


def assemble(halves):
    units, width = halves[0].shape
    return pl.pallas_call(
        assemble_kernel,
        out_shape=(
            jax.ShapeDtypeStruct((4 * units, width), jnp.bfloat16),
            jax.ShapeDtypeStruct((2 * units, width), jnp.bfloat16),
        ),
        in_specs=[ANY] * 6,
        out_specs=(VMEM, VMEM),
        scratch_shapes=[pltpu.SemaphoreType.DMA((6,))],
        compiler_params=pltpu.CompilerParams(vmem_limit_bytes=36 * 1024 * 1024),
        name="assemble_weights",
    )(*halves)


def gates_at(place, rows, pieces):
    piece = place.bit_length()
    at = (place - (1 << piece >> 1)) * rows
    return pieces[piece][:, at : at + rows]


def expert_kernel(places, pieces, where_ref, *refs):
    count = len(places)
    blocks, gates, (gate_up, down) = refs[:count], refs[count : count + pieces], refs[count + pieces :][:2]
    outs = refs[count + pieces + 2 :]
    units = down.shape[0]
    rows = blocks[0].shape[0]
    for first in range(0, count, 2):
        group = range(first, min(first + 2, count))
        tokens = jnp.concatenate([blocks[i][...] for i in group], axis=0)
        gate = lax.dot_general(tokens, gate_up[:units, :], NT, preferred_element_type=jnp.float32)
        up = lax.dot_general(tokens, gate_up[units:, :], NT, preferred_element_type=jnp.float32)
        act = (gate / (1.0 + jnp.exp(-gate)) * up).astype(jnp.bfloat16)
        result = jnp.dot(act, down[...], preferred_element_type=jnp.float32)
        for i in group:
            here, *other = [gates_at(place, rows, gates) for place in sorted(set(places[i]))]
            if other:
                swap = where_ref[1] == (1 if places[i][0] < places[i][1] else 0)
                here = jnp.where(swap, other[0], here)
            expert = lax.broadcasted_iota(jnp.int32, here.shape, 0)
            chosen = jnp.sum(jnp.where(expert == where_ref[0], here, 0.0), axis=0, keepdims=True)
            chosen = jnp.transpose(jnp.broadcast_to(chosen, (rows, rows)))[:, :1]
            part = result[(i - first) * rows : (i - first + 1) * rows]
            outs[i][...] = (part * chosen).astype(jnp.bfloat16)


def expert(blocks, places, where, gates, weights):
    rows, width = blocks[0].shape
    count = len(blocks)
    return pl.pallas_call(
        functools.partial(expert_kernel, places, len(gates)),
        out_shape=[jax.ShapeDtypeStruct((rows, width), jnp.bfloat16)] * count,
        in_specs=[pl.BlockSpec(memory_space=pltpu.SMEM)] + [VMEM] * (count + len(gates) + 2),
        out_specs=[VMEM] * count,
        compiler_params=pltpu.CompilerParams(vmem_limit_bytes=24 * 1024 * 1024),
        name="expert_rows",
    )(where, *blocks, *gates, *weights)


def add(*terms):
    total = terms[0].astype(jnp.float32)
    for term in terms[1:]:
        total = total + term.astype(jnp.float32)
    return total


def add_small(*terms):
    return add(*terms).astype(jnp.bfloat16)


UP, DOWN = 16, 32


def ring(block, hops):
    count = lax.axis_size("seq")
    return lax.ppermute(block, "seq", [((i + 4 * hops) % count, i) for i in range(count)])


def step_layer(normed, stream, run, weights):
    o = normed
    uo, wo, xo, yo = ring(o, 1), ring(o, -1), flip(o, 1), flip(o, 2)

    fo = ring(after(uo, weights[0]), 1)
    wx = ring(after(xo, wo, weights[0]), -1)
    do, uy = flip(after(yo, xo, weights[0]), 1), flip(after(uo, yo, weights[0]), 2)
    po, pxo, pyo, puo = run([after(o, wo), xo, yo, uo], (0, 1, 2, UP))

    ux, wy = ring(after(xo, fo, po), 1), ring(after(yo, wx, po), -1)
    fx, fy = flip(after(fo, do, po), 1), flip(after(fo, uy, po), 2)
    pwo, pfo, pwx, puy, pdo = run([after(wo, po), fo, wx, uy, do], (DOWN, 8, DOWN + 1, UP + 2, 3))

    ud, wd = ring(after(do, ux, pwo), 1), ring(after(do, wy, pwo), -1)
    fd = flip(after(fy, fx, pwo), 1)
    pux, pwy, pfx, pfy = run([after(ux, pwo), wy, fx, fy], (UP + 1, DOWN + 2, 9, 10))

    pfd, pud = run([after(fd, pux, wd), ud], (11, UP + 3))
    (pwd,) = run([after(wd, pfd)], (DOWN + 3,))
    to_fy, down, up = flip(pfd, 1), ring(pud, -1), ring(pwd, 1)

    pfy, pdo = add_small(pfy, to_fy), add_small(pdo, down, up)
    by_x, by_y = flip(after(pfx, to_fy), 1), flip(pfy, 2)
    to_xo, to_yo = ring(after(pux, down), -1), ring(after(pwy, up), 1)

    pfo, pxo, pyo = add_small(pfo, by_x, by_y), add_small(pxo, to_xo), add_small(pyo, to_yo)
    to_uo, to_xo = ring(after(pfo, to_xo), -1), ring(after(pwx, to_yo), 1)
    to_yo, by_y = flip(after(pdo, by_x), 1), flip(after(puy, by_y), 2)

    puo = add_small(puo, to_uo, by_y)
    pxo, pyo = add_small(pxo, to_xo), add_small(pyo, to_yo)
    down, up = ring(after(puo, to_uo), -1), ring(after(pwo, to_xo), 1)
    by_x, by_y = flip(after(pxo, to_yo), 1), flip(after(pyo, by_y), 2)
    return add(stream, po, down, up, by_x, by_y)


def expert_layer(normed, stream, where, gates, weights):
    count = lax.axis_size("seq")

    def run(blocks, masks):
        places = []
        for mask in masks:
            even = odd = mask
            if count == 16 and mask >= UP:
                even, odd = (4, 12) if mask < DOWN else (12, 4)
                even, odd = even + mask % 4, odd + mask % 4
            places.append((place_of(even), place_of(odd)))
        return expert(blocks, tuple(places), where, gates, weights)

    if count == 16:
        return step_layer(normed, stream, run, weights)
    blocks, mask = [normed], 1
    while mask < count:
        blocks = blocks + [flip(block, mask) for block in blocks]
        mask *= 2
    parts = []
    for first in range(0, count, 4):
        parts += run(blocks[first : first + 4], range(first, first + 4))
    while mask > 1:
        mask //= 2
        parts = [add_small(parts[i], flip(parts[i + mask], mask)) for i in range(mask)]
    return add(stream, parts[0])


def shards(
    queries,
    keys,
    values,
    resid,
    pair_ids,
    out_weight,
    norm_gain,
    experts,
    gates,
    w_gate,
    w_up,
    w_down,
):
    tok_rows = queries.shape[0]
    moe_rows = resid.shape[0]
    shard = lax.axis_index("seq")
    core = lax.axis_index("exp")
    count = lax.axis_size("seq")

    def halo(part):
        beside = flip(part, 1)
        ahead = [(i, i + 2) for i in range(0, count - 2, 2)]
        back = [(i + 2, i) for i in range(1, count - 2, 2)]
        return beside, part, lax.ppermute(beside, "seq", ahead + back)

    out_other = lax.ppermute(out_weight, "exp", SWAP)
    near_keys, near_values = halo(keys), halo(values)
    chosen = experts.T[:, None, :] == jnp.arange(count, dtype=jnp.int32)[None, :, None]
    all_gates = gather_gates(jnp.sum(jnp.where(chosen, gates.T[:, None, :], 0.0), axis=0))
    id_pad = jnp.pad(pair_ids, (tok_rows, tok_rows), constant_values=-1)
    ids = lax.dynamic_slice_in_dim(id_pad, shard * tok_rows, 3 * tok_rows, 0)[None, :]
    gate_w, up_w = jnp.swapaxes(w_gate[0], 0, 1), jnp.swapaxes(w_up[0], 0, 1)
    gate_other = lax.ppermute(gate_w, "exp", SWAP)
    ready = (*near_keys, *near_values, all_gates[-1], ids)
    up_other = lax.ppermute(after(up_w, *ready), "exp", SWAP)
    down_other = lax.ppermute(after(w_down[0], *ready), "exp", SWAP)
    halves = [gate_w, gate_other, up_w, up_other, w_down[0], down_other]

    where = jnp.stack([core, shard % 2])
    place = jnp.stack([shard, shard // 4 % 2])
    theirs, mine = attention(where, queries, ids, near_keys, near_values, out_other, gate_other)
    received = lax.ppermute(theirs, "exp", SWAP)
    stream, normed = project_and_norm(
        mine, received, out_weight, out_other, resid, norm_gain[None, :], up_other, down_other
    )
    mixed = expert_layer(normed, stream, place, all_gates, assemble(halves))
    return mixed.astype(jnp.bfloat16)


def solution(mesh):
    in_specs = (
        P("seq", "exp"),
        P("seq", "exp"),
        P("seq", "exp"),
        P(("seq", "exp"), None),
        P(),
        P("exp", None),
        P(),
        P(("seq", "exp"), None),
        P(("seq", "exp"), None),
        P("seq", None, "exp"),
        P("seq", None, "exp"),
        P("seq", "exp", None),
    )
    out_specs = P(("seq", "exp"), None)
    return jax.shard_map(shards, mesh=mesh, in_specs=in_specs, out_specs=out_specs, check_vma=False)
```

```python
import functools
import math

import jax
import jax.numpy as jnp
from jax import lax
from jax.experimental import pallas as pl
from jax.experimental.pallas import tpu as pltpu
from jax.sharding import PartitionSpec as P

HD = 128
SWAP = [(0, 1), (1, 0)]
VMEM = pl.BlockSpec(memory_space=pltpu.VMEM)
ANY = pl.BlockSpec(memory_space=pl.ANY)
NT = (((1,), (1,)), ((), ()))


def flip(block, mask):
    count = lax.axis_size("seq")
    return lax.ppermute(block, "seq", [(i, i ^ mask) for i in range(count)])


def after(block, *arrays):
    return lax.optimization_barrier((block, *arrays))[0]


def gate_order(count):
    masks = [1 << bit for bit in range(count.bit_length() - 1)]
    return masks[2:] + masks[1::-1]


def gather_gates(pieces, *waits):
    held = jnp.concatenate(pieces, axis=1) if len(pieces) > 1 else pieces[0]
    mask = gate_order(lax.axis_size("seq"))[len(pieces) - 1]
    return [*pieces, flip(after(held, *waits) if waits else held, mask)]


def place_of(j):
    return sum(1 << bit for bit, mask in enumerate(gate_order(lax.axis_size("seq"))) if j & mask)


def attention_kernel(where_ref, q_ref, ids_ref, *refs):
    keys, values, (theirs_ref, mine_ref, both) = refs[:3], refs[3:6], refs[-3:]
    rows = q_ref.shape[0]
    some = rows // 2
    core, odd = where_ref[0], where_ref[1]
    scale = 1.0 / math.sqrt(HD)
    ids = [ids_ref[:, i * rows : (i + 1) * rows] for i in range(3)]
    column = jnp.transpose(jnp.broadcast_to(ids[1], (HD, rows)))[:, :1]
    back, front = jnp.where(odd == 1, ids[0], ids[2]), jnp.where(odd == 1, ids[2], ids[0])
    apart = lax.broadcasted_iota(jnp.int32, (rows, rows), 0) - lax.broadcasted_iota(
        jnp.int32, (rows, rows), 1
    )
    side = rows * (2 * odd - 1)
    allowed = jnp.concatenate(
        [
            (column == back) & (jnp.abs(apart + side) < rows),
            column == ids[1],
            (column == front) & (jnp.abs(apart - side) < rows),
        ],
        axis=1,
    )
    for head in range(q_ref.shape[1] // HD):
        cols = slice(head * HD, (head + 1) * HD)
        query = q_ref[:, cols]
        score = jnp.concatenate(
            [
                lax.dot_general(query, ref[:, cols], NT, preferred_element_type=jnp.float32)
                for ref in keys
            ],
            axis=1,
        )
        score = jnp.where(allowed, score * scale, -jnp.inf)
        weights = jnp.exp(score - jnp.max(score, axis=-1, keepdims=True))
        share = 1.0 / jnp.sum(weights, axis=-1, keepdims=True)
        probs = (weights * share).astype(jnp.bfloat16)
        total = jnp.zeros((rows, HD), jnp.float32)
        for i, ref in enumerate(values):
            total += jnp.dot(
                probs[:, i * rows : (i + 1) * rows], ref[:, cols], preferred_element_type=jnp.float32
            )
        both[:, cols] = total.astype(jnp.bfloat16)
    at = pl.multiple_of(core * some, some)
    mine_ref[...] = both[pl.ds(at, some), :]
    theirs_ref[...] = both[pl.ds(some - at, some), :]


def attention(where, queries, ids, near_keys, near_values, *ahead):
    rows, width = queries.shape
    half = jax.ShapeDtypeStruct((rows // 2, width), jnp.bfloat16)
    return pl.pallas_call(
        attention_kernel,
        out_shape=(half, half),
        in_specs=[pl.BlockSpec(memory_space=pltpu.SMEM)] + [VMEM] * 8 + [ANY] * len(ahead),
        out_specs=(VMEM, VMEM),
        scratch_shapes=[pltpu.VMEM((rows, width), jnp.bfloat16)],
        compiler_params=pltpu.CompilerParams(vmem_limit_bytes=63 * 1024 * 1024),
        name="window_attention",
    )(where, queries, ids, *near_keys, *near_values, *ahead)


PIECES = 4


def norm_kernel(mine_ref, theirs_ref, own_w, other_w, resid_ref, gain_ref, *refs):
    stream_ref, normed_ref, weights, sems = refs[-4:]
    depth, piece = own_w.shape[0], own_w.shape[1] // PIECES
    copies = []
    for i in range(PIECES):
        cols = pl.ds(i * piece, piece)
        for half, ref in enumerate((own_w, other_w)):
            target = weights.at[pl.ds(half * depth, depth), cols]
            copies.append(pltpu.make_async_copy(ref.at[:, cols], target, sems.at[2 * i + half]))
    for copy in copies:
        copy.start()
    both = jnp.concatenate([mine_ref[...], theirs_ref[...]], axis=1)
    total = 0.0
    for i in range(PIECES):
        copies[2 * i].wait()
        copies[2 * i + 1].wait()
        cols = slice(i * piece, (i + 1) * piece)
        part = resid_ref[:, cols].astype(jnp.float32)
        part += jnp.dot(both, weights[:, cols], preferred_element_type=jnp.float32)
        stream_ref[:, cols] = part
        total += jnp.sum(part * part, axis=-1, keepdims=True)
    scale = lax.rsqrt(total / own_w.shape[1] + 1e-05)
    normed_ref[...] = (stream_ref[...] * scale * gain_ref[...]).astype(jnp.bfloat16)


def project_and_norm(mine, theirs, own_w, other_w, resid, gain, *ahead):
    rows, width = resid.shape
    return pl.pallas_call(
        norm_kernel,
        out_shape=(
            jax.ShapeDtypeStruct((rows, width), jnp.float32),
            jax.ShapeDtypeStruct((rows, width), jnp.bfloat16),
        ),
        in_specs=[VMEM] * 2 + [ANY] * 2 + [VMEM] * 2 + [ANY] * len(ahead),
        out_specs=(VMEM, VMEM),
        scratch_shapes=[
            pltpu.VMEM((2 * own_w.shape[0], width), jnp.bfloat16),
            pltpu.SemaphoreType.DMA((2 * PIECES,)),
        ],
        compiler_params=pltpu.CompilerParams(vmem_limit_bytes=63 * 1024 * 1024),
        name="project_and_norm",
    )(mine, theirs, own_w, other_w, resid, gain, *ahead)


def assemble_kernel(*refs):
    halves, (gate_up, down, sems) = refs[:6], refs[6:]
    units = halves[0].shape[0]
    copies = []
    for i, half in enumerate(halves):
        target, at = (gate_up, i * units) if i < 4 else (down, (i - 4) * units)
        copies.append(pltpu.make_async_copy(half, target.at[pl.ds(at, units), :], sems.at[i]))
    for copy in copies:
        copy.start()
    for copy in copies:
        copy.wait()


def assemble(halves):
    units, width = halves[0].shape
    return pl.pallas_call(
        assemble_kernel,
        out_shape=(
            jax.ShapeDtypeStruct((4 * units, width), jnp.bfloat16),
            jax.ShapeDtypeStruct((2 * units, width), jnp.bfloat16),
        ),
        in_specs=[ANY] * 6,
        out_specs=(VMEM, VMEM),
        scratch_shapes=[pltpu.SemaphoreType.DMA((6,))],
        compiler_params=pltpu.CompilerParams(vmem_limit_bytes=36 * 1024 * 1024),
        name="assemble_weights",
    )(*halves)


def expert_kernel(places, pieces, shard_ref, *refs):
    count = len(places)
    blocks, gates, (gate_up, down) = refs[:count], refs[count : count + pieces], refs[count + pieces :][:2]
    outs = refs[count + pieces + 2 :]
    units = down.shape[0]
    rows = blocks[0].shape[0]
    for first in range(0, count, 2):
        group = range(first, min(first + 2, count))
        tokens = jnp.concatenate([blocks[i][...] for i in group], axis=0)
        gate = lax.dot_general(tokens, gate_up[:units, :], NT, preferred_element_type=jnp.float32)
        up = lax.dot_general(tokens, gate_up[units:, :], NT, preferred_element_type=jnp.float32)
        act = (gate / (1.0 + jnp.exp(-gate)) * up).astype(jnp.bfloat16)
        result = jnp.dot(act, down[...], preferred_element_type=jnp.float32)
        for i in group:
            piece = places[i].bit_length()
            at = (places[i] - (1 << piece >> 1)) * rows
            here = gates[piece][:, at : at + rows]
            expert = lax.broadcasted_iota(jnp.int32, here.shape, 0)
            chosen = jnp.sum(jnp.where(expert == shard_ref[0], here, 0.0), axis=0, keepdims=True)
            chosen = jnp.transpose(jnp.broadcast_to(chosen, (rows, rows)))[:, :1]
            part = result[(i - first) * rows : (i - first + 1) * rows]
            outs[i][...] = (part * chosen).astype(jnp.bfloat16)


def expert(blocks, places, shard, gates, weights):
    rows, width = blocks[0].shape
    count = len(blocks)
    return pl.pallas_call(
        functools.partial(expert_kernel, places, len(gates)),
        out_shape=[jax.ShapeDtypeStruct((rows, width), jnp.bfloat16)] * count,
        in_specs=[pl.BlockSpec(memory_space=pltpu.SMEM)] + [VMEM] * (count + len(gates) + 2),
        out_specs=[VMEM] * count,
        compiler_params=pltpu.CompilerParams(vmem_limit_bytes=36 * 1024 * 1024),
        name="expert_rows",
    )(shard, *blocks, *gates, *weights)


def add(*terms):
    total = terms[0].astype(jnp.float32)
    for term in terms[1:]:
        total = total + term.astype(jnp.float32)
    return total


def add_small(*terms):
    return add(*terms).astype(jnp.bfloat16)


def shift(block, pairs):
    return lax.ppermute(block, "seq", [(4 * a + i, 4 * b + i) for a, b in pairs for i in range(4)])


OUTWARD, INWARD, MIDDLE = [(1, 0), (2, 3)], [(0, 1), (3, 2)], [(1, 2), (2, 1)]


def step_layer(normed, stream, run, gates, weights):
    z = lax.axis_index("seq") // 4
    inner = (z == 1) | (z == 2)

    o0 = normed
    o1, near3, x0, y0 = flip(o0, 4), shift(o0, MIDDLE), flip(o0, 1), flip(o0, 2)
    gates = gather_gates(gates, o0)

    ends2, near2 = shift(after(near3, o1), OUTWARD), shift(after(o1, near3), MIDDLE)
    d0, y1 = flip(after(y0, x0), 1), flip(after(o1, y0), 2)
    gates = gather_gates(gates, o1, y0)
    run = functools.partial(run, gates)

    ends3 = shift(after(near2, ends2), OUTWARD)
    o2 = jnp.where(inner, near2, ends2)
    x2, y2 = flip(after(o2, d0, weights[0]), 1), flip(after(o2, y1, weights[0]), 2)
    p0, px0, py0, pd0 = run([after(o0, o2), x0, y0, d0], (0, 1, 2, 3))

    x1 = flip(after(x0, ends3, p0), 4)
    o3 = jnp.where(inner, near3, ends3)
    x3, y3 = flip(after(o3, x2, p0), 1), flip(after(o3, y2, p0), 2)
    p1, py1, p2, px2, py2, p3 = run([after(o1, p0), y1, o2, x2, y2, o3], (4, 6, 8, 9, 10, 12))

    d1 = flip(after(d0, x1, p1), 4)
    d2, d3 = flip(after(y2, x3, p1), 1), flip(after(x3, y3, p1), 2)
    px3, py3, px1 = run([after(x3, p1), y3, x1], (13, 14, 5))

    pd2, pd3 = run([after(d2, px3), d3], (11, 15))
    (pd1,) = run([after(d1, pd2)], (7,))
    to_x3, to_y2, to_d0 = flip(pd3, 2), flip(pd2, 1), flip(pd1, 4)

    px3, py2, pd0 = add_small(px3, to_x3), add_small(py2, to_y2), add_small(pd0, to_d0)
    by_x, by_y = flip(after(px3, to_y2), 1), flip(after(py3, to_x3), 2)
    to_x0 = flip(after(px1, to_d0), 4)

    p3, px0 = add_small(p3, by_x, by_y), add_small(px0, to_x0)
    to_2 = shift(after(p3, to_x0), INWARD)
    by_x, by_y = flip(after(px2, by_x), 1), flip(after(py2, by_y), 2)

    p2 = add_small(p2, by_x, by_y, to_2)
    to_3, to_1 = shift(after(p2, to_2), INWARD), shift(p2, MIDDLE)
    to_y0, by_y = flip(after(pd0, by_x), 1), flip(after(py1, by_y), 2)

    p3, p1, py0 = add_small(p3, to_3), add_small(p1, by_y, to_1), add_small(py0, to_y0)
    by_z, by_middle = flip(after(p1, to_3), 4), shift(after(p3, to_1), MIDDLE)
    by_x, by_y = flip(after(px0, to_y0), 1), flip(after(py0, by_y), 2)
    return add(stream, p0, by_z, by_middle, by_x, by_y)


def expert_layer(normed, stream, shard, gates, weights):
    count = lax.axis_size("seq")

    def run(gates, blocks, masks):
        places = tuple(place_of(mask) for mask in masks)
        return expert(blocks, places, shard, gates, weights)

    if count == 16:
        return step_layer(normed, stream, run, gates, weights)
    while len(gates) < count.bit_length():
        gates = gather_gates(gates)
    blocks, mask = [normed], 1
    while mask < count:
        blocks = blocks + [flip(block, mask) for block in blocks]
        mask *= 2
    parts = []
    for first in range(0, count, 4):
        parts += run(gates, blocks[first : first + 4], range(first, first + 4))
    while mask > 1:
        mask //= 2
        parts = [add_small(parts[i], flip(parts[i + mask], mask)) for i in range(mask)]
    return add(stream, parts[0])


def shards(
    queries,
    keys,
    values,
    resid,
    pair_ids,
    out_weight,
    norm_gain,
    experts,
    gates,
    w_gate,
    w_up,
    w_down,
):
    tok_rows = queries.shape[0]
    moe_rows = resid.shape[0]
    shard = lax.axis_index("seq")
    core = lax.axis_index("exp")
    count = lax.axis_size("seq")

    def halo(part):
        beside = flip(part, 1)
        ahead = [(i, i + 2) for i in range(0, count - 2, 2)]
        back = [(i + 2, i) for i in range(1, count - 2, 2)]
        return beside, part, lax.ppermute(beside, "seq", ahead + back)

    near_keys, near_values = halo(keys), halo(values)
    chosen = experts.T[:, None, :] == jnp.arange(count, dtype=jnp.int32)[None, :, None]
    some_gates = [jnp.sum(jnp.where(chosen, gates.T[:, None, :], 0.0), axis=0)]
    some_gates = gather_gates(gather_gates(some_gates))
    id_pad = jnp.pad(pair_ids, (tok_rows, tok_rows), constant_values=-1)
    ids = lax.dynamic_slice_in_dim(id_pad, shard * tok_rows, 3 * tok_rows, 0)[None, :]
    out_other = lax.ppermute(out_weight, "exp", SWAP)
    gate_w, up_w = jnp.swapaxes(w_gate[0], 0, 1), jnp.swapaxes(w_up[0], 0, 1)
    gate_other = lax.ppermute(gate_w, "exp", SWAP)
    ready = (*near_keys, *near_values, some_gates[-1], ids)
    up_other = lax.ppermute(after(up_w, *ready), "exp", SWAP)
    down_other = lax.ppermute(after(w_down[0], *ready), "exp", SWAP)
    halves = [gate_w, gate_other, up_w, up_other, w_down[0], down_other]

    where = jnp.stack([core, shard % 2])
    theirs, mine = attention(where, queries, ids, near_keys, near_values, out_other, gate_other)
    received = lax.ppermute(theirs, "exp", SWAP)
    stream, normed = project_and_norm(
        mine, received, out_weight, out_other, resid, norm_gain[None, :], up_other, down_other
    )
    mixed = expert_layer(normed, stream, shard.reshape(1), some_gates, assemble(halves))
    return mixed.astype(jnp.bfloat16)


def solution(mesh):
    in_specs = (
        P("seq", "exp"),
        P("seq", "exp"),
        P("seq", "exp"),
        P(("seq", "exp"), None),
        P(),
        P("exp", None),
        P(),
        P(("seq", "exp"), None),
        P(("seq", "exp"), None),
        P("seq", None, "exp"),
        P("seq", None, "exp"),
        P("seq", "exp", None),
    )
    out_specs = P(("seq", "exp"), None)
    return jax.shard_map(shards, mesh=mesh, in_specs=in_specs, out_specs=out_specs, check_vma=False)
```

```python
import functools
import math

import jax
import jax.numpy as jnp
from jax import lax
from jax.experimental import pallas as pl
from jax.experimental.pallas import tpu as pltpu
from jax.sharding import PartitionSpec as P

HD = 128
SWAP = [(0, 1), (1, 0)]
VMEM = pl.BlockSpec(memory_space=pltpu.VMEM)
ANY = pl.BlockSpec(memory_space=pl.ANY)
NT = (((1,), (1,)), ((), ()))


def flip(block, mask):
    count = lax.axis_size("seq")
    return lax.ppermute(block, "seq", [(i, i ^ mask) for i in range(count)])


def cross(block, masks):
    count = lax.axis_size("seq")
    pairs = [(2 * i + c, 2 * (i ^ masks[c]) + c) for i in range(count) for c in range(2)]
    return lax.ppermute(block, ("seq", "exp"), pairs)


def after(block, *arrays):
    return lax.optimization_barrier((block, *arrays))[0]


def gate_order(count):
    masks = [1 << bit for bit in range(count.bit_length() - 1)]
    return masks[2:] + masks[1::-1]


def gather_gates(pieces, *waits):
    held = jnp.concatenate(pieces, axis=1) if len(pieces) > 1 else pieces[0]
    mask = gate_order(lax.axis_size("seq"))[len(pieces) - 1]
    return [*pieces, flip(after(held, *waits) if waits else held, mask)]


def place_of(j):
    return sum(1 << bit for bit, mask in enumerate(gate_order(lax.axis_size("seq"))) if j & mask)


def attention_kernel(where_ref, q_ref, ids_ref, *refs):
    keys, values, (theirs_ref, mine_ref, both) = refs[:3], refs[3:6], refs[-3:]
    rows = q_ref.shape[0]
    some = rows // 2
    core, odd = where_ref[0], where_ref[1]
    scale = 1.0 / math.sqrt(HD)
    ids = [ids_ref[:, i * rows : (i + 1) * rows] for i in range(3)]
    column = jnp.transpose(jnp.broadcast_to(ids[1], (HD, rows)))[:, :1]
    back, front = jnp.where(odd == 1, ids[0], ids[2]), jnp.where(odd == 1, ids[2], ids[0])
    apart = lax.broadcasted_iota(jnp.int32, (rows, rows), 0) - lax.broadcasted_iota(
        jnp.int32, (rows, rows), 1
    )
    side = rows * (2 * odd - 1)
    allowed = jnp.concatenate(
        [
            (column == back) & (jnp.abs(apart + side) < rows),
            column == ids[1],
            (column == front) & (jnp.abs(apart - side) < rows),
        ],
        axis=1,
    )
    for head in range(q_ref.shape[1] // HD):
        cols = slice(head * HD, (head + 1) * HD)
        query = q_ref[:, cols]
        score = jnp.concatenate(
            [
                lax.dot_general(query, ref[:, cols], NT, preferred_element_type=jnp.float32)
                for ref in keys
            ],
            axis=1,
        )
        score = jnp.where(allowed, score * scale, -jnp.inf)
        weights = jnp.exp(score - jnp.max(score, axis=-1, keepdims=True))
        share = 1.0 / jnp.sum(weights, axis=-1, keepdims=True)
        probs = (weights * share).astype(jnp.bfloat16)
        total = jnp.zeros((rows, HD), jnp.float32)
        for i, ref in enumerate(values):
            total += jnp.dot(
                probs[:, i * rows : (i + 1) * rows], ref[:, cols], preferred_element_type=jnp.float32
            )
        both[:, cols] = total.astype(jnp.bfloat16)
    at = pl.multiple_of(core * some, some)
    mine_ref[...] = both[pl.ds(at, some), :]
    theirs_ref[...] = both[pl.ds(some - at, some), :]


def attention(where, queries, ids, near_keys, near_values, *ahead):
    rows, width = queries.shape
    half = jax.ShapeDtypeStruct((rows // 2, width), jnp.bfloat16)
    return pl.pallas_call(
        attention_kernel,
        out_shape=(half, half),
        in_specs=[pl.BlockSpec(memory_space=pltpu.SMEM)] + [VMEM] * 8 + [ANY] * len(ahead),
        out_specs=(VMEM, VMEM),
        scratch_shapes=[pltpu.VMEM((rows, width), jnp.bfloat16)],
        compiler_params=pltpu.CompilerParams(vmem_limit_bytes=63 * 1024 * 1024),
        name="window_attention",
    )(where, queries, ids, *near_keys, *near_values, *ahead)


def norm_kernel(mine_ref, theirs_ref, own_w, other_w, resid_ref, gain_ref, *refs):
    stream_ref, normed_ref = refs[-2:]
    stream = resid_ref[...].astype(jnp.float32)
    stream += jnp.dot(mine_ref[...], own_w[...], preferred_element_type=jnp.float32)
    stream += jnp.dot(theirs_ref[...], other_w[...], preferred_element_type=jnp.float32)
    meansq = jnp.mean(stream * stream, axis=-1, keepdims=True)
    stream_ref[...] = stream
    normed_ref[...] = (stream * lax.rsqrt(meansq + 1e-05) * gain_ref[...]).astype(jnp.bfloat16)


def project_and_norm(mine, theirs, own_w, other_w, resid, gain, *ahead):
    rows, width = resid.shape
    return pl.pallas_call(
        norm_kernel,
        out_shape=(
            jax.ShapeDtypeStruct((rows, width), jnp.float32),
            jax.ShapeDtypeStruct((rows, width), jnp.bfloat16),
        ),
        in_specs=[VMEM] * 6 + [ANY] * len(ahead),
        out_specs=(VMEM, VMEM),
        compiler_params=pltpu.CompilerParams(vmem_limit_bytes=63 * 1024 * 1024),
        name="project_and_norm",
    )(mine, theirs, own_w, other_w, resid, gain, *ahead)


def assemble_kernel(*refs):
    halves, (gate_up, down, sems) = refs[:6], refs[6:]
    units = halves[0].shape[0]
    copies = []
    for i, half in enumerate(halves):
        target, at = (gate_up, i * units) if i < 4 else (down, (i - 4) * units)
        copies.append(pltpu.make_async_copy(half, target.at[pl.ds(at, units), :], sems.at[i]))
    for copy in copies:
        copy.start()
    for copy in copies:
        copy.wait()


def assemble(halves):
    units, width = halves[0].shape
    return pl.pallas_call(
        assemble_kernel,
        out_shape=(
            jax.ShapeDtypeStruct((4 * units, width), jnp.bfloat16),
            jax.ShapeDtypeStruct((2 * units, width), jnp.bfloat16),
        ),
        in_specs=[ANY] * 6,
        out_specs=(VMEM, VMEM),
        scratch_shapes=[pltpu.SemaphoreType.DMA((6,))],
        compiler_params=pltpu.CompilerParams(vmem_limit_bytes=36 * 1024 * 1024),
        name="assemble_weights",
    )(*halves)


def gates_at(place, rows, pieces):
    piece = place.bit_length()
    at = (place - (1 << piece >> 1)) * rows
    return pieces[piece][:, at : at + rows]


def expert_kernel(places, pieces, where_ref, *refs):
    count = len(places)
    blocks, gates, (gate_up, down) = refs[:count], refs[count : count + pieces], refs[count + pieces :][:2]
    outs = refs[count + pieces + 2 :]
    units = down.shape[0]
    rows = blocks[0].shape[0]
    for first in range(0, count, 2):
        group = range(first, min(first + 2, count))
        tokens = jnp.concatenate([blocks[i][...] for i in group], axis=0)
        gate = lax.dot_general(tokens, gate_up[:units, :], NT, preferred_element_type=jnp.float32)
        up = lax.dot_general(tokens, gate_up[units:, :], NT, preferred_element_type=jnp.float32)
        act = (gate / (1.0 + jnp.exp(-gate)) * up).astype(jnp.bfloat16)
        result = jnp.dot(act, down[...], preferred_element_type=jnp.float32)
        for i in group:
            here, other = (gates_at(place, rows, gates) for place in places[i])
            here = jnp.where(where_ref[1] == 1, other, here)
            expert = lax.broadcasted_iota(jnp.int32, here.shape, 0)
            chosen = jnp.sum(jnp.where(expert == where_ref[0], here, 0.0), axis=0, keepdims=True)
            chosen = jnp.transpose(jnp.broadcast_to(chosen, (rows, rows)))[:, :1]
            part = result[(i - first) * rows : (i - first + 1) * rows]
            outs[i][...] = (part * chosen).astype(jnp.bfloat16)


def expert(blocks, places, where, gates, weights):
    rows, width = blocks[0].shape
    count = len(blocks)
    return pl.pallas_call(
        functools.partial(expert_kernel, places, len(gates)),
        out_shape=[jax.ShapeDtypeStruct((rows, width), jnp.bfloat16)] * count,
        in_specs=[pl.BlockSpec(memory_space=pltpu.SMEM)] + [VMEM] * (count + len(gates) + 2),
        out_specs=[VMEM] * count,
        compiler_params=pltpu.CompilerParams(vmem_limit_bytes=36 * 1024 * 1024),
        name="expert_rows",
    )(where, *blocks, *gates, *weights)


def add(*terms):
    total = terms[0].astype(jnp.float32)
    for term in terms[1:]:
        total = total + term.astype(jnp.float32)
    return total


def add_small(*terms):
    return add(*terms).astype(jnp.bfloat16)


def shift(block, pairs):
    return lax.ppermute(block, "seq", [(4 * a + i, 4 * b + i) for a, b in pairs for i in range(4)])


OUTWARD, INWARD, MIDDLE = [(1, 0), (2, 3)], [(0, 1), (3, 2)], [(1, 2), (2, 1)]
X, Y = (1, 2), (2, 1)


def step_layer(normed, stream, run, weights):
    z = lax.axis_index("seq") // 4
    inner = (z == 1) | (z == 2)

    o0 = normed
    o1, near3, x0, y0 = flip(o0, 4), shift(o0, MIDDLE), cross(o0, X), cross(o0, Y)
    weights = weights(x0, y0)

    ends2, near2 = shift(after(near3, o1), OUTWARD), shift(after(o1, near3), MIDDLE)
    d0, y1 = cross(after(y0, x0), X), cross(after(o1, y0), Y)

    ends3 = shift(after(near2, ends2), OUTWARD)
    o2 = jnp.where(inner, near2, ends2)
    x2, y2 = cross(after(o2, d0, weights[0]), X), cross(after(o2, y1, weights[0]), Y)
    run = functools.partial(run, weights)
    p0, px0, py0, pd0 = run([after(o0, o2), x0, y0, d0], (0, X, Y, 3))

    x1 = flip(after(x0, ends3, p0), 4)
    o3 = jnp.where(inner, near3, ends3)
    x3, y3 = cross(after(o3, x2, p0), X), cross(after(o3, y2, p0), Y)
    p1, py1, p2, px2, py2, p3 = run(
        [after(o1, p0), y1, o2, x2, y2, o3], (4, plane(Y, 4), 8, plane(X, 8), plane(Y, 8), 12)
    )

    d1 = flip(after(d0, x1, p1), 4)
    d2, d3 = cross(after(y2, x3, p1), X), cross(after(x3, y3, p1), Y)
    px3, py3, px1 = run([after(x3, p1), y3, x1], (plane(X, 12), plane(Y, 12), plane(X, 4)))

    pd2, pd3 = run([after(d2, px3), d3], (11, 15))
    (pd1,) = run([after(d1, pd2)], (7,))
    to_x3, to_y2, to_d0 = cross(pd3, Y), cross(pd2, X), flip(pd1, 4)

    px3, py2, pd0 = add_small(px3, to_x3), add_small(py2, to_y2), add_small(pd0, to_d0)
    by_x, by_y = cross(after(px3, to_y2), X), cross(after(py3, to_x3), Y)
    to_x0 = flip(after(px1, to_d0), 4)

    p3, px0 = add_small(p3, by_x, by_y), add_small(px0, to_x0)
    to_2 = shift(after(p3, to_x0), INWARD)
    by_x, by_y = cross(after(px2, by_x), X), cross(after(py2, by_y), Y)

    p2 = add_small(p2, by_x, by_y, to_2)
    to_3, to_1 = shift(after(p2, to_2), INWARD), shift(p2, MIDDLE)
    to_y0, by_y = cross(after(pd0, by_x), X), cross(after(py1, by_y), Y)

    p3, p1, py0 = add_small(p3, to_3), add_small(p1, by_y, to_1), add_small(py0, to_y0)
    by_z, by_middle = flip(after(p1, to_3), 4), shift(after(p3, to_1), MIDDLE)
    by_x, by_y = cross(after(px0, to_y0), X), cross(after(py0, by_y), Y)
    return add(stream, p0, by_z, by_middle, by_x, by_y)


def plane(masks, distance):
    return tuple(mask + distance for mask in masks)


def expert_layer(normed, stream, where, gates, halves):
    count = lax.axis_size("seq")

    def weights(*waits):
        return assemble([after(half, *waits) for half in halves])

    def run(weights, blocks, masks):
        masks = [mask if isinstance(mask, tuple) else (mask, mask) for mask in masks]
        places = tuple(tuple(place_of(j) for j in mask) for mask in masks)
        return expert(blocks, places, where, gates, weights)

    if count == 16:
        return step_layer(normed, stream, run, weights)
    held = weights()
    blocks, mask = [normed], 1
    while mask < count:
        blocks = blocks + [flip(block, mask) for block in blocks]
        mask *= 2
    parts = []
    for first in range(0, count, 4):
        parts += run(held, blocks[first : first + 4], range(first, first + 4))
    while mask > 1:
        mask //= 2
        parts = [add_small(parts[i], flip(parts[i + mask], mask)) for i in range(mask)]
    return add(stream, parts[0])


def shards(
    queries,
    keys,
    values,
    resid,
    pair_ids,
    out_weight,
    norm_gain,
    experts,
    gates,
    w_gate,
    w_up,
    w_down,
):
    tok_rows = queries.shape[0]
    moe_rows = resid.shape[0]
    shard = lax.axis_index("seq")
    core = lax.axis_index("exp")
    count = lax.axis_size("seq")

    def halo(part):
        beside = flip(part, 1)
        ahead = [(i, i + 2) for i in range(0, count - 2, 2)]
        back = [(i + 2, i) for i in range(1, count - 2, 2)]
        return beside, part, lax.ppermute(beside, "seq", ahead + back)

    near_keys, near_values = halo(keys), halo(values)
    chosen = experts.T[:, None, :] == jnp.arange(count, dtype=jnp.int32)[None, :, None]
    some_gates = [jnp.sum(jnp.where(chosen, gates.T[:, None, :], 0.0), axis=0)]
    while len(some_gates) < count.bit_length() - 1:
        some_gates = gather_gates(some_gates)
    id_pad = jnp.pad(pair_ids, (tok_rows, tok_rows), constant_values=-1)
    ids = lax.dynamic_slice_in_dim(id_pad, shard * tok_rows, 3 * tok_rows, 0)[None, :]
    out_other = lax.ppermute(out_weight, "exp", SWAP)
    gate_w, up_w = jnp.swapaxes(w_gate[0], 0, 1), jnp.swapaxes(w_up[0], 0, 1)
    gate_other = lax.ppermute(gate_w, "exp", SWAP)
    ready = (*near_keys, *near_values, some_gates[-1], ids)
    up_other = lax.ppermute(after(up_w, *ready), "exp", SWAP)
    down_other = lax.ppermute(after(w_down[0], *ready), "exp", SWAP)
    halves = [gate_w, gate_other, up_w, up_other, w_down[0], down_other]

    where = jnp.stack([core, shard % 2])
    theirs, mine = attention(where, queries, ids, near_keys, near_values, out_other, gate_other)
    all_gates = gather_gates(some_gates, theirs)
    received = lax.ppermute(theirs, "exp", SWAP)
    stream, normed = project_and_norm(
        mine, received, out_weight, out_other, resid, norm_gain[None, :], up_other, down_other
    )
    mixed = expert_layer(normed, stream, jnp.stack([shard, core]), all_gates, halves)
    return mixed.astype(jnp.bfloat16)


def solution(mesh):
    in_specs = (
        P("seq", "exp"),
        P("seq", "exp"),
        P("seq", "exp"),
        P(("seq", "exp"), None),
        P(),
        P("exp", None),
        P(),
        P(("seq", "exp"), None),
        P(("seq", "exp"), None),
        P("seq", None, "exp"),
        P("seq", None, "exp"),
        P("seq", "exp", None),
    )
    out_specs = P(("seq", "exp"), None)
    return jax.shard_map(shards, mesh=mesh, in_specs=in_specs, out_specs=out_specs, check_vma=False)
```

```python
import functools
import math

import jax
import jax.numpy as jnp
from jax import lax
from jax.experimental import pallas as pl
from jax.experimental.pallas import tpu as pltpu
from jax.sharding import PartitionSpec as P

HD = 128
SWAP = [(0, 1), (1, 0)]
VMEM = pl.BlockSpec(memory_space=pltpu.VMEM)
ANY = pl.BlockSpec(memory_space=pl.ANY)
NT = (((1,), (1,)), ((), ()))


def flip(block, mask):
    count = lax.axis_size("seq")
    return lax.ppermute(block, "seq", [(i, i ^ mask) for i in range(count)])


def cross(block, masks):
    count = lax.axis_size("seq")
    pairs = [(2 * i + c, 2 * (i ^ masks[c]) + c) for i in range(count) for c in range(2)]
    return lax.ppermute(block, ("seq", "exp"), pairs)


def after(block, *arrays):
    return lax.optimization_barrier((block, *arrays))[0]


def gate_order(count):
    masks = [1 << bit for bit in range(count.bit_length() - 1)]
    return masks[2:] + masks[1::-1]


def gather_gates(pieces, *waits):
    held = jnp.concatenate(pieces, axis=1) if len(pieces) > 1 else pieces[0]
    mask = gate_order(lax.axis_size("seq"))[len(pieces) - 1]
    return [*pieces, flip(after(held, *waits) if waits else held, mask)]


def place_of(j):
    return sum(1 << bit for bit, mask in enumerate(gate_order(lax.axis_size("seq"))) if j & mask)


def attention_kernel(where_ref, q_ref, ids_ref, *refs):
    keys, values, (theirs_ref, mine_ref, both) = refs[:3], refs[3:6], refs[-3:]
    rows = q_ref.shape[0]
    some = rows // 2
    core, odd = where_ref[0], where_ref[1]
    scale = 1.0 / math.sqrt(HD)
    ids = [ids_ref[:, i * rows : (i + 1) * rows] for i in range(3)]
    column = jnp.transpose(jnp.broadcast_to(ids[1], (HD, rows)))[:, :1]
    back, front = jnp.where(odd == 1, ids[0], ids[2]), jnp.where(odd == 1, ids[2], ids[0])
    apart = lax.broadcasted_iota(jnp.int32, (rows, rows), 0) - lax.broadcasted_iota(
        jnp.int32, (rows, rows), 1
    )
    side = rows * (2 * odd - 1)
    allowed = jnp.concatenate(
        [
            (column == back) & (jnp.abs(apart + side) < rows),
            column == ids[1],
            (column == front) & (jnp.abs(apart - side) < rows),
        ],
        axis=1,
    )
    for head in range(q_ref.shape[1] // HD):
        cols = slice(head * HD, (head + 1) * HD)
        query = q_ref[:, cols]
        score = jnp.concatenate(
            [
                lax.dot_general(query, ref[:, cols], NT, preferred_element_type=jnp.float32)
                for ref in keys
            ],
            axis=1,
        )
        score = jnp.where(allowed, score * scale, -jnp.inf)
        weights = jnp.exp(score - jnp.max(score, axis=-1, keepdims=True))
        share = 1.0 / jnp.sum(weights, axis=-1, keepdims=True)
        probs = (weights * share).astype(jnp.bfloat16)
        total = jnp.zeros((rows, HD), jnp.float32)
        for i, ref in enumerate(values):
            total += jnp.dot(
                probs[:, i * rows : (i + 1) * rows], ref[:, cols], preferred_element_type=jnp.float32
            )
        both[:, cols] = total.astype(jnp.bfloat16)
    at = pl.multiple_of(core * some, some)
    mine_ref[...] = both[pl.ds(at, some), :]
    theirs_ref[...] = both[pl.ds(some - at, some), :]


def attention(where, queries, ids, near_keys, near_values, *ahead):
    rows, width = queries.shape
    half = jax.ShapeDtypeStruct((rows // 2, width), jnp.bfloat16)
    return pl.pallas_call(
        attention_kernel,
        out_shape=(half, half),
        in_specs=[pl.BlockSpec(memory_space=pltpu.SMEM)] + [VMEM] * 8 + [ANY] * len(ahead),
        out_specs=(VMEM, VMEM),
        scratch_shapes=[pltpu.VMEM((rows, width), jnp.bfloat16)],
        compiler_params=pltpu.CompilerParams(vmem_limit_bytes=63 * 1024 * 1024),
        name="window_attention",
    )(where, queries, ids, *near_keys, *near_values, *ahead)


def norm_kernel(mine_ref, theirs_ref, own_w, other_w, resid_ref, gain_ref, *refs):
    stream_ref, normed_ref = refs[-2:]
    stream = resid_ref[...].astype(jnp.float32)
    stream += jnp.dot(mine_ref[...], own_w[...], preferred_element_type=jnp.float32)
    stream += jnp.dot(theirs_ref[...], other_w[...], preferred_element_type=jnp.float32)
    meansq = jnp.mean(stream * stream, axis=-1, keepdims=True)
    stream_ref[...] = stream
    normed_ref[...] = (stream * lax.rsqrt(meansq + 1e-05) * gain_ref[...]).astype(jnp.bfloat16)


def project_and_norm(mine, theirs, own_w, other_w, resid, gain, *ahead):
    rows, width = resid.shape
    return pl.pallas_call(
        norm_kernel,
        out_shape=(
            jax.ShapeDtypeStruct((rows, width), jnp.float32),
            jax.ShapeDtypeStruct((rows, width), jnp.bfloat16),
        ),
        in_specs=[VMEM] * 6 + [ANY] * len(ahead),
        out_specs=(VMEM, VMEM),
        compiler_params=pltpu.CompilerParams(vmem_limit_bytes=63 * 1024 * 1024),
        name="project_and_norm",
    )(mine, theirs, own_w, other_w, resid, gain, *ahead)


def assemble_kernel(*refs):
    halves, (gate_up, down, sems) = refs[:6], refs[6:]
    units = halves[0].shape[0]
    copies = []
    for i, half in enumerate(halves):
        target, at = (gate_up, i * units) if i < 4 else (down, (i - 4) * units)
        copies.append(pltpu.make_async_copy(half, target.at[pl.ds(at, units), :], sems.at[i]))
    for copy in copies:
        copy.start()
    for copy in copies:
        copy.wait()


def assemble(halves):
    units, width = halves[0].shape
    return pl.pallas_call(
        assemble_kernel,
        out_shape=(
            jax.ShapeDtypeStruct((4 * units, width), jnp.bfloat16),
            jax.ShapeDtypeStruct((2 * units, width), jnp.bfloat16),
        ),
        in_specs=[ANY] * 6,
        out_specs=(VMEM, VMEM),
        scratch_shapes=[pltpu.SemaphoreType.DMA((6,))],
        compiler_params=pltpu.CompilerParams(vmem_limit_bytes=36 * 1024 * 1024),
        name="assemble_weights",
    )(*halves)


def gates_at(place, rows, pieces):
    piece = place.bit_length()
    at = (place - (1 << piece >> 1)) * rows
    return pieces[piece][:, at : at + rows]


def expert_kernel(places, pieces, where_ref, *refs):
    count = len(places)
    blocks, gates, (gate_up, down) = refs[:count], refs[count : count + pieces], refs[count + pieces :][:2]
    outs = refs[count + pieces + 2 :]
    units = down.shape[0]
    rows = blocks[0].shape[0]
    for first in range(0, count, 2):
        group = range(first, min(first + 2, count))
        tokens = jnp.concatenate([blocks[i][...] for i in group], axis=0)
        gate = lax.dot_general(tokens, gate_up[:units, :], NT, preferred_element_type=jnp.float32)
        up = lax.dot_general(tokens, gate_up[units:, :], NT, preferred_element_type=jnp.float32)
        act = (gate / (1.0 + jnp.exp(-gate)) * up).astype(jnp.bfloat16)
        result = jnp.dot(act, down[...], preferred_element_type=jnp.float32)
        for i in group:
            here, other = (gates_at(place, rows, gates) for place in places[i])
            here = jnp.where(where_ref[1] == 1, other, here)
            expert = lax.broadcasted_iota(jnp.int32, here.shape, 0)
            chosen = jnp.sum(jnp.where(expert == where_ref[0], here, 0.0), axis=0, keepdims=True)
            chosen = jnp.transpose(jnp.broadcast_to(chosen, (rows, rows)))[:, :1]
            part = result[(i - first) * rows : (i - first + 1) * rows]
            outs[i][...] = (part * chosen).astype(jnp.bfloat16)


def expert(blocks, places, where, gates, weights):
    rows, width = blocks[0].shape
    count = len(blocks)
    return pl.pallas_call(
        functools.partial(expert_kernel, places, len(gates)),
        out_shape=[jax.ShapeDtypeStruct((rows, width), jnp.bfloat16)] * count,
        in_specs=[pl.BlockSpec(memory_space=pltpu.SMEM)] + [VMEM] * (count + len(gates) + 2),
        out_specs=[VMEM] * count,
        compiler_params=pltpu.CompilerParams(vmem_limit_bytes=36 * 1024 * 1024),
        name="expert_rows",
    )(where, *blocks, *gates, *weights)


def add(*terms):
    total = terms[0].astype(jnp.float32)
    for term in terms[1:]:
        total = total + term.astype(jnp.float32)
    return total


def add_small(*terms):
    return add(*terms).astype(jnp.bfloat16)


def shift(block, pairs):
    return lax.ppermute(block, "seq", [(4 * a + i, 4 * b + i) for a, b in pairs for i in range(4)])


OUTWARD, INWARD, MIDDLE = [(1, 0), (2, 3)], [(0, 1), (3, 2)], [(1, 2), (2, 1)]
X, Y = (1, 2), (2, 1)


def step_layer(normed, stream, run, weights):
    z = lax.axis_index("seq") // 4
    inner = (z == 1) | (z == 2)

    o0 = normed
    o1, near3, x0, y0 = flip(o0, 4), shift(o0, MIDDLE), cross(o0, X), cross(o0, Y)
    weights = weights(x0, y0)

    ends2, near2 = shift(near3, OUTWARD), shift(o1, MIDDLE)
    d0, y1 = cross(after(y0, x0), X), cross(after(o1, y0), Y)

    ends3 = shift(after(near2, ends2), OUTWARD)
    o2 = jnp.where(inner, near2, ends2)
    x2, y2 = cross(after(o2, d0, weights[0]), X), cross(after(o2, y1, weights[0]), Y)
    run = functools.partial(run, weights)
    p0, px0, py0, pd0 = run([after(o0, o2), x0, y0, d0], (0, X, Y, 3))

    x1 = flip(after(x0, ends3, p0), 4)
    o3 = jnp.where(inner, near3, ends3)
    x3, y3 = cross(after(o3, x2, p0), X), cross(after(o3, y2, p0), Y)
    p1, py1, p2, px2, py2, p3 = run(
        [after(o1, p0), y1, o2, x2, y2, o3], (4, plane(Y, 4), 8, plane(X, 8), plane(Y, 8), 12)
    )

    d1 = flip(after(d0, x1, p1), 4)
    d2, d3 = cross(after(y2, x3, p1), X), cross(after(x3, y3, p1), Y)
    px3, py3, px1 = run([after(x3, p1), y3, x1], (plane(X, 12), plane(Y, 12), plane(X, 4)))

    pd2, pd3 = run([after(d2, px3), d3], (11, 15))
    (pd1,) = run([after(d1, pd2)], (7,))
    to_x3, to_y2, to_d0 = cross(pd3, Y), cross(pd2, X), flip(pd1, 4)

    px3, py2, pd0 = add_small(px3, to_x3), add_small(py2, to_y2), add_small(pd0, to_d0)
    by_x, by_y = cross(after(px3, to_y2), X), cross(after(py3, to_x3), Y)
    to_x0 = flip(after(px1, to_d0), 4)

    p3, px0 = add_small(p3, by_x, by_y), add_small(px0, to_x0)
    to_2 = shift(after(p3, to_x0), INWARD)
    by_x, by_y = cross(after(px2, by_x), X), cross(after(py2, by_y), Y)

    p2 = add_small(p2, by_x, by_y, to_2)
    to_3, to_1 = shift(after(p2, to_2), INWARD), shift(p2, MIDDLE)
    to_y0, by_y = cross(after(pd0, by_x), X), cross(after(py1, by_y), Y)

    p1, py0 = add_small(p1, by_y, to_1), add_small(py0, to_y0)
    p3 = add_small(after(p3, p1), to_3)
    by_z, by_middle = flip(after(p1, to_3), 4), shift(p3, MIDDLE)
    by_x, by_y = cross(after(px0, to_y0), X), cross(after(py0, by_y), Y)
    return add(stream, p0, by_z, by_middle, by_x, by_y)


def plane(masks, distance):
    return tuple(mask + distance for mask in masks)


def expert_layer(normed, stream, where, gates, halves):
    count = lax.axis_size("seq")

    def weights(*waits):
        return assemble([after(half, *waits) for half in halves])

    def run(weights, blocks, masks):
        masks = [mask if isinstance(mask, tuple) else (mask, mask) for mask in masks]
        places = tuple(tuple(place_of(j) for j in mask) for mask in masks)
        return expert(blocks, places, where, gates, weights)

    if count == 16:
        return step_layer(normed, stream, run, weights)
    held = weights()
    blocks, mask = [normed], 1
    while mask < count:
        blocks = blocks + [flip(block, mask) for block in blocks]
        mask *= 2
    parts = []
    for first in range(0, count, 4):
        parts += run(held, blocks[first : first + 4], range(first, first + 4))
    while mask > 1:
        mask //= 2
        parts = [add_small(parts[i], flip(parts[i + mask], mask)) for i in range(mask)]
    return add(stream, parts[0])


def shards(
    queries,
    keys,
    values,
    resid,
    pair_ids,
    out_weight,
    norm_gain,
    experts,
    gates,
    w_gate,
    w_up,
    w_down,
):
    tok_rows = queries.shape[0]
    moe_rows = resid.shape[0]
    shard = lax.axis_index("seq")
    core = lax.axis_index("exp")
    count = lax.axis_size("seq")

    def halo(part):
        beside = flip(part, 1)
        ahead = [(i, i + 2) for i in range(0, count - 2, 2)]
        back = [(i + 2, i) for i in range(1, count - 2, 2)]
        return beside, part, lax.ppermute(beside, "seq", ahead + back)

    near_keys, near_values = halo(keys), halo(values)
    chosen = experts.T[:, None, :] == jnp.arange(count, dtype=jnp.int32)[None, :, None]
    some_gates = [jnp.sum(jnp.where(chosen, gates.T[:, None, :], 0.0), axis=0)]
    while len(some_gates) < count.bit_length() - 1:
        some_gates = gather_gates(some_gates)
    id_pad = jnp.pad(pair_ids, (tok_rows, tok_rows), constant_values=-1)
    ids = lax.dynamic_slice_in_dim(id_pad, shard * tok_rows, 3 * tok_rows, 0)[None, :]
    out_other = lax.ppermute(out_weight, "exp", SWAP)
    gate_w, up_w = jnp.swapaxes(w_gate[0], 0, 1), jnp.swapaxes(w_up[0], 0, 1)
    gate_other = lax.ppermute(gate_w, "exp", SWAP)
    where = jnp.stack([core, shard % 2])
    ready = (where, *near_keys, *near_values, some_gates[-1], ids)
    up_other = lax.ppermute(after(up_w, *ready), "exp", SWAP)
    down_other = lax.ppermute(after(w_down[0], *ready), "exp", SWAP)
    halves = [gate_w, gate_other, up_w, up_other, w_down[0], down_other]

    theirs, mine = attention(where, queries, ids, near_keys, near_values, out_other, gate_other)
    all_gates = gather_gates(some_gates, theirs)
    received = lax.ppermute(theirs, "exp", SWAP)
    stream, normed = project_and_norm(
        mine, received, out_weight, out_other, resid, norm_gain[None, :], up_other, down_other
    )
    mixed = expert_layer(normed, stream, jnp.stack([shard, core]), all_gates, halves)
    return mixed.astype(jnp.bfloat16)


def solution(mesh):
    in_specs = (
        P("seq", "exp"),
        P("seq", "exp"),
        P("seq", "exp"),
        P(("seq", "exp"), None),
        P(),
        P("exp", None),
        P(),
        P(("seq", "exp"), None),
        P(("seq", "exp"), None),
        P("seq", None, "exp"),
        P("seq", None, "exp"),
        P("seq", "exp", None),
    )
    out_specs = P(("seq", "exp"), None)
    return jax.shard_map(shards, mesh=mesh, in_specs=in_specs, out_specs=out_specs, check_vma=False)
```

```python
import functools
import math

import jax
import jax.numpy as jnp
from jax import lax
from jax.experimental import pallas as pl
from jax.experimental.pallas import tpu as pltpu
from jax.sharding import PartitionSpec as P

HD = 128
SWAP = [(0, 1), (1, 0)]
VMEM = pl.BlockSpec(memory_space=pltpu.VMEM)
ANY = pl.BlockSpec(memory_space=pl.ANY)
NT = (((1,), (1,)), ((), ()))


def flip(block, mask):
    count = lax.axis_size("seq")
    return lax.ppermute(block, "seq", [(i, i ^ mask) for i in range(count)])


def cross(block, masks):
    count = lax.axis_size("seq")
    pairs = [(2 * i + c, 2 * (i ^ masks[c]) + c) for i in range(count) for c in range(2)]
    return lax.ppermute(block, ("seq", "exp"), pairs)


def after(block, *arrays):
    return lax.optimization_barrier((block, *arrays))[0]


def gate_order(count):
    masks = [1 << bit for bit in range(count.bit_length() - 1)]
    return masks[2:] + masks[1::-1]


def gather_gates(pieces, *waits):
    held = jnp.concatenate(pieces, axis=1) if len(pieces) > 1 else pieces[0]
    mask = gate_order(lax.axis_size("seq"))[len(pieces) - 1]
    return [*pieces, flip(after(held, *waits) if waits else held, mask)]


def place_of(j):
    return sum(1 << bit for bit, mask in enumerate(gate_order(lax.axis_size("seq"))) if j & mask)


def attention_kernel(where_ref, q_ref, ids_ref, *refs):
    keys, values, (theirs_ref, mine_ref, both) = refs[:3], refs[3:6], refs[-3:]
    rows = q_ref.shape[0]
    some = rows // 2
    core, odd = where_ref[0], where_ref[1]
    scale = 1.0 / math.sqrt(HD)
    ids = [ids_ref[:, i * rows : (i + 1) * rows] for i in range(3)]
    column = jnp.transpose(jnp.broadcast_to(ids[1], (HD, rows)))[:, :1]
    back, front = jnp.where(odd == 1, ids[0], ids[2]), jnp.where(odd == 1, ids[2], ids[0])
    apart = lax.broadcasted_iota(jnp.int32, (rows, rows), 0) - lax.broadcasted_iota(
        jnp.int32, (rows, rows), 1
    )
    side = rows * (2 * odd - 1)
    allowed = jnp.concatenate(
        [
            (column == back) & (jnp.abs(apart + side) < rows),
            column == ids[1],
            (column == front) & (jnp.abs(apart - side) < rows),
        ],
        axis=1,
    )
    for head in range(q_ref.shape[1] // HD):
        cols = slice(head * HD, (head + 1) * HD)
        query = q_ref[:, cols]
        score = jnp.concatenate(
            [
                lax.dot_general(query, ref[:, cols], NT, preferred_element_type=jnp.float32)
                for ref in keys
            ],
            axis=1,
        )
        score = jnp.where(allowed, score * scale, -jnp.inf)
        weights = jnp.exp(score - jnp.max(score, axis=-1, keepdims=True))
        share = 1.0 / jnp.sum(weights, axis=-1, keepdims=True)
        probs = (weights * share).astype(jnp.bfloat16)
        total = jnp.zeros((rows, HD), jnp.float32)
        for i, ref in enumerate(values):
            total += jnp.dot(
                probs[:, i * rows : (i + 1) * rows], ref[:, cols], preferred_element_type=jnp.float32
            )
        both[:, cols] = total.astype(jnp.bfloat16)
    at = pl.multiple_of(core * some, some)
    mine_ref[...] = both[pl.ds(at, some), :]
    theirs_ref[...] = both[pl.ds(some - at, some), :]


def attention(where, queries, ids, near_keys, near_values, *ahead):
    rows, width = queries.shape
    half = jax.ShapeDtypeStruct((rows // 2, width), jnp.bfloat16)
    return pl.pallas_call(
        attention_kernel,
        out_shape=(half, half),
        in_specs=[pl.BlockSpec(memory_space=pltpu.SMEM)] + [VMEM] * 8 + [ANY] * len(ahead),
        out_specs=(VMEM, VMEM),
        scratch_shapes=[pltpu.VMEM((rows, width), jnp.bfloat16)],
        compiler_params=pltpu.CompilerParams(vmem_limit_bytes=63 * 1024 * 1024),
        name="window_attention",
    )(where, queries, ids, *near_keys, *near_values, *ahead)


def norm_kernel(mine_ref, theirs_ref, own_w, other_w, resid_ref, gain_ref, *refs):
    stream_ref, normed_ref = refs[-2:]
    stream = resid_ref[...].astype(jnp.float32)
    stream += jnp.dot(mine_ref[...], own_w[...], preferred_element_type=jnp.float32)
    stream += jnp.dot(theirs_ref[...], other_w[...], preferred_element_type=jnp.float32)
    meansq = jnp.mean(stream * stream, axis=-1, keepdims=True)
    stream_ref[...] = stream
    normed_ref[...] = (stream * lax.rsqrt(meansq + 1e-05) * gain_ref[...]).astype(jnp.bfloat16)


def project_and_norm(mine, theirs, own_w, other_w, resid, gain, *ahead):
    rows, width = resid.shape
    return pl.pallas_call(
        norm_kernel,
        out_shape=(
            jax.ShapeDtypeStruct((rows, width), jnp.float32),
            jax.ShapeDtypeStruct((rows, width), jnp.bfloat16),
        ),
        in_specs=[VMEM] * 6 + [ANY] * len(ahead),
        out_specs=(VMEM, VMEM),
        compiler_params=pltpu.CompilerParams(vmem_limit_bytes=63 * 1024 * 1024),
        name="project_and_norm",
    )(mine, theirs, own_w, other_w, resid, gain, *ahead)


def assemble_kernel(*refs):
    halves, (gate_up, down, sems) = refs[:6], refs[6:]
    units = halves[0].shape[0]
    copies = []
    for i, half in enumerate(halves):
        target, at = (gate_up, i * units) if i < 4 else (down, (i - 4) * units)
        copies.append(pltpu.make_async_copy(half, target.at[pl.ds(at, units), :], sems.at[i]))
    for copy in copies:
        copy.start()
    for copy in copies:
        copy.wait()


def assemble(halves):
    units, width = halves[0].shape
    return pl.pallas_call(
        assemble_kernel,
        out_shape=(
            jax.ShapeDtypeStruct((4 * units, width), jnp.bfloat16),
            jax.ShapeDtypeStruct((2 * units, width), jnp.bfloat16),
        ),
        in_specs=[ANY] * 6,
        out_specs=(VMEM, VMEM),
        scratch_shapes=[pltpu.SemaphoreType.DMA((6,))],
        compiler_params=pltpu.CompilerParams(vmem_limit_bytes=36 * 1024 * 1024),
        name="assemble_weights",
    )(*halves)


def gates_at(place, rows, pieces):
    piece = place.bit_length()
    at = (place - (1 << piece >> 1)) * rows
    return pieces[piece][:, at : at + rows]


def expert_kernel(places, pieces, where_ref, *refs):
    count = len(places)
    blocks, gates, (gate_up, down) = refs[:count], refs[count : count + pieces], refs[count + pieces :][:2]
    outs = refs[count + pieces + 2 :]
    units = down.shape[0]
    rows = blocks[0].shape[0]
    for first in range(0, count, 2):
        group = range(first, min(first + 2, count))
        tokens = jnp.concatenate([blocks[i][...] for i in group], axis=0)
        gate = lax.dot_general(tokens, gate_up[:units, :], NT, preferred_element_type=jnp.float32)
        up = lax.dot_general(tokens, gate_up[units:, :], NT, preferred_element_type=jnp.float32)
        act = (gate / (1.0 + jnp.exp(-gate)) * up).astype(jnp.bfloat16)
        result = jnp.dot(act, down[...], preferred_element_type=jnp.float32)
        for i in group:
            here, other = (gates_at(place, rows, gates) for place in places[i])
            here = jnp.where(where_ref[1] == 1, other, here)
            expert = lax.broadcasted_iota(jnp.int32, here.shape, 0)
            chosen = jnp.sum(jnp.where(expert == where_ref[0], here, 0.0), axis=0, keepdims=True)
            chosen = jnp.transpose(jnp.broadcast_to(chosen, (rows, rows)))[:, :1]
            part = result[(i - first) * rows : (i - first + 1) * rows]
            outs[i][...] = (part * chosen).astype(jnp.bfloat16)


def expert(blocks, places, where, gates, weights):
    rows, width = blocks[0].shape
    count = len(blocks)
    return pl.pallas_call(
        functools.partial(expert_kernel, places, len(gates)),
        out_shape=[jax.ShapeDtypeStruct((rows, width), jnp.bfloat16)] * count,
        in_specs=[pl.BlockSpec(memory_space=pltpu.SMEM)] + [VMEM] * (count + len(gates) + 2),
        out_specs=[VMEM] * count,
        compiler_params=pltpu.CompilerParams(vmem_limit_bytes=36 * 1024 * 1024),
        name="expert_rows",
    )(where, *blocks, *gates, *weights)


def add(*terms):
    total = terms[0].astype(jnp.float32)
    for term in terms[1:]:
        total = total + term.astype(jnp.float32)
    return total


def add_small(*terms):
    return add(*terms).astype(jnp.bfloat16)


def shift(block, pairs):
    return lax.ppermute(block, "seq", [(4 * a + i, 4 * b + i) for a, b in pairs for i in range(4)])


OUTWARD, INWARD, MIDDLE = [(1, 0), (2, 3)], [(0, 1), (3, 2)], [(1, 2), (2, 1)]
X, Y = (1, 2), (2, 1)


def step_layer(normed, stream, run, weights):
    z = lax.axis_index("seq") // 4
    inner = (z == 1) | (z == 2)

    o0 = normed
    o1, near3, x0, y0 = flip(o0, 4), shift(o0, MIDDLE), cross(o0, X), cross(o0, Y)
    weights = weights(x0, y0)

    ends2, near2 = shift(near3, OUTWARD), shift(o1, MIDDLE)
    d0, y1 = cross(after(y0, x0), X), cross(after(o1, y0), Y)

    o2 = jnp.where(inner, near2, ends2)
    ends3 = shift(after(near2, o2, d0, y1), OUTWARD)
    x2, y2 = cross(after(o2, d0, weights[0]), X), cross(after(o2, y1, weights[0]), Y)
    run = functools.partial(run, weights)
    p0, px0, py0, pd0 = run([after(o0, o2), x0, y0, d0], (0, X, Y, 3))

    o3 = jnp.where(inner, near3, after(ends3, x2, y2))
    x1 = flip(after(x0, ends3, p0), 4)
    x3, y3 = cross(after(o3, x2, p0), X), cross(after(o3, y2, p0), Y)
    p1, py1, p2, px2, py2, p3 = run(
        [after(o1, p0), y1, o2, x2, y2, o3], (4, plane(Y, 4), 8, plane(X, 8), plane(Y, 8), 12)
    )

    d1 = flip(after(d0, x1, p1), 4)
    d2, d3 = cross(after(y2, x3, p1), X), cross(after(x3, y3, p1), Y)
    px3, py3, px1 = run([after(x3, p1), y3, x1], (plane(X, 12), plane(Y, 12), plane(X, 4)))

    pd2, pd3 = run([after(d2, px3), d3], (11, 15))
    (pd1,) = run([after(d1, pd2)], (7,))
    to_x3, to_y2, to_d0 = cross(pd3, Y), cross(pd2, X), flip(pd1, 4)

    px3, py2, pd0 = add_small(px3, to_x3), add_small(py2, to_y2), add_small(pd0, to_d0)
    by_x, by_y = cross(after(px3, to_y2), X), cross(after(py3, to_x3), Y)
    to_x0 = flip(after(px1, to_d0), 4)

    p3, px0 = add_small(p3, by_x, by_y), add_small(px0, to_x0)
    to_2 = shift(after(p3, to_x0), INWARD)
    by_x, by_y = cross(after(px2, by_x), X), cross(after(py2, by_y), Y)

    p2 = add_small(p2, by_x, by_y, to_2)
    to_3, to_1 = shift(after(p2, to_2), INWARD), shift(p2, MIDDLE)
    to_y0, by_y = cross(after(pd0, by_x), X), cross(after(py1, by_y), Y)

    p1, py0 = add_small(p1, by_y, to_1), add_small(py0, to_y0)
    p3 = add_small(after(p3, p1), to_3)
    by_middle, by_z = shift(p3, MIDDLE), flip(p1, 4)
    by_x, by_y = cross(after(px0, to_y0), X), cross(after(py0, by_y), Y)
    return add(stream, p0, by_x, by_y, by_z, by_middle)


def plane(masks, distance):
    return tuple(mask + distance for mask in masks)


def expert_layer(normed, stream, where, gates, halves):
    count = lax.axis_size("seq")

    def weights(*waits):
        return assemble([after(half, gates[-1], *waits) for half in halves])

    def run(weights, blocks, masks):
        masks = [mask if isinstance(mask, tuple) else (mask, mask) for mask in masks]
        places = tuple(tuple(place_of(j) for j in mask) for mask in masks)
        return expert(blocks, places, where, gates, weights)

    if count == 16:
        return step_layer(normed, stream, run, weights)
    held = weights()
    blocks, mask = [normed], 1
    while mask < count:
        blocks = blocks + [flip(block, mask) for block in blocks]
        mask *= 2
    parts = []
    for first in range(0, count, 4):
        parts += run(held, blocks[first : first + 4], range(first, first + 4))
    while mask > 1:
        mask //= 2
        parts = [add_small(parts[i], flip(parts[i + mask], mask)) for i in range(mask)]
    return add(stream, parts[0])


def shards(
    queries,
    keys,
    values,
    resid,
    pair_ids,
    out_weight,
    norm_gain,
    experts,
    gates,
    w_gate,
    w_up,
    w_down,
):
    tok_rows = queries.shape[0]
    moe_rows = resid.shape[0]
    shard = lax.axis_index("seq")
    core = lax.axis_index("exp")
    count = lax.axis_size("seq")

    def halo(part):
        beside = flip(part, 1)
        ahead = [(i, i + 2) for i in range(0, count - 2, 2)]
        back = [(i + 2, i) for i in range(1, count - 2, 2)]
        return beside, part, lax.ppermute(beside, "seq", ahead + back)

    near_keys, near_values = halo(keys), halo(values)
    chosen = experts.T[:, None, :] == jnp.arange(count, dtype=jnp.int32)[None, :, None]
    some_gates = [jnp.sum(jnp.where(chosen, gates.T[:, None, :], 0.0), axis=0)]
    while len(some_gates) < count.bit_length() - 1:
        some_gates = gather_gates(some_gates)
    id_pad = jnp.pad(pair_ids, (tok_rows, tok_rows), constant_values=-1)
    ids = lax.dynamic_slice_in_dim(id_pad, shard * tok_rows, 3 * tok_rows, 0)[None, :]
    out_other = lax.ppermute(out_weight, "exp", SWAP)
    gate_w, up_w = jnp.swapaxes(w_gate[0], 0, 1), jnp.swapaxes(w_up[0], 0, 1)
    gate_other = lax.ppermute(gate_w, "exp", SWAP)
    where = jnp.stack([core, shard % 2])
    ready = (where, *near_keys, *near_values, some_gates[-1], ids)
    up_other = lax.ppermute(after(up_w, *ready), "exp", SWAP)
    down_other = lax.ppermute(after(w_down[0], *ready), "exp", SWAP)
    halves = [gate_w, gate_other, up_w, up_other, w_down[0], down_other]

    theirs, mine = attention(where, queries, ids, near_keys, near_values, out_other, gate_other)
    all_gates = gather_gates(some_gates, theirs)
    received = lax.ppermute(theirs, "exp", SWAP)
    stream, normed = project_and_norm(
        mine, received, out_weight, out_other, resid, norm_gain[None, :], up_other, down_other
    )
    mixed = expert_layer(normed, stream, jnp.stack([shard, core]), all_gates, halves)
    return mixed.astype(jnp.bfloat16)


def solution(mesh):
    in_specs = (
        P("seq", "exp"),
        P("seq", "exp"),
        P("seq", "exp"),
        P(("seq", "exp"), None),
        P(),
        P("exp", None),
        P(),
        P(("seq", "exp"), None),
        P(("seq", "exp"), None),
        P("seq", None, "exp"),
        P("seq", None, "exp"),
        P("seq", "exp", None),
    )
    out_specs = P(("seq", "exp"), None)
    return jax.shard_map(shards, mesh=mesh, in_specs=in_specs, out_specs=out_specs, check_vma=False)
```

```python
import functools
import math

import jax
import jax.numpy as jnp
from jax import lax
from jax.experimental import pallas as pl
from jax.experimental.pallas import tpu as pltpu
from jax.sharding import PartitionSpec as P

HD = 128
SWAP = [(0, 1), (1, 0)]
VMEM = pl.BlockSpec(memory_space=pltpu.VMEM)
ANY = pl.BlockSpec(memory_space=pl.ANY)
NT = (((1,), (1,)), ((), ()))


def flip(block, mask):
    count = lax.axis_size("seq")
    return lax.ppermute(block, "seq", [(i, i ^ mask) for i in range(count)])


def cross(block, masks):
    count = lax.axis_size("seq")
    pairs = [(2 * i + c, 2 * (i ^ masks[c]) + c) for i in range(count) for c in range(2)]
    return lax.ppermute(block, ("seq", "exp"), pairs)


def after(block, *arrays):
    return lax.optimization_barrier((block, *arrays))[0]


def gate_order(count):
    masks = [1 << bit for bit in range(count.bit_length() - 1)]
    return masks[2:] + masks[1::-1]


def gather_gates(pieces, *waits):
    held = jnp.concatenate(pieces, axis=1) if len(pieces) > 1 else pieces[0]
    mask = gate_order(lax.axis_size("seq"))[len(pieces) - 1]
    return [*pieces, flip(after(held, *waits) if waits else held, mask)]


def place_of(j):
    return sum(1 << bit for bit, mask in enumerate(gate_order(lax.axis_size("seq"))) if j & mask)


def attention_kernel(where_ref, q_ref, ids_ref, *refs):
    keys, values, (theirs_ref, mine_ref, both) = refs[:3], refs[3:6], refs[-3:]
    rows = q_ref.shape[0]
    some = rows // 2
    core, odd = where_ref[0], where_ref[1]
    scale = 1.0 / math.sqrt(HD)
    ids = [ids_ref[:, i * rows : (i + 1) * rows] for i in range(3)]
    column = jnp.transpose(jnp.broadcast_to(ids[1], (HD, rows)))[:, :1]
    back, front = jnp.where(odd == 1, ids[0], ids[2]), jnp.where(odd == 1, ids[2], ids[0])
    apart = lax.broadcasted_iota(jnp.int32, (rows, rows), 0) - lax.broadcasted_iota(
        jnp.int32, (rows, rows), 1
    )
    side = rows * (2 * odd - 1)
    allowed = jnp.concatenate(
        [
            (column == back) & (jnp.abs(apart + side) < rows),
            column == ids[1],
            (column == front) & (jnp.abs(apart - side) < rows),
        ],
        axis=1,
    )
    for head in range(q_ref.shape[1] // HD):
        cols = slice(head * HD, (head + 1) * HD)
        query = q_ref[:, cols]
        score = jnp.concatenate(
            [
                lax.dot_general(query, ref[:, cols], NT, preferred_element_type=jnp.float32)
                for ref in keys
            ],
            axis=1,
        )
        score = jnp.where(allowed, score * scale, -jnp.inf)
        weights = jnp.exp(score - jnp.max(score, axis=-1, keepdims=True))
        share = 1.0 / jnp.sum(weights, axis=-1, keepdims=True)
        probs = (weights * share).astype(jnp.bfloat16)
        total = jnp.zeros((rows, HD), jnp.float32)
        for i, ref in enumerate(values):
            total += jnp.dot(
                probs[:, i * rows : (i + 1) * rows], ref[:, cols], preferred_element_type=jnp.float32
            )
        both[:, cols] = total.astype(jnp.bfloat16)
    at = pl.multiple_of(core * some, some)
    mine_ref[...] = both[pl.ds(at, some), :]
    theirs_ref[...] = both[pl.ds(some - at, some), :]


def attention(where, queries, ids, near_keys, near_values, *ahead):
    rows, width = queries.shape
    half = jax.ShapeDtypeStruct((rows // 2, width), jnp.bfloat16)
    return pl.pallas_call(
        attention_kernel,
        out_shape=(half, half),
        in_specs=[pl.BlockSpec(memory_space=pltpu.SMEM)] + [VMEM] * 8 + [ANY] * len(ahead),
        out_specs=(VMEM, VMEM),
        scratch_shapes=[pltpu.VMEM((rows, width), jnp.bfloat16)],
        compiler_params=pltpu.CompilerParams(vmem_limit_bytes=63 * 1024 * 1024),
        name="window_attention",
    )(where, queries, ids, *near_keys, *near_values, *ahead)


def norm_kernel(mine_ref, theirs_ref, own_w, other_w, resid_ref, gain_ref, *refs):
    stream_ref, normed_ref = refs[-2:]
    stream = resid_ref[...].astype(jnp.float32)
    stream += jnp.dot(mine_ref[...], own_w[...], preferred_element_type=jnp.float32)
    stream += jnp.dot(theirs_ref[...], other_w[...], preferred_element_type=jnp.float32)
    meansq = jnp.mean(stream * stream, axis=-1, keepdims=True)
    stream_ref[...] = stream
    normed_ref[...] = (stream * lax.rsqrt(meansq + 1e-05) * gain_ref[...]).astype(jnp.bfloat16)


def project_and_norm(mine, theirs, own_w, other_w, resid, gain, *ahead):
    rows, width = resid.shape
    return pl.pallas_call(
        norm_kernel,
        out_shape=(
            jax.ShapeDtypeStruct((rows, width), jnp.float32),
            jax.ShapeDtypeStruct((rows, width), jnp.bfloat16),
        ),
        in_specs=[VMEM] * 6 + [ANY] * len(ahead),
        out_specs=(VMEM, VMEM),
        compiler_params=pltpu.CompilerParams(vmem_limit_bytes=63 * 1024 * 1024),
        name="project_and_norm",
    )(mine, theirs, own_w, other_w, resid, gain, *ahead)


def assemble_kernel(*refs):
    halves, (gate_up, down, sems) = refs[:6], refs[6:]
    units = halves[0].shape[0]
    copies = []
    for i, half in enumerate(halves):
        target, at = (gate_up, i * units) if i < 4 else (down, (i - 4) * units)
        copies.append(pltpu.make_async_copy(half, target.at[pl.ds(at, units), :], sems.at[i]))
    for copy in copies:
        copy.start()
    for copy in copies:
        copy.wait()


def assemble(halves):
    units, width = halves[0].shape
    return pl.pallas_call(
        assemble_kernel,
        out_shape=(
            jax.ShapeDtypeStruct((4 * units, width), jnp.bfloat16),
            jax.ShapeDtypeStruct((2 * units, width), jnp.bfloat16),
        ),
        in_specs=[ANY] * 6,
        out_specs=(VMEM, VMEM),
        scratch_shapes=[pltpu.SemaphoreType.DMA((6,))],
        compiler_params=pltpu.CompilerParams(vmem_limit_bytes=36 * 1024 * 1024),
        name="assemble_weights",
    )(*halves)


def gates_at(place, rows, pieces):
    piece = place.bit_length()
    at = (place - (1 << piece >> 1)) * rows
    return pieces[piece][:, at : at + rows]


def expert_kernel(places, pieces, where_ref, *refs):
    count = len(places)
    blocks, gates, (gate_up, down) = refs[:count], refs[count : count + pieces], refs[count + pieces :][:2]
    outs = refs[count + pieces + 2 :]
    units = down.shape[0]
    rows = blocks[0].shape[0]
    for first in range(0, count, 2):
        group = range(first, min(first + 2, count))
        tokens = jnp.concatenate([blocks[i][...] for i in group], axis=0)
        gate = lax.dot_general(tokens, gate_up[:units, :], NT, preferred_element_type=jnp.float32)
        up = lax.dot_general(tokens, gate_up[units:, :], NT, preferred_element_type=jnp.float32)
        act = (gate / (1.0 + jnp.exp(-gate)) * up).astype(jnp.bfloat16)
        result = jnp.dot(act, down[...], preferred_element_type=jnp.float32)
        for i in group:
            here = gates_at(places[i][0], rows, gates)
            if places[i][0] != places[i][1]:
                here = jnp.where(where_ref[1] == 1, gates_at(places[i][1], rows, gates), here)
            expert = lax.broadcasted_iota(jnp.int32, here.shape, 0)
            chosen = jnp.sum(jnp.where(expert == where_ref[0], here, 0.0), axis=0, keepdims=True)
            chosen = jnp.transpose(jnp.broadcast_to(chosen, (rows, rows)))[:, :1]
            part = result[(i - first) * rows : (i - first + 1) * rows]
            outs[i][...] = (part * chosen).astype(jnp.bfloat16)


def expert(blocks, places, where, gates, weights):
    rows, width = blocks[0].shape
    count = len(blocks)
    return pl.pallas_call(
        functools.partial(expert_kernel, places, len(gates)),
        out_shape=[jax.ShapeDtypeStruct((rows, width), jnp.bfloat16)] * count,
        in_specs=[pl.BlockSpec(memory_space=pltpu.SMEM)] + [VMEM] * (count + len(gates) + 2),
        out_specs=[VMEM] * count,
        compiler_params=pltpu.CompilerParams(vmem_limit_bytes=36 * 1024 * 1024),
        name="expert_rows",
    )(where, *blocks, *gates, *weights)


def add(*terms):
    total = terms[0].astype(jnp.float32)
    for term in terms[1:]:
        total = total + term.astype(jnp.float32)
    return total


def add_small(*terms):
    return add(*terms).astype(jnp.bfloat16)


def shift(block, pairs):
    return lax.ppermute(block, "seq", [(4 * a + i, 4 * b + i) for a, b in pairs for i in range(4)])


OUTWARD, INWARD, MIDDLE = [(1, 0), (2, 3)], [(0, 1), (3, 2)], [(1, 2), (2, 1)]
X, Y = (1, 2), (2, 1)


def step_layer(normed, stream, run, weights):
    z = lax.axis_index("seq") // 4
    inner = (z == 1) | (z == 2)

    o0 = normed
    o1, near3, x0, y0 = flip(o0, 4), shift(o0, MIDDLE), cross(o0, X), cross(o0, Y)
    weights = weights(x0, y0)

    ends2, near2 = shift(near3, OUTWARD), shift(o1, MIDDLE)
    d0, y1 = cross(after(y0, x0), X), cross(after(o1, y0), Y)

    ends3 = shift(after(near2, ends2), OUTWARD)
    o2 = jnp.where(inner, near2, ends2)
    x2, y2 = cross(after(o2, d0, weights[0]), X), cross(after(o2, y1, weights[0]), Y)
    run = functools.partial(run, weights)
    p0, px0, py0, pd0 = run([after(o0, o2), x0, y0, d0], (0, X, Y, 3))

    x1 = flip(after(x0, ends3, p0), 4)
    o3 = jnp.where(inner, near3, ends3)
    x3, y3 = cross(after(o3, x2, p0), X), cross(after(o3, y2, p0), Y)
    p1, py1, p2, px2, py2, p3 = run(
        [after(o1, p0), y1, o2, x2, y2, o3], (4, plane(Y, 4), 8, plane(X, 8), plane(Y, 8), 12)
    )

    d1 = flip(after(d0, x1, p1), 4)
    d2, d3 = cross(after(y2, x3, p1), X), cross(after(x3, y3, p1), Y)
    px3, py3, px1 = run([after(x3, p1), y3, x1], (plane(X, 12), plane(Y, 12), plane(X, 4)))

    to_x0 = flip(after(px1, d1), 4)
    pd2, pd3 = run([after(d2, px3), d3], (11, 15))
    (pd1,) = run([after(d1, pd2)], (7,))
    to_x3, to_y2, to_d0 = cross(pd3, Y), cross(pd2, X), flip(after(pd1, to_x0), 4)

    px3, py2, px0 = add_small(px3, to_x3), add_small(py2, to_y2), add_small(px0, to_x0)
    by_x, by_y = cross(after(px3, to_y2), X), cross(after(py3, to_x3), Y)

    p3, pd0 = add_small(p3, by_x, by_y), add_small(pd0, to_d0)
    to_2 = shift(after(p3, to_d0), INWARD)
    by_x, by_y = cross(after(px2, by_x), X), cross(after(py2, by_y), Y)

    p2 = add_small(p2, by_x, by_y, to_2)
    to_3, to_1 = shift(after(p2, to_2), INWARD), shift(p2, MIDDLE)
    to_y0, by_y = cross(after(pd0, by_x), X), cross(after(py1, by_y), Y)

    p1, py0 = add_small(p1, by_y, to_1), add_small(py0, to_y0)
    p3 = add_small(after(p3, p1), to_3)
    by_z, by_middle = flip(after(p1, to_3), 4), shift(p3, MIDDLE)
    by_x, by_y = cross(after(px0, to_y0), X), cross(after(py0, by_y), Y)
    return add(stream, p0, by_z, by_middle, by_x, by_y)


def plane(masks, distance):
    return tuple(mask + distance for mask in masks)


def expert_layer(normed, stream, where, gates, halves):
    count = lax.axis_size("seq")

    def weights(*waits):
        return assemble([after(half, *waits) for half in halves])

    def run(weights, blocks, masks):
        masks = [mask if isinstance(mask, tuple) else (mask, mask) for mask in masks]
        places = tuple(tuple(place_of(j) for j in mask) for mask in masks)
        return expert(blocks, places, where, gates, weights)

    if count == 16:
        return step_layer(normed, stream, run, weights)
    held = weights()
    blocks, mask = [normed], 1
    while mask < count:
        blocks = blocks + [flip(block, mask) for block in blocks]
        mask *= 2
    parts = []
    for first in range(0, count, 4):
        parts += run(held, blocks[first : first + 4], range(first, first + 4))
    while mask > 1:
        mask //= 2
        parts = [add_small(parts[i], flip(parts[i + mask], mask)) for i in range(mask)]
    return add(stream, parts[0])


def shards(
    queries,
    keys,
    values,
    resid,
    pair_ids,
    out_weight,
    norm_gain,
    experts,
    gates,
    w_gate,
    w_up,
    w_down,
):
    tok_rows = queries.shape[0]
    moe_rows = resid.shape[0]
    shard = lax.axis_index("seq")
    core = lax.axis_index("exp")
    count = lax.axis_size("seq")

    def halo(part):
        beside = flip(part, 1)
        ahead = [(i, i + 2) for i in range(0, count - 2, 2)]
        back = [(i + 2, i) for i in range(1, count - 2, 2)]
        return beside, part, lax.ppermute(beside, "seq", ahead + back)

    near_keys, near_values = halo(keys), halo(values)
    chosen = experts.T[:, None, :] == jnp.arange(count, dtype=jnp.int32)[None, :, None]
    some_gates = [jnp.sum(jnp.where(chosen, gates.T[:, None, :], 0.0), axis=0)]
    while len(some_gates) < count.bit_length() - 1:
        some_gates = gather_gates(some_gates)
    id_pad = jnp.pad(pair_ids, (tok_rows, tok_rows), constant_values=-1)
    ids = lax.dynamic_slice_in_dim(id_pad, shard * tok_rows, 3 * tok_rows, 0)[None, :]
    out_other = lax.ppermute(out_weight, "exp", SWAP)
    gate_w, up_w = jnp.swapaxes(w_gate[0], 0, 1), jnp.swapaxes(w_up[0], 0, 1)
    gate_other = lax.ppermute(gate_w, "exp", SWAP)
    where = jnp.stack([core, shard % 2])
    ready = (where, *near_keys, *near_values, some_gates[-1], ids)
    up_other = lax.ppermute(after(up_w, *ready), "exp", SWAP)
    down_other = lax.ppermute(after(w_down[0], *ready), "exp", SWAP)
    halves = [gate_w, gate_other, up_w, up_other, w_down[0], down_other]

    theirs, mine = attention(where, queries, ids, near_keys, near_values, out_other, gate_other)
    all_gates = gather_gates(some_gates, theirs)
    received = lax.ppermute(theirs, "exp", SWAP)
    stream, normed = project_and_norm(
        mine, received, out_weight, out_other, resid, norm_gain[None, :], up_other, down_other
    )
    mixed = expert_layer(normed, stream, jnp.stack([shard, core]), all_gates, halves)
    return mixed.astype(jnp.bfloat16)


def solution(mesh):
    in_specs = (
        P("seq", "exp"),
        P("seq", "exp"),
        P("seq", "exp"),
        P(("seq", "exp"), None),
        P(),
        P("exp", None),
        P(),
        P(("seq", "exp"), None),
        P(("seq", "exp"), None),
        P("seq", None, "exp"),
        P("seq", None, "exp"),
        P("seq", "exp", None),
    )
    out_specs = P(("seq", "exp"), None)
    return jax.shard_map(shards, mesh=mesh, in_specs=in_specs, out_specs=out_specs, check_vma=False)
```

```python
import functools
import math

import jax
import jax.numpy as jnp
from jax import lax
from jax.experimental import pallas as pl
from jax.experimental.pallas import tpu as pltpu
from jax.sharding import PartitionSpec as P

HD = 128
SWAP = [(0, 1), (1, 0)]
VMEM = pl.BlockSpec(memory_space=pltpu.VMEM)
ANY = pl.BlockSpec(memory_space=pl.ANY)
NT = (((1,), (1,)), ((), ()))


def flip(block, mask):
    count = lax.axis_size("seq")
    return lax.ppermute(block, "seq", [(i, i ^ mask) for i in range(count)])


def cross(block, masks):
    count = lax.axis_size("seq")
    pairs = [(2 * i + c, 2 * (i ^ masks[c]) + c) for i in range(count) for c in range(2)]
    return lax.ppermute(block, ("seq", "exp"), pairs)


def after(block, *arrays):
    return lax.optimization_barrier((block, *arrays))[0]


def gate_order(count):
    masks = [1 << bit for bit in range(count.bit_length() - 1)]
    return masks[2:] + masks[1::-1]


def gather_gates(pieces, *waits):
    held = jnp.concatenate(pieces, axis=1) if len(pieces) > 1 else pieces[0]
    mask = gate_order(lax.axis_size("seq"))[len(pieces) - 1]
    return [*pieces, flip(after(held, *waits) if waits else held, mask)]


def place_of(j):
    return sum(1 << bit for bit, mask in enumerate(gate_order(lax.axis_size("seq"))) if j & mask)


def attention_kernel(where_ref, q_ref, ids_ref, *refs):
    keys, values, (theirs_ref, mine_ref, both) = refs[:3], refs[3:6], refs[-3:]
    rows = q_ref.shape[0]
    some = rows // 2
    core, odd = where_ref[0], where_ref[1]
    scale = 1.0 / math.sqrt(HD)
    ids = [ids_ref[:, i * rows : (i + 1) * rows] for i in range(3)]
    column = jnp.transpose(jnp.broadcast_to(ids[1], (HD, rows)))[:, :1]
    back, front = jnp.where(odd == 1, ids[0], ids[2]), jnp.where(odd == 1, ids[2], ids[0])
    apart = lax.broadcasted_iota(jnp.int32, (rows, rows), 0) - lax.broadcasted_iota(
        jnp.int32, (rows, rows), 1
    )
    side = rows * (2 * odd - 1)
    allowed = jnp.concatenate(
        [
            (column == back) & (jnp.abs(apart + side) < rows),
            column == ids[1],
            (column == front) & (jnp.abs(apart - side) < rows),
        ],
        axis=1,
    )
    for head in range(q_ref.shape[1] // HD):
        cols = slice(head * HD, (head + 1) * HD)
        query = q_ref[:, cols]
        score = jnp.concatenate(
            [
                lax.dot_general(query, ref[:, cols], NT, preferred_element_type=jnp.float32)
                for ref in keys
            ],
            axis=1,
        )
        score = jnp.where(allowed, score * scale, -jnp.inf)
        weights = jnp.exp(score - jnp.max(score, axis=-1, keepdims=True))
        share = 1.0 / jnp.sum(weights, axis=-1, keepdims=True)
        probs = (weights * share).astype(jnp.bfloat16)
        total = jnp.zeros((rows, HD), jnp.float32)
        for i, ref in enumerate(values):
            total += jnp.dot(
                probs[:, i * rows : (i + 1) * rows], ref[:, cols], preferred_element_type=jnp.float32
            )
        both[:, cols] = total.astype(jnp.bfloat16)
    at = pl.multiple_of(core * some, some)
    mine_ref[...] = both[pl.ds(at, some), :]
    theirs_ref[...] = both[pl.ds(some - at, some), :]


def attention(where, queries, ids, near_keys, near_values, *ahead):
    rows, width = queries.shape
    half = jax.ShapeDtypeStruct((rows // 2, width), jnp.bfloat16)
    return pl.pallas_call(
        attention_kernel,
        out_shape=(half, half),
        in_specs=[pl.BlockSpec(memory_space=pltpu.SMEM)] + [VMEM] * 8 + [ANY] * len(ahead),
        out_specs=(VMEM, VMEM),
        scratch_shapes=[pltpu.VMEM((rows, width), jnp.bfloat16)],
        compiler_params=pltpu.CompilerParams(vmem_limit_bytes=63 * 1024 * 1024),
        name="window_attention",
    )(where, queries, ids, *near_keys, *near_values, *ahead)


def norm_kernel(mine_ref, theirs_ref, own_w, other_w, resid_ref, gain_ref, *refs):
    stream_ref, normed_ref = refs[-2:]
    stream = resid_ref[...].astype(jnp.float32)
    stream += jnp.dot(mine_ref[...], own_w[...], preferred_element_type=jnp.float32)
    stream += jnp.dot(theirs_ref[...], other_w[...], preferred_element_type=jnp.float32)
    meansq = jnp.mean(stream * stream, axis=-1, keepdims=True)
    stream_ref[...] = stream
    normed_ref[...] = (stream * lax.rsqrt(meansq + 1e-05) * gain_ref[...]).astype(jnp.bfloat16)


def project_and_norm(mine, theirs, own_w, other_w, resid, gain, *ahead):
    rows, width = resid.shape
    return pl.pallas_call(
        norm_kernel,
        out_shape=(
            jax.ShapeDtypeStruct((rows, width), jnp.float32),
            jax.ShapeDtypeStruct((rows, width), jnp.bfloat16),
        ),
        in_specs=[VMEM] * 6 + [ANY] * len(ahead),
        out_specs=(VMEM, VMEM),
        compiler_params=pltpu.CompilerParams(vmem_limit_bytes=63 * 1024 * 1024),
        name="project_and_norm",
    )(mine, theirs, own_w, other_w, resid, gain, *ahead)


def assemble_kernel(*refs):
    halves, (gate_up, down, sems) = refs[:6], refs[6:]
    units = halves[0].shape[0]
    copies = []
    for i, half in enumerate(halves):
        target, at = (gate_up, i * units) if i < 4 else (down, (i - 4) * units)
        copies.append(pltpu.make_async_copy(half, target.at[pl.ds(at, units), :], sems.at[i]))
    for copy in copies:
        copy.start()
    for copy in copies:
        copy.wait()


def assemble(halves):
    units, width = halves[0].shape
    return pl.pallas_call(
        assemble_kernel,
        out_shape=(
            jax.ShapeDtypeStruct((4 * units, width), jnp.bfloat16),
            jax.ShapeDtypeStruct((2 * units, width), jnp.bfloat16),
        ),
        in_specs=[ANY] * 6,
        out_specs=(VMEM, VMEM),
        scratch_shapes=[pltpu.SemaphoreType.DMA((6,))],
        compiler_params=pltpu.CompilerParams(vmem_limit_bytes=36 * 1024 * 1024),
        name="assemble_weights",
    )(*halves)


def gates_at(place, rows, pieces):
    piece = place.bit_length()
    at = (place - (1 << piece >> 1)) * rows
    return pieces[piece][:, at : at + rows]


def expert_kernel(places, pieces, where_ref, *refs):
    count = len(places)
    blocks, gates, (gate_up, down) = refs[:count], refs[count : count + pieces], refs[count + pieces :][:2]
    outs = refs[count + pieces + 2 :]
    units = down.shape[0]
    rows = blocks[0].shape[0]
    for first in range(0, count, 2):
        group = range(first, min(first + 2, count))
        tokens = jnp.concatenate([blocks[i][...] for i in group], axis=0)
        gate = lax.dot_general(tokens, gate_up[:units, :], NT, preferred_element_type=jnp.float32)
        up = lax.dot_general(tokens, gate_up[units:, :], NT, preferred_element_type=jnp.float32)
        act = (gate / (1.0 + jnp.exp(-gate)) * up).astype(jnp.bfloat16)
        result = jnp.dot(act, down[...], preferred_element_type=jnp.float32)
        for i in group:
            here = gates_at(places[i][0], rows, gates)
            if places[i][0] != places[i][1]:
                here = jnp.where(where_ref[1] == 1, gates_at(places[i][1], rows, gates), here)
            expert = lax.broadcasted_iota(jnp.int32, here.shape, 0)
            chosen = jnp.sum(jnp.where(expert == where_ref[0], here, 0.0), axis=0, keepdims=True)
            chosen = jnp.transpose(jnp.broadcast_to(chosen, (rows, rows)))[:, :1]
            part = result[(i - first) * rows : (i - first + 1) * rows]
            outs[i][...] = (part * chosen).astype(jnp.bfloat16)


def expert(blocks, places, where, gates, weights):
    rows, width = blocks[0].shape
    count = len(blocks)
    return pl.pallas_call(
        functools.partial(expert_kernel, places, len(gates)),
        out_shape=[jax.ShapeDtypeStruct((rows, width), jnp.bfloat16)] * count,
        in_specs=[pl.BlockSpec(memory_space=pltpu.SMEM)] + [VMEM] * (count + len(gates) + 2),
        out_specs=[VMEM] * count,
        compiler_params=pltpu.CompilerParams(vmem_limit_bytes=36 * 1024 * 1024),
        name="expert_rows",
    )(where, *blocks, *gates, *weights)


def add(*terms):
    total = terms[0].astype(jnp.float32)
    for term in terms[1:]:
        total = total + term.astype(jnp.float32)
    return total


def add_small(*terms):
    return add(*terms).astype(jnp.bfloat16)


def shift(block, pairs):
    return lax.ppermute(block, "seq", [(4 * a + i, 4 * b + i) for a, b in pairs for i in range(4)])


OUTWARD, INWARD, MIDDLE = [(1, 0), (2, 3)], [(0, 1), (3, 2)], [(1, 2), (2, 1)]
X, Y = (1, 2), (2, 1)


def step_layer(normed, stream, run, weights):
    z = lax.axis_index("seq") // 4
    inner = (z == 1) | (z == 2)

    o0 = normed
    o1, near3, x0, y0 = flip(o0, 4), shift(o0, MIDDLE), cross(o0, X), cross(o0, Y)
    weights = weights(x0, y0)

    ends2, near2 = shift(near3, OUTWARD), shift(o1, MIDDLE)
    d0, y1 = cross(after(y0, x0), X), cross(after(o1, y0), Y)

    ends3 = shift(near2, OUTWARD)
    o2 = jnp.where(inner, near2, ends2)
    x2, y2 = cross(after(o2, d0, weights[0]), X), cross(after(o2, y1, weights[0]), Y)
    run = functools.partial(run, weights)
    p0, px0, py0, pd0 = run([after(o0, o2), x0, y0, d0], (0, X, Y, 3))

    x1 = flip(after(x0, ends3, p0), 4)
    o3 = jnp.where(inner, near3, ends3)
    x3, y3 = cross(after(o3, x2, p0), X), cross(after(o3, y2, p0), Y)
    p1, py1, p2, px2, py2, p3 = run(
        [after(o1, p0), y1, o2, x2, y2, o3], (4, plane(Y, 4), 8, plane(X, 8), plane(Y, 8), 12)
    )

    d1 = flip(after(d0, x1, p1), 4)
    d2, d3 = cross(after(y2, x3, p1), X), cross(after(x3, y3, p1), Y)
    px3, py3, px1 = run([after(x3, p1), y3, x1], (plane(X, 12), plane(Y, 12), plane(X, 4)))

    to_x0 = flip(after(px1, d1), 4)
    pd2, pd3 = run([after(d2, px3), d3], (11, 15))
    (pd1,) = run([after(d1, pd2)], (7,))
    to_x3, to_y2, to_d0 = cross(pd3, Y), cross(pd2, X), flip(after(pd1, to_x0), 4)

    px3, py2, px0 = add_small(px3, to_x3), add_small(py2, to_y2), add_small(px0, to_x0)
    by_x, by_y = cross(after(px3, to_y2), X), cross(after(py3, to_x3), Y)

    p3, pd0 = add_small(p3, by_x, by_y), add_small(pd0, to_d0)
    to_2 = shift(after(p3, to_d0), INWARD)
    by_x, by_y = cross(after(px2, by_x), X), cross(after(py2, by_y), Y)

    p2 = add_small(p2, by_x, by_y, to_2)
    to_3, to_1 = shift(after(p2, to_2), INWARD), shift(p2, MIDDLE)
    to_y0, by_y = cross(after(pd0, by_x), X), cross(after(py1, by_y), Y)

    p1, py0 = add_small(p1, by_y, to_1), add_small(py0, to_y0)
    p3 = add_small(after(p3, p1), to_3)
    by_z, by_middle = flip(after(p1, to_3), 4), shift(p3, MIDDLE)
    by_x, by_y = cross(after(px0, to_y0), X), cross(after(py0, by_y), Y)
    return add(stream, p0, by_z, by_middle, by_x, by_y)


def plane(masks, distance):
    return tuple(mask + distance for mask in masks)


def expert_layer(normed, stream, where, gates, halves):
    count = lax.axis_size("seq")

    def weights(*waits):
        return assemble([after(half, *waits) for half in halves])

    def run(weights, blocks, masks):
        masks = [mask if isinstance(mask, tuple) else (mask, mask) for mask in masks]
        places = tuple(tuple(place_of(j) for j in mask) for mask in masks)
        return expert(blocks, places, where, gates, weights)

    if count == 16:
        return step_layer(normed, stream, run, weights)
    held = weights()
    blocks, mask = [normed], 1
    while mask < count:
        blocks = blocks + [flip(block, mask) for block in blocks]
        mask *= 2
    parts = []
    for first in range(0, count, 4):
        parts += run(held, blocks[first : first + 4], range(first, first + 4))
    while mask > 1:
        mask //= 2
        parts = [add_small(parts[i], flip(parts[i + mask], mask)) for i in range(mask)]
    return add(stream, parts[0])


def shards(
    queries,
    keys,
    values,
    resid,
    pair_ids,
    out_weight,
    norm_gain,
    experts,
    gates,
    w_gate,
    w_up,
    w_down,
):
    tok_rows = queries.shape[0]
    moe_rows = resid.shape[0]
    shard = lax.axis_index("seq")
    core = lax.axis_index("exp")
    count = lax.axis_size("seq")

    def halo(part):
        beside = flip(part, 1)
        ahead = [(i, i + 2) for i in range(0, count - 2, 2)]
        back = [(i + 2, i) for i in range(1, count - 2, 2)]
        return beside, part, lax.ppermute(beside, "seq", ahead + back)

    near_keys, near_values = halo(keys), halo(values)
    chosen = experts.T[:, None, :] == jnp.arange(count, dtype=jnp.int32)[None, :, None]
    some_gates = [jnp.sum(jnp.where(chosen, gates.T[:, None, :], 0.0), axis=0)]
    while len(some_gates) < count.bit_length() - 1:
        some_gates = gather_gates(some_gates)
    id_pad = jnp.pad(pair_ids, (tok_rows, tok_rows), constant_values=-1)
    ids = lax.dynamic_slice_in_dim(id_pad, shard * tok_rows, 3 * tok_rows, 0)[None, :]
    out_other = lax.ppermute(out_weight, "exp", SWAP)
    gate_w, up_w = jnp.swapaxes(w_gate[0], 0, 1), jnp.swapaxes(w_up[0], 0, 1)
    gate_other = lax.ppermute(gate_w, "exp", SWAP)
    where = jnp.stack([core, shard % 2])
    ready = (where, *near_keys, *near_values, some_gates[-1], ids)
    up_other = lax.ppermute(after(up_w, *ready), "exp", SWAP)
    down_other = lax.ppermute(after(w_down[0], *ready), "exp", SWAP)
    halves = [gate_w, gate_other, up_w, up_other, w_down[0], down_other]

    theirs, mine = attention(where, queries, ids, near_keys, near_values, out_other, gate_other)
    all_gates = gather_gates(some_gates, theirs)
    received = lax.ppermute(theirs, "exp", SWAP)
    stream, normed = project_and_norm(
        mine, received, out_weight, out_other, resid, norm_gain[None, :], up_other, down_other
    )
    mixed = expert_layer(normed, stream, jnp.stack([shard, core]), all_gates, halves)
    return mixed.astype(jnp.bfloat16)


def solution(mesh):
    in_specs = (
        P("seq", "exp"),
        P("seq", "exp"),
        P("seq", "exp"),
        P(("seq", "exp"), None),
        P(),
        P("exp", None),
        P(),
        P(("seq", "exp"), None),
        P(("seq", "exp"), None),
        P("seq", None, "exp"),
        P("seq", None, "exp"),
        P("seq", "exp", None),
    )
    out_specs = P(("seq", "exp"), None)
    return jax.shard_map(shards, mesh=mesh, in_specs=in_specs, out_specs=out_specs, check_vma=False)
```

```python
import functools
import math

import jax
import jax.numpy as jnp
from jax import lax
from jax.experimental import pallas as pl
from jax.experimental.pallas import tpu as pltpu
from jax.sharding import PartitionSpec as P

HD = 128
SWAP = [(0, 1), (1, 0)]
VMEM = pl.BlockSpec(memory_space=pltpu.VMEM)
ANY = pl.BlockSpec(memory_space=pl.ANY)
NT = (((1,), (1,)), ((), ()))


def flip(block, mask):
    count = lax.axis_size("seq")
    return lax.ppermute(block, "seq", [(i, i ^ mask) for i in range(count)])


def cross(block, masks):
    count = lax.axis_size("seq")
    pairs = [(2 * i + c, 2 * (i ^ masks[c]) + c) for i in range(count) for c in range(2)]
    return lax.ppermute(block, ("seq", "exp"), pairs)


def after(block, *arrays):
    return lax.optimization_barrier((block, *arrays))[0]


def gate_order(count):
    masks = [1 << bit for bit in range(count.bit_length() - 1)]
    return masks[2:] + masks[1::-1]


def gather_gates(pieces, *waits):
    held = jnp.concatenate(pieces, axis=1) if len(pieces) > 1 else pieces[0]
    mask = gate_order(lax.axis_size("seq"))[len(pieces) - 1]
    return [*pieces, flip(after(held, *waits) if waits else held, mask)]


def place_of(j):
    return sum(1 << bit for bit, mask in enumerate(gate_order(lax.axis_size("seq"))) if j & mask)


def attention_kernel(where_ref, q_ref, ids_ref, *refs):
    keys, values, (theirs_ref, mine_ref, both) = refs[:3], refs[3:6], refs[-3:]
    rows = q_ref.shape[0]
    some = rows // 2
    core, odd = where_ref[0], where_ref[1]
    scale = 1.0 / math.sqrt(HD)
    ids = [ids_ref[:, i * rows : (i + 1) * rows] for i in range(3)]
    column = jnp.transpose(jnp.broadcast_to(ids[1], (HD, rows)))[:, :1]
    back, front = jnp.where(odd == 1, ids[0], ids[2]), jnp.where(odd == 1, ids[2], ids[0])
    apart = lax.broadcasted_iota(jnp.int32, (rows, rows), 0) - lax.broadcasted_iota(
        jnp.int32, (rows, rows), 1
    )
    side = rows * (2 * odd - 1)
    allowed = jnp.concatenate(
        [
            (column == back) & (jnp.abs(apart + side) < rows),
            column == ids[1],
            (column == front) & (jnp.abs(apart - side) < rows),
        ],
        axis=1,
    )
    for head in range(q_ref.shape[1] // HD):
        cols = slice(head * HD, (head + 1) * HD)
        query = q_ref[:, cols]
        score = jnp.concatenate(
            [
                lax.dot_general(query, ref[:, cols], NT, preferred_element_type=jnp.float32)
                for ref in keys
            ],
            axis=1,
        )
        score = jnp.where(allowed, score * scale, -jnp.inf)
        weights = jnp.exp(score - jnp.max(score, axis=-1, keepdims=True))
        share = 1.0 / jnp.sum(weights, axis=-1, keepdims=True)
        probs = (weights * share).astype(jnp.bfloat16)
        total = jnp.zeros((rows, HD), jnp.float32)
        for i, ref in enumerate(values):
            total += jnp.dot(
                probs[:, i * rows : (i + 1) * rows], ref[:, cols], preferred_element_type=jnp.float32
            )
        both[:, cols] = total.astype(jnp.bfloat16)
    at = pl.multiple_of(core * some, some)
    mine_ref[...] = both[pl.ds(at, some), :]
    theirs_ref[...] = both[pl.ds(some - at, some), :]


def attention(where, queries, ids, near_keys, near_values, *ahead):
    rows, width = queries.shape
    half = jax.ShapeDtypeStruct((rows // 2, width), jnp.bfloat16)
    return pl.pallas_call(
        attention_kernel,
        out_shape=(half, half),
        in_specs=[pl.BlockSpec(memory_space=pltpu.SMEM)] + [VMEM] * 8 + [ANY] * len(ahead),
        out_specs=(VMEM, VMEM),
        scratch_shapes=[pltpu.VMEM((rows, width), jnp.bfloat16)],
        compiler_params=pltpu.CompilerParams(vmem_limit_bytes=63 * 1024 * 1024),
        name="window_attention",
    )(where, queries, ids, *near_keys, *near_values, *ahead)


def norm_kernel(mine_ref, theirs_ref, own_w, other_w, resid_ref, gain_ref, *refs):
    stream_ref, normed_ref = refs[-2:]
    stream = resid_ref[...].astype(jnp.float32)
    stream += jnp.dot(mine_ref[...], own_w[...], preferred_element_type=jnp.float32)
    stream += jnp.dot(theirs_ref[...], other_w[...], preferred_element_type=jnp.float32)
    meansq = jnp.mean(stream * stream, axis=-1, keepdims=True)
    stream_ref[...] = stream
    normed_ref[...] = (stream * lax.rsqrt(meansq + 1e-05) * gain_ref[...]).astype(jnp.bfloat16)


def project_and_norm(mine, theirs, own_w, other_w, resid, gain, *ahead):
    rows, width = resid.shape
    return pl.pallas_call(
        norm_kernel,
        out_shape=(
            jax.ShapeDtypeStruct((rows, width), jnp.float32),
            jax.ShapeDtypeStruct((rows, width), jnp.bfloat16),
        ),
        in_specs=[VMEM] * 6 + [ANY] * len(ahead),
        out_specs=(VMEM, VMEM),
        compiler_params=pltpu.CompilerParams(vmem_limit_bytes=63 * 1024 * 1024),
        name="project_and_norm",
    )(mine, theirs, own_w, other_w, resid, gain, *ahead)


def assemble_kernel(*refs):
    halves, (gate_up, down, sems) = refs[:6], refs[6:]
    units = halves[0].shape[0]
    copies = []
    for i, half in enumerate(halves):
        target, at = (gate_up, i * units) if i < 4 else (down, (i - 4) * units)
        copies.append(pltpu.make_async_copy(half, target.at[pl.ds(at, units), :], sems.at[i]))
    for copy in copies:
        copy.start()
    for copy in copies:
        copy.wait()


def assemble(halves):
    units, width = halves[0].shape
    return pl.pallas_call(
        assemble_kernel,
        out_shape=(
            jax.ShapeDtypeStruct((4 * units, width), jnp.bfloat16),
            jax.ShapeDtypeStruct((2 * units, width), jnp.bfloat16),
        ),
        in_specs=[ANY] * 6,
        out_specs=(VMEM, VMEM),
        scratch_shapes=[pltpu.SemaphoreType.DMA((6,))],
        compiler_params=pltpu.CompilerParams(vmem_limit_bytes=36 * 1024 * 1024),
        name="assemble_weights",
    )(*halves)


def gates_at(place, rows, pieces):
    piece = place.bit_length()
    at = (place - (1 << piece >> 1)) * rows
    return pieces[piece][:, at : at + rows]


def expert_kernel(places, pieces, where_ref, *refs):
    count = len(places)
    blocks, gates, (gate_up, down) = refs[:count], refs[count : count + pieces], refs[count + pieces :][:2]
    outs = refs[count + pieces + 2 :]
    units = down.shape[0]
    rows = blocks[0].shape[0]
    for first in range(0, count, 2):
        group = range(first, min(first + 2, count))
        tokens = jnp.concatenate([blocks[i][...] for i in group], axis=0)
        gate = lax.dot_general(tokens, gate_up[:units, :], NT, preferred_element_type=jnp.float32)
        up = lax.dot_general(tokens, gate_up[units:, :], NT, preferred_element_type=jnp.float32)
        act = (gate / (1.0 + jnp.exp(-gate)) * up).astype(jnp.bfloat16)
        result = jnp.dot(act, down[...], preferred_element_type=jnp.float32)
        for i in group:
            here = gates_at(places[i][0], rows, gates)
            if places[i][0] != places[i][1]:
                here = jnp.where(where_ref[1] == 1, gates_at(places[i][1], rows, gates), here)
            expert = lax.broadcasted_iota(jnp.int32, here.shape, 0)
            chosen = jnp.sum(jnp.where(expert == where_ref[0], here, 0.0), axis=0, keepdims=True)
            chosen = jnp.transpose(jnp.broadcast_to(chosen, (rows, rows)))[:, :1]
            part = result[(i - first) * rows : (i - first + 1) * rows]
            outs[i][...] = (part * chosen).astype(jnp.bfloat16)


def expert(blocks, places, where, gates, weights):
    rows, width = blocks[0].shape
    count = len(blocks)
    return pl.pallas_call(
        functools.partial(expert_kernel, places, len(gates)),
        out_shape=[jax.ShapeDtypeStruct((rows, width), jnp.bfloat16)] * count,
        in_specs=[pl.BlockSpec(memory_space=pltpu.SMEM)] + [VMEM] * (count + len(gates) + 2),
        out_specs=[VMEM] * count,
        compiler_params=pltpu.CompilerParams(vmem_limit_bytes=36 * 1024 * 1024),
        name="expert_rows",
    )(where, *blocks, *gates, *weights)


def add(*terms):
    total = terms[0].astype(jnp.float32)
    for term in terms[1:]:
        total = total + term.astype(jnp.float32)
    return total


def add_small(*terms):
    return add(*terms).astype(jnp.bfloat16)


def shift(block, pairs):
    return lax.ppermute(block, "seq", [(4 * a + i, 4 * b + i) for a, b in pairs for i in range(4)])


OUTWARD, INWARD, MIDDLE = [(1, 0), (2, 3)], [(0, 1), (3, 2)], [(1, 2), (2, 1)]
X, Y = (1, 2), (2, 1)


def step_layer(normed, stream, run, weights):
    z = lax.axis_index("seq") // 4
    inner = (z == 1) | (z == 2)

    o0 = normed
    o1, near3, x0, y0 = flip(o0, 4), shift(o0, MIDDLE), cross(o0, X), cross(o0, Y)
    weights = weights(x0, y0)

    ends2, near2 = shift(near3, OUTWARD), shift(o1, MIDDLE)
    d0, y1 = cross(after(y0, x0), X), cross(after(o1, y0), Y)

    ends3 = shift(near2, OUTWARD)
    o2 = jnp.where(inner, near2, ends2)
    x2, y2 = cross(after(o2, d0, weights[0]), X), cross(after(o2, y1, weights[0]), Y)
    run = functools.partial(run, weights)
    p0, px0, py0, pd0 = run([after(o0, o2), x0, y0, d0], (0, X, Y, 3))

    x1 = flip(after(x0, ends3, p0), 4)
    o3 = jnp.where(inner, near3, ends3)
    x3, y3 = cross(after(o3, x2, p0), X), cross(after(o3, y2, p0), Y)
    p1, py1, p2, px2, py2, p3 = run(
        [after(o1, p0), y1, o2, x2, y2, o3], (4, plane(Y, 4), 8, plane(X, 8), plane(Y, 8), 12)
    )

    d1 = flip(after(d0, x1, p1), 4)
    d2, d3 = cross(after(y2, x3, p1), X), cross(after(x3, y3, p1), Y)
    px3, py3, px1 = run([after(x3, p1), y3, x1], (plane(X, 12), plane(Y, 12), plane(X, 4)))

    to_x0 = flip(after(px1, d1), 4)
    pd2, pd3 = run([after(d2, px3), d3], (11, 15))
    (pd1,) = run([after(d1, pd2)], (7,))
    to_x3, to_y2, to_d0 = cross(pd3, Y), cross(pd2, X), flip(after(pd1, to_x0), 4)

    px3, py2, px0 = add_small(px3, to_x3), add_small(py2, to_y2), add_small(px0, to_x0)
    by_x, by_y = cross(after(px3, to_y2), X), cross(after(py3, to_x3), Y)

    p3, pd0 = add_small(p3, by_x, by_y), add_small(pd0, to_d0)
    to_2 = shift(after(p3, to_d0), INWARD)
    by_x, by_y = cross(after(px2, by_x), X), cross(after(py2, by_y), Y)

    p2 = add_small(p2, by_x, by_y, to_2)
    to_3, to_1 = shift(after(p2, to_2), INWARD), shift(p2, MIDDLE)
    to_y0, by_y = cross(after(pd0, by_x), X), cross(after(py1, by_y), Y)

    p1, py0 = add_small(p1, by_y, to_1), add_small(py0, to_y0)
    p3 = add_small(after(p3, p1), to_3)
    by_z, by_middle = flip(p1, 4), shift(p3, MIDDLE)
    by_x, by_y = cross(after(px0, to_y0), X), cross(after(py0, by_y), Y)
    most = after(add(stream, p0, by_x, by_y, by_z))
    return add(most, by_middle)


def plane(masks, distance):
    return tuple(mask + distance for mask in masks)


def expert_layer(normed, stream, where, gates, halves):
    count = lax.axis_size("seq")

    def weights(*waits):
        return assemble([after(half, *waits) for half in halves])

    def run(weights, blocks, masks):
        masks = [mask if isinstance(mask, tuple) else (mask, mask) for mask in masks]
        places = tuple(tuple(place_of(j) for j in mask) for mask in masks)
        return expert(blocks, places, where, gates, weights)

    if count == 16:
        return step_layer(normed, stream, run, weights)
    held = weights()
    blocks, mask = [normed], 1
    while mask < count:
        blocks = blocks + [flip(block, mask) for block in blocks]
        mask *= 2
    parts = []
    for first in range(0, count, 4):
        parts += run(held, blocks[first : first + 4], range(first, first + 4))
    while mask > 1:
        mask //= 2
        parts = [add_small(parts[i], flip(parts[i + mask], mask)) for i in range(mask)]
    return add(stream, parts[0])


def shards(
    queries,
    keys,
    values,
    resid,
    pair_ids,
    out_weight,
    norm_gain,
    experts,
    gates,
    w_gate,
    w_up,
    w_down,
):
    tok_rows = queries.shape[0]
    moe_rows = resid.shape[0]
    shard = lax.axis_index("seq")
    core = lax.axis_index("exp")
    count = lax.axis_size("seq")

    def halo(part):
        beside = flip(part, 1)
        ahead = [(i, i + 2) for i in range(0, count - 2, 2)]
        back = [(i + 2, i) for i in range(1, count - 2, 2)]
        return beside, part, lax.ppermute(beside, "seq", ahead + back)

    near_keys, near_values = halo(keys), halo(values)
    chosen = experts.T[:, None, :] == jnp.arange(count, dtype=jnp.int32)[None, :, None]
    some_gates = [jnp.sum(jnp.where(chosen, gates.T[:, None, :], 0.0), axis=0)]
    while len(some_gates) < count.bit_length() - 1:
        some_gates = gather_gates(some_gates)
    id_pad = jnp.pad(pair_ids, (tok_rows, tok_rows), constant_values=-1)
    ids = lax.dynamic_slice_in_dim(id_pad, shard * tok_rows, 3 * tok_rows, 0)[None, :]
    out_other = lax.ppermute(out_weight, "exp", SWAP)
    gate_w, up_w = jnp.swapaxes(w_gate[0], 0, 1), jnp.swapaxes(w_up[0], 0, 1)
    gate_other = lax.ppermute(gate_w, "exp", SWAP)
    where = jnp.stack([core, shard % 2])
    ready = (where, *near_keys, *near_values, some_gates[-1], ids)
    up_other = lax.ppermute(after(up_w, *ready), "exp", SWAP)
    down_other = lax.ppermute(after(w_down[0], *ready), "exp", SWAP)
    halves = [gate_w, gate_other, up_w, up_other, w_down[0], down_other]

    theirs, mine = attention(where, queries, ids, near_keys, near_values, out_other, gate_other)
    all_gates = gather_gates(some_gates, theirs)
    received = lax.ppermute(theirs, "exp", SWAP)
    stream, normed = project_and_norm(
        mine, received, out_weight, out_other, resid, norm_gain[None, :], up_other, down_other
    )
    mixed = expert_layer(normed, stream, jnp.stack([shard, core]), all_gates, halves)
    return mixed.astype(jnp.bfloat16)


def solution(mesh):
    in_specs = (
        P("seq", "exp"),
        P("seq", "exp"),
        P("seq", "exp"),
        P(("seq", "exp"), None),
        P(),
        P("exp", None),
        P(),
        P(("seq", "exp"), None),
        P(("seq", "exp"), None),
        P("seq", None, "exp"),
        P("seq", None, "exp"),
        P("seq", "exp", None),
    )
    out_specs = P(("seq", "exp"), None)
    return jax.shard_map(shards, mesh=mesh, in_specs=in_specs, out_specs=out_specs, check_vma=False)
```

```python
import functools
import math

import jax
import jax.numpy as jnp
from jax import lax
from jax.experimental import pallas as pl
from jax.experimental.pallas import tpu as pltpu
from jax.sharding import PartitionSpec as P

HD = 128
SWAP = [(0, 1), (1, 0)]
VMEM = pl.BlockSpec(memory_space=pltpu.VMEM)
ANY = pl.BlockSpec(memory_space=pl.ANY)
NT = (((1,), (1,)), ((), ()))


def flip(block, mask):
    count = lax.axis_size("seq")
    return lax.ppermute(block, "seq", [(i, i ^ mask) for i in range(count)])


def cross(block, masks):
    count = lax.axis_size("seq")
    pairs = [(2 * i + c, 2 * (i ^ masks[c]) + c) for i in range(count) for c in range(2)]
    return lax.ppermute(block, ("seq", "exp"), pairs)


def after(block, *arrays):
    return lax.optimization_barrier((block, *arrays))[0]


def gate_order(count):
    masks = [1 << bit for bit in range(count.bit_length() - 1)]
    return masks[2:] + masks[1::-1]


def gather_gates(pieces, *waits):
    held = jnp.concatenate(pieces, axis=1) if len(pieces) > 1 else pieces[0]
    mask = gate_order(lax.axis_size("seq"))[len(pieces) - 1]
    return [*pieces, flip(after(held, *waits) if waits else held, mask)]


def place_of(j):
    return sum(1 << bit for bit, mask in enumerate(gate_order(lax.axis_size("seq"))) if j & mask)


def attention_kernel(where_ref, q_ref, ids_ref, *refs):
    keys, values, (theirs_ref, mine_ref, both) = refs[:3], refs[3:6], refs[-3:]
    rows = q_ref.shape[0]
    some = rows // 2
    core, odd = where_ref[0], where_ref[1]
    scale = 1.0 / math.sqrt(HD)
    ids = [ids_ref[:, i * rows : (i + 1) * rows] for i in range(3)]
    column = jnp.transpose(jnp.broadcast_to(ids[1], (HD, rows)))[:, :1]
    back, front = jnp.where(odd == 1, ids[0], ids[2]), jnp.where(odd == 1, ids[2], ids[0])
    apart = lax.broadcasted_iota(jnp.int32, (rows, rows), 0) - lax.broadcasted_iota(
        jnp.int32, (rows, rows), 1
    )
    side = rows * (2 * odd - 1)
    allowed = jnp.concatenate(
        [
            (column == back) & (jnp.abs(apart + side) < rows),
            column == ids[1],
            (column == front) & (jnp.abs(apart - side) < rows),
        ],
        axis=1,
    )
    for head in range(q_ref.shape[1] // HD):
        cols = slice(head * HD, (head + 1) * HD)
        query = q_ref[:, cols]
        score = jnp.concatenate(
            [
                lax.dot_general(query, ref[:, cols], NT, preferred_element_type=jnp.float32)
                for ref in keys
            ],
            axis=1,
        )
        score = jnp.where(allowed, score * scale, -jnp.inf)
        weights = jnp.exp(score - jnp.max(score, axis=-1, keepdims=True))
        share = 1.0 / jnp.sum(weights, axis=-1, keepdims=True)
        probs = (weights * share).astype(jnp.bfloat16)
        total = jnp.zeros((rows, HD), jnp.float32)
        for i, ref in enumerate(values):
            total += jnp.dot(
                probs[:, i * rows : (i + 1) * rows], ref[:, cols], preferred_element_type=jnp.float32
            )
        both[:, cols] = total.astype(jnp.bfloat16)
    at = pl.multiple_of(core * some, some)
    mine_ref[...] = both[pl.ds(at, some), :]
    theirs_ref[...] = both[pl.ds(some - at, some), :]


def attention(where, queries, ids, near_keys, near_values, *ahead):
    rows, width = queries.shape
    half = jax.ShapeDtypeStruct((rows // 2, width), jnp.bfloat16)
    return pl.pallas_call(
        attention_kernel,
        out_shape=(half, half),
        in_specs=[pl.BlockSpec(memory_space=pltpu.SMEM)] + [VMEM] * 8 + [ANY] * len(ahead),
        out_specs=(VMEM, VMEM),
        scratch_shapes=[pltpu.VMEM((rows, width), jnp.bfloat16)],
        compiler_params=pltpu.CompilerParams(vmem_limit_bytes=63 * 1024 * 1024),
        name="window_attention",
    )(where, queries, ids, *near_keys, *near_values, *ahead)


def norm_kernel(mine_ref, theirs_ref, own_w, other_w, resid_ref, gain_ref, *refs):
    stream_ref, normed_ref = refs[-2:]
    stream = resid_ref[...].astype(jnp.float32)
    stream += jnp.dot(mine_ref[...], own_w[...], preferred_element_type=jnp.float32)
    stream += jnp.dot(theirs_ref[...], other_w[...], preferred_element_type=jnp.float32)
    meansq = jnp.mean(stream * stream, axis=-1, keepdims=True)
    stream_ref[...] = stream
    normed_ref[...] = (stream * lax.rsqrt(meansq + 1e-05) * gain_ref[...]).astype(jnp.bfloat16)


def project_and_norm(mine, theirs, own_w, other_w, resid, gain, *ahead):
    rows, width = resid.shape
    return pl.pallas_call(
        norm_kernel,
        out_shape=(
            jax.ShapeDtypeStruct((rows, width), jnp.float32),
            jax.ShapeDtypeStruct((rows, width), jnp.bfloat16),
        ),
        in_specs=[VMEM] * 6 + [ANY] * len(ahead),
        out_specs=(VMEM, VMEM),
        compiler_params=pltpu.CompilerParams(vmem_limit_bytes=63 * 1024 * 1024),
        name="project_and_norm",
    )(mine, theirs, own_w, other_w, resid, gain, *ahead)


def assemble_kernel(*refs):
    halves, (gate_up, down, sems) = refs[:6], refs[6:]
    units = halves[0].shape[0]
    copies = []
    for i, half in enumerate(halves):
        target, at = (gate_up, i * units) if i < 4 else (down, (i - 4) * units)
        copies.append(pltpu.make_async_copy(half, target.at[pl.ds(at, units), :], sems.at[i]))
    for copy in copies:
        copy.start()
    for copy in copies:
        copy.wait()


def assemble(halves):
    units, width = halves[0].shape
    return pl.pallas_call(
        assemble_kernel,
        out_shape=(
            jax.ShapeDtypeStruct((4 * units, width), jnp.bfloat16),
            jax.ShapeDtypeStruct((2 * units, width), jnp.bfloat16),
        ),
        in_specs=[ANY] * 6,
        out_specs=(VMEM, VMEM),
        scratch_shapes=[pltpu.SemaphoreType.DMA((6,))],
        compiler_params=pltpu.CompilerParams(vmem_limit_bytes=36 * 1024 * 1024),
        name="assemble_weights",
    )(*halves)


def gates_at(place, rows, pieces):
    piece = place.bit_length()
    at = (place - (1 << piece >> 1)) * rows
    return pieces[piece][:, at : at + rows]


def expert_kernel(places, pieces, where_ref, *refs):
    count = len(places)
    blocks, gates, (gate_up, down) = refs[:count], refs[count : count + pieces], refs[count + pieces :][:2]
    outs = refs[count + pieces + 2 :]
    units = down.shape[0]
    rows = blocks[0].shape[0]
    for first in range(0, count, 2):
        group = range(first, min(first + 2, count))
        tokens = jnp.concatenate([blocks[i][...] for i in group], axis=0)
        gate = lax.dot_general(tokens, gate_up[:units, :], NT, preferred_element_type=jnp.float32)
        up = lax.dot_general(tokens, gate_up[units:, :], NT, preferred_element_type=jnp.float32)
        act = (gate / (1.0 + jnp.exp(-gate)) * up).astype(jnp.bfloat16)
        result = jnp.dot(act, down[...], preferred_element_type=jnp.float32)
        for i in group:
            here = gates_at(places[i][0], rows, gates)
            if places[i][0] != places[i][1]:
                here = jnp.where(where_ref[1] == 1, gates_at(places[i][1], rows, gates), here)
            expert = lax.broadcasted_iota(jnp.int32, here.shape, 0)
            chosen = jnp.sum(jnp.where(expert == where_ref[0], here, 0.0), axis=0, keepdims=True)
            chosen = jnp.transpose(jnp.broadcast_to(chosen, (rows, rows)))[:, :1]
            part = result[(i - first) * rows : (i - first + 1) * rows]
            outs[i][...] = (part * chosen).astype(jnp.bfloat16)


def expert(blocks, places, where, gates, weights):
    rows, width = blocks[0].shape
    count = len(blocks)
    return pl.pallas_call(
        functools.partial(expert_kernel, places, len(gates)),
        out_shape=[jax.ShapeDtypeStruct((rows, width), jnp.bfloat16)] * count,
        in_specs=[pl.BlockSpec(memory_space=pltpu.SMEM)] + [VMEM] * (count + len(gates) + 2),
        out_specs=[VMEM] * count,
        compiler_params=pltpu.CompilerParams(vmem_limit_bytes=36 * 1024 * 1024),
        name="expert_rows",
    )(where, *blocks, *gates, *weights)


def add(*terms):
    total = terms[0].astype(jnp.float32)
    for term in terms[1:]:
        total = total + term.astype(jnp.float32)
    return total


def add_small(*terms):
    return add(*terms).astype(jnp.bfloat16)


def shift(block, pairs):
    return lax.ppermute(block, "seq", [(4 * a + i, 4 * b + i) for a, b in pairs for i in range(4)])


OUTWARD, INWARD, MIDDLE = [(1, 0), (2, 3)], [(0, 1), (3, 2)], [(1, 2), (2, 1)]
X, Y = (1, 2), (2, 1)


def step_layer(normed, stream, run, weights):
    z = lax.axis_index("seq") // 4
    inner = (z == 1) | (z == 2)

    o0 = normed
    o1, near3, x0, y0 = flip(o0, 4), shift(o0, MIDDLE), cross(o0, X), cross(o0, Y)
    weights = weights(x0, y0)

    ends2, near2 = shift(near3, OUTWARD), shift(o1, MIDDLE)
    d0, y1 = cross(after(y0, x0), X), cross(after(o1, y0), Y)

    ends3 = shift(near2, OUTWARD)
    o2 = jnp.where(inner, near2, ends2)
    x2, y2 = cross(after(o2, d0, weights[0]), X), cross(after(o2, y1, weights[0]), Y)
    run = functools.partial(run, weights)
    p0, px0, py0, pd0 = run([after(o0, o2), x0, y0, d0], (0, X, Y, 3))

    x1 = flip(after(x0, ends3, p0), 4)
    o3 = jnp.where(inner, near3, ends3)
    x3, y3 = cross(after(o3, x2, p0), X), cross(after(o3, y2, p0), Y)
    p1, py1, p2, px2, py2, p3 = run(
        [after(o1, p0), y1, o2, x2, y2, o3], (4, plane(Y, 4), 8, plane(X, 8), plane(Y, 8), 12)
    )

    d1 = flip(after(d0, x1, p1), 4)
    d2, d3 = cross(after(y2, x3, p1), X), cross(after(x3, y3, p1), Y)
    px3, py3, px1 = run([after(x3, p1), y3, x1], (plane(X, 12), plane(Y, 12), plane(X, 4)))

    to_x0 = flip(after(px1, d1), 4)
    pd2, pd3 = run([after(d2, px3), d3], (11, 15))
    (pd1,) = run([after(d1, pd2)], (7,))
    to_x3, to_y2, to_d0 = cross(pd3, Y), cross(pd2, X), flip(after(pd1, to_x0), 4)

    px3, py2, px0 = add_small(px3, to_x3), add_small(py2, to_y2), add_small(px0, to_x0)
    by_x, by_y = cross(after(px3, to_y2), X), cross(after(py3, to_x3), Y)

    p3, pd0 = add_small(p3, by_x, by_y), add_small(pd0, to_d0)
    to_2 = shift(after(p3, to_d0), INWARD)
    by_x, by_y = cross(after(px2, by_x), X), cross(after(py2, by_y), Y)

    p2 = add_small(p2, by_x, by_y, to_2)
    to_3, to_1 = shift(after(p2, to_2), INWARD), shift(p2, MIDDLE)
    to_y0, by_y = cross(after(pd0, by_x), X), cross(after(py1, by_y), Y)

    p1, py0 = add_small(p1, by_y, to_1), add_small(py0, to_y0)
    p3 = add_small(after(p3, p1), to_3)
    by_z, by_middle = flip(after(p1, to_3), 4), shift(p3, MIDDLE)
    by_x, by_y = cross(after(px0, to_y0), X), cross(after(py0, by_y), Y)
    most = after(add(stream, p0, by_x, by_y, by_z))
    return add(most, by_middle)


def plane(masks, distance):
    return tuple(mask + distance for mask in masks)


def expert_layer(normed, stream, where, gates, halves):
    count = lax.axis_size("seq")

    def weights(*waits):
        return assemble([after(half, *waits) for half in halves])

    def run(weights, blocks, masks):
        masks = [mask if isinstance(mask, tuple) else (mask, mask) for mask in masks]
        places = tuple(tuple(place_of(j) for j in mask) for mask in masks)
        return expert(blocks, places, where, gates, weights)

    if count == 16:
        return step_layer(normed, stream, run, weights)
    held = weights()
    blocks, mask = [normed], 1
    while mask < count:
        blocks = blocks + [flip(block, mask) for block in blocks]
        mask *= 2
    parts = []
    for first in range(0, count, 4):
        parts += run(held, blocks[first : first + 4], range(first, first + 4))
    while mask > 1:
        mask //= 2
        parts = [add_small(parts[i], flip(parts[i + mask], mask)) for i in range(mask)]
    return add(stream, parts[0])


def shards(
    queries,
    keys,
    values,
    resid,
    pair_ids,
    out_weight,
    norm_gain,
    experts,
    gates,
    w_gate,
    w_up,
    w_down,
):
    tok_rows = queries.shape[0]
    moe_rows = resid.shape[0]
    shard = lax.axis_index("seq")
    core = lax.axis_index("exp")
    count = lax.axis_size("seq")

    def halo(part):
        beside = flip(part, 1)
        ahead = [(i, i + 2) for i in range(0, count - 2, 2)]
        back = [(i + 2, i) for i in range(1, count - 2, 2)]
        return beside, part, lax.ppermute(beside, "seq", ahead + back)

    near_keys, near_values = halo(keys), halo(values)
    chosen = experts.T[:, None, :] == jnp.arange(count, dtype=jnp.int32)[None, :, None]
    some_gates = [jnp.sum(jnp.where(chosen, gates.T[:, None, :], 0.0), axis=0)]
    while len(some_gates) < count.bit_length() - 1:
        some_gates = gather_gates(some_gates)
    id_pad = jnp.pad(pair_ids, (tok_rows, tok_rows), constant_values=-1)
    ids = lax.dynamic_slice_in_dim(id_pad, shard * tok_rows, 3 * tok_rows, 0)[None, :]
    out_other = lax.ppermute(out_weight, "exp", SWAP)
    gate_w, up_w = jnp.swapaxes(w_gate[0], 0, 1), jnp.swapaxes(w_up[0], 0, 1)
    gate_other = lax.ppermute(gate_w, "exp", SWAP)
    where = jnp.stack([core, shard % 2])
    ready = (where, *near_keys, *near_values, some_gates[-1], ids)
    up_other = lax.ppermute(after(up_w, *ready), "exp", SWAP)
    down_other = lax.ppermute(after(w_down[0], *ready), "exp", SWAP)
    halves = [gate_w, gate_other, up_w, up_other, w_down[0], down_other]

    theirs, mine = attention(where, queries, ids, near_keys, near_values, out_other, gate_other)
    all_gates = gather_gates(some_gates, theirs)
    received = lax.ppermute(theirs, "exp", SWAP)
    stream, normed = project_and_norm(
        mine, received, out_weight, out_other, resid, norm_gain[None, :], up_other, down_other
    )
    mixed = expert_layer(normed, stream, jnp.stack([shard, core]), all_gates, halves)
    return mixed.astype(jnp.bfloat16)


def solution(mesh):
    in_specs = (
        P("seq", "exp"),
        P("seq", "exp"),
        P("seq", "exp"),
        P(("seq", "exp"), None),
        P(),
        P("exp", None),
        P(),
        P(("seq", "exp"), None),
        P(("seq", "exp"), None),
        P("seq", None, "exp"),
        P("seq", None, "exp"),
        P("seq", "exp", None),
    )
    out_specs = P(("seq", "exp"), None)
    return jax.shard_map(shards, mesh=mesh, in_specs=in_specs, out_specs=out_specs, check_vma=False)
```

```python
import functools
import math

import jax
import jax.numpy as jnp
from jax import lax
from jax.experimental import pallas as pl
from jax.experimental.pallas import tpu as pltpu
from jax.sharding import PartitionSpec as P

HD = 128
SWAP = [(0, 1), (1, 0)]
VMEM = pl.BlockSpec(memory_space=pltpu.VMEM)
ANY = pl.BlockSpec(memory_space=pl.ANY)
NT = (((1,), (1,)), ((), ()))


def flip(block, mask):
    count = lax.axis_size("seq")
    return lax.ppermute(block, "seq", [(i, i ^ mask) for i in range(count)])


def cross(block, masks):
    count = lax.axis_size("seq")
    pairs = [(2 * i + c, 2 * (i ^ masks[c]) + c) for i in range(count) for c in range(2)]
    return lax.ppermute(block, ("seq", "exp"), pairs)


def after(block, *arrays):
    return lax.optimization_barrier((block, *arrays))[0]


def gate_order(count):
    masks = [1 << bit for bit in range(count.bit_length() - 1)]
    return masks[2:] + masks[1::-1]


def gather_gates(pieces, *waits):
    held = jnp.concatenate(pieces, axis=1) if len(pieces) > 1 else pieces[0]
    mask = gate_order(lax.axis_size("seq"))[len(pieces) - 1]
    return [*pieces, flip(after(held, *waits) if waits else held, mask)]


def place_of(j):
    return sum(1 << bit for bit, mask in enumerate(gate_order(lax.axis_size("seq"))) if j & mask)


def attention_kernel(where_ref, q_ref, ids_ref, *refs):
    keys, values, (theirs_ref, mine_ref, both) = refs[:3], refs[3:6], refs[-3:]
    rows = q_ref.shape[0]
    some = rows // 2
    core, odd = where_ref[0], where_ref[1]
    scale = 1.0 / math.sqrt(HD)
    ids = [ids_ref[:, i * rows : (i + 1) * rows] for i in range(3)]
    column = jnp.transpose(jnp.broadcast_to(ids[1], (HD, rows)))[:, :1]
    back, front = jnp.where(odd == 1, ids[0], ids[2]), jnp.where(odd == 1, ids[2], ids[0])
    apart = lax.broadcasted_iota(jnp.int32, (rows, rows), 0) - lax.broadcasted_iota(
        jnp.int32, (rows, rows), 1
    )
    side = rows * (2 * odd - 1)
    allowed = jnp.concatenate(
        [
            (column == back) & (jnp.abs(apart + side) < rows),
            column == ids[1],
            (column == front) & (jnp.abs(apart - side) < rows),
        ],
        axis=1,
    )
    for head in range(q_ref.shape[1] // HD):
        cols = slice(head * HD, (head + 1) * HD)
        query = q_ref[:, cols]
        score = jnp.concatenate(
            [
                lax.dot_general(query, ref[:, cols], NT, preferred_element_type=jnp.float32)
                for ref in keys
            ],
            axis=1,
        )
        score = jnp.where(allowed, score * scale, -jnp.inf)
        weights = jnp.exp(score - jnp.max(score, axis=-1, keepdims=True))
        share = 1.0 / jnp.sum(weights, axis=-1, keepdims=True)
        probs = (weights * share).astype(jnp.bfloat16)
        total = jnp.zeros((rows, HD), jnp.float32)
        for i, ref in enumerate(values):
            total += jnp.dot(
                probs[:, i * rows : (i + 1) * rows], ref[:, cols], preferred_element_type=jnp.float32
            )
        both[:, cols] = total.astype(jnp.bfloat16)
    at = pl.multiple_of(core * some, some)
    mine_ref[...] = both[pl.ds(at, some), :]
    theirs_ref[...] = both[pl.ds(some - at, some), :]


def attention(where, queries, ids, near_keys, near_values, *ahead):
    rows, width = queries.shape
    half = jax.ShapeDtypeStruct((rows // 2, width), jnp.bfloat16)
    return pl.pallas_call(
        attention_kernel,
        out_shape=(half, half),
        in_specs=[pl.BlockSpec(memory_space=pltpu.SMEM)] + [VMEM] * 8 + [ANY] * len(ahead),
        out_specs=(VMEM, VMEM),
        scratch_shapes=[pltpu.VMEM((rows, width), jnp.bfloat16)],
        compiler_params=pltpu.CompilerParams(vmem_limit_bytes=63 * 1024 * 1024),
        name="window_attention",
    )(where, queries, ids, *near_keys, *near_values, *ahead)


def norm_kernel(mine_ref, theirs_ref, own_w, other_w, resid_ref, gain_ref, *refs):
    stream_ref, normed_ref = refs[-2:]
    stream = resid_ref[...].astype(jnp.float32)
    stream += jnp.dot(mine_ref[...], own_w[...], preferred_element_type=jnp.float32)
    stream += jnp.dot(theirs_ref[...], other_w[...], preferred_element_type=jnp.float32)
    meansq = jnp.mean(stream * stream, axis=-1, keepdims=True)
    stream_ref[...] = stream
    normed_ref[...] = (stream * lax.rsqrt(meansq + 1e-05) * gain_ref[...]).astype(jnp.bfloat16)


def project_and_norm(mine, theirs, own_w, other_w, resid, gain, *ahead):
    rows, width = resid.shape
    return pl.pallas_call(
        norm_kernel,
        out_shape=(
            jax.ShapeDtypeStruct((rows, width), jnp.float32),
            jax.ShapeDtypeStruct((rows, width), jnp.bfloat16),
        ),
        in_specs=[VMEM] * 6 + [ANY] * len(ahead),
        out_specs=(VMEM, VMEM),
        compiler_params=pltpu.CompilerParams(vmem_limit_bytes=63 * 1024 * 1024),
        name="project_and_norm",
    )(mine, theirs, own_w, other_w, resid, gain, *ahead)


def assemble_kernel(*refs):
    halves, (gate_up, down, sems) = refs[:6], refs[6:]
    units = halves[0].shape[0]
    copies = []
    for i, half in enumerate(halves):
        target, at = (gate_up, i * units) if i < 4 else (down, (i - 4) * units)
        copies.append(pltpu.make_async_copy(half, target.at[pl.ds(at, units), :], sems.at[i]))
    for copy in copies:
        copy.start()
    for copy in copies:
        copy.wait()


def assemble(halves):
    units, width = halves[0].shape
    return pl.pallas_call(
        assemble_kernel,
        out_shape=(
            jax.ShapeDtypeStruct((4 * units, width), jnp.bfloat16),
            jax.ShapeDtypeStruct((2 * units, width), jnp.bfloat16),
        ),
        in_specs=[ANY] * 6,
        out_specs=(VMEM, VMEM),
        scratch_shapes=[pltpu.SemaphoreType.DMA((6,))],
        compiler_params=pltpu.CompilerParams(vmem_limit_bytes=36 * 1024 * 1024),
        name="assemble_weights",
    )(*halves)


def own_gates_kernel(where_ref, *refs):
    at = 0
    for piece in refs[:-1]:
        expert = lax.broadcasted_iota(jnp.int32, piece.shape, 0)
        chosen = jnp.where(expert == where_ref[0], piece[...], 0.0)
        refs[-1][:, at : at + piece.shape[1]] = jnp.sum(chosen, axis=0, keepdims=True)
        at += piece.shape[1]


def own_gates(where, pieces):
    width = sum(piece.shape[1] for piece in pieces)
    return pl.pallas_call(
        own_gates_kernel,
        out_shape=jax.ShapeDtypeStruct((1, width), jnp.float32),
        in_specs=[pl.BlockSpec(memory_space=pltpu.SMEM)] + [VMEM] * len(pieces),
        out_specs=VMEM,
        compiler_params=pltpu.CompilerParams(vmem_limit_bytes=8 * 1024 * 1024),
        name="own_gates",
    )(where, *pieces)


def expert_kernel(places, where_ref, *refs):
    count = len(places)
    blocks, (gates, gate_up, down), outs = refs[:count], refs[count : count + 3], refs[count + 3 :]
    units = down.shape[0]
    rows = blocks[0].shape[0]
    for first in range(0, count, 2):
        group = range(first, min(first + 2, count))
        tokens = jnp.concatenate([blocks[i][...] for i in group], axis=0)
        gate = lax.dot_general(tokens, gate_up[:units, :], NT, preferred_element_type=jnp.float32)
        up = lax.dot_general(tokens, gate_up[units:, :], NT, preferred_element_type=jnp.float32)
        act = (gate / (1.0 + jnp.exp(-gate)) * up).astype(jnp.bfloat16)
        result = jnp.dot(act, down[...], preferred_element_type=jnp.float32)
        for i in group:
            chosen = gates[:, places[i][0] * rows : (places[i][0] + 1) * rows]
            if places[i][0] != places[i][1]:
                other = gates[:, places[i][1] * rows : (places[i][1] + 1) * rows]
                chosen = jnp.where(where_ref[1] == 1, other, chosen)
            chosen = jnp.transpose(jnp.broadcast_to(chosen, (rows, rows)))[:, :1]
            part = result[(i - first) * rows : (i - first + 1) * rows]
            outs[i][...] = (part * chosen).astype(jnp.bfloat16)


def expert(blocks, places, where, gates, weights):
    rows, width = blocks[0].shape
    count = len(blocks)
    return pl.pallas_call(
        functools.partial(expert_kernel, places),
        out_shape=[jax.ShapeDtypeStruct((rows, width), jnp.bfloat16)] * count,
        in_specs=[pl.BlockSpec(memory_space=pltpu.SMEM)] + [VMEM] * (count + 3),
        out_specs=[VMEM] * count,
        compiler_params=pltpu.CompilerParams(vmem_limit_bytes=36 * 1024 * 1024),
        name="expert_rows",
    )(where, *blocks, gates, *weights)


def add(*terms):
    total = terms[0].astype(jnp.float32)
    for term in terms[1:]:
        total = total + term.astype(jnp.float32)
    return total


def add_small(*terms):
    return add(*terms).astype(jnp.bfloat16)


def shift(block, pairs):
    return lax.ppermute(block, "seq", [(4 * a + i, 4 * b + i) for a, b in pairs for i in range(4)])


OUTWARD, INWARD, MIDDLE = [(1, 0), (2, 3)], [(0, 1), (3, 2)], [(1, 2), (2, 1)]
X, Y = (1, 2), (2, 1)


def step_layer(normed, stream, run, weights):
    z = lax.axis_index("seq") // 4
    inner = (z == 1) | (z == 2)

    o0 = normed
    o1, near3, x0, y0 = flip(o0, 4), shift(o0, MIDDLE), cross(o0, X), cross(o0, Y)
    weights = weights(x0, y0)

    ends2, near2 = shift(near3, OUTWARD), shift(o1, MIDDLE)
    d0, y1 = cross(after(y0, x0), X), cross(after(o1, y0), Y)

    ends3 = shift(near2, OUTWARD)
    o2 = jnp.where(inner, near2, ends2)
    x2, y2 = cross(after(o2, d0, weights[0]), X), cross(after(o2, y1, weights[0]), Y)
    run = functools.partial(run, weights)
    p0, px0, py0, pd0 = run([after(o0, o2), x0, y0, d0], (0, X, Y, 3))

    x1 = flip(after(x0, ends3, p0), 4)
    o3 = jnp.where(inner, near3, ends3)
    x3, y3 = cross(after(o3, x2, p0), X), cross(after(o3, y2, p0), Y)
    p1, py1, p2, px2, py2, p3 = run(
        [after(o1, p0), y1, o2, x2, y2, o3], (4, plane(Y, 4), 8, plane(X, 8), plane(Y, 8), 12)
    )

    d1 = flip(after(d0, x1, p1), 4)
    d2, d3 = cross(after(y2, x3, p1), X), cross(after(x3, y3, p1), Y)
    px3, py3, px1 = run([after(x3, p1), y3, x1], (plane(X, 12), plane(Y, 12), plane(X, 4)))

    to_x0 = flip(after(px1, d1), 4)
    pd2, pd3 = run([after(d2, px3), d3], (11, 15))
    (pd1,) = run([after(d1, pd2)], (7,))
    to_x3, to_y2, to_d0 = cross(pd3, Y), cross(pd2, X), flip(after(pd1, to_x0), 4)

    px3, py2, px0 = add_small(px3, to_x3), add_small(py2, to_y2), add_small(px0, to_x0)
    by_x, by_y = cross(after(px3, to_y2), X), cross(after(py3, to_x3), Y)

    p3, pd0 = add_small(p3, by_x, by_y), add_small(pd0, to_d0)
    to_2 = shift(after(p3, to_d0), INWARD)
    by_x, by_y = cross(after(px2, by_x), X), cross(after(py2, by_y), Y)

    p2 = add_small(p2, by_x, by_y, to_2)
    to_3, to_1 = shift(after(p2, to_2), INWARD), shift(p2, MIDDLE)
    to_y0, by_y = cross(after(pd0, by_x), X), cross(after(py1, by_y), Y)

    p1, py0 = add_small(p1, by_y, to_1), add_small(py0, to_y0)
    p3 = add_small(after(p3, p1), to_3)
    by_z, by_middle = flip(after(p1, to_3), 4), shift(p3, MIDDLE)
    by_x, by_y = cross(after(px0, to_y0), X), cross(after(py0, by_y), Y)
    return add(stream, p0, by_z, by_middle, by_x, by_y)


def plane(masks, distance):
    return tuple(mask + distance for mask in masks)


def expert_layer(normed, stream, where, gates, halves):
    count = lax.axis_size("seq")

    def weights(*waits):
        return assemble([after(half, *waits) for half in halves])

    row = own_gates(where, gates)

    def run(weights, blocks, masks):
        masks = [mask if isinstance(mask, tuple) else (mask, mask) for mask in masks]
        places = tuple(tuple(place_of(j) for j in mask) for mask in masks)
        return expert(blocks, places, where, row, weights)

    if count == 16:
        return step_layer(normed, stream, run, weights)
    held = weights()
    blocks, mask = [normed], 1
    while mask < count:
        blocks = blocks + [flip(block, mask) for block in blocks]
        mask *= 2
    parts = []
    for first in range(0, count, 4):
        parts += run(held, blocks[first : first + 4], range(first, first + 4))
    while mask > 1:
        mask //= 2
        parts = [add_small(parts[i], flip(parts[i + mask], mask)) for i in range(mask)]
    return add(stream, parts[0])


def shards(
    queries,
    keys,
    values,
    resid,
    pair_ids,
    out_weight,
    norm_gain,
    experts,
    gates,
    w_gate,
    w_up,
    w_down,
):
    tok_rows = queries.shape[0]
    moe_rows = resid.shape[0]
    shard = lax.axis_index("seq")
    core = lax.axis_index("exp")
    count = lax.axis_size("seq")

    def halo(part):
        beside = flip(part, 1)
        ahead = [(i, i + 2) for i in range(0, count - 2, 2)]
        back = [(i + 2, i) for i in range(1, count - 2, 2)]
        return beside, part, lax.ppermute(beside, "seq", ahead + back)

    near_keys, near_values = halo(keys), halo(values)
    chosen = experts.T[:, None, :] == jnp.arange(count, dtype=jnp.int32)[None, :, None]
    some_gates = [jnp.sum(jnp.where(chosen, gates.T[:, None, :], 0.0), axis=0)]
    while len(some_gates) < count.bit_length() - 1:
        some_gates = gather_gates(some_gates)
    id_pad = jnp.pad(pair_ids, (tok_rows, tok_rows), constant_values=-1)
    ids = lax.dynamic_slice_in_dim(id_pad, shard * tok_rows, 3 * tok_rows, 0)[None, :]
    out_other = lax.ppermute(out_weight, "exp", SWAP)
    gate_w, up_w = jnp.swapaxes(w_gate[0], 0, 1), jnp.swapaxes(w_up[0], 0, 1)
    gate_other = lax.ppermute(gate_w, "exp", SWAP)
    where = jnp.stack([core, shard % 2])
    ready = (where, *near_keys, *near_values, some_gates[-1], ids)
    up_other = lax.ppermute(after(up_w, *ready), "exp", SWAP)
    down_other = lax.ppermute(after(w_down[0], *ready), "exp", SWAP)
    halves = [gate_w, gate_other, up_w, up_other, w_down[0], down_other]

    theirs, mine = attention(where, queries, ids, near_keys, near_values, out_other, gate_other)
    all_gates = gather_gates(some_gates, theirs)
    received = lax.ppermute(theirs, "exp", SWAP)
    stream, normed = project_and_norm(
        mine, received, out_weight, out_other, resid, norm_gain[None, :], up_other, down_other
    )
    mixed = expert_layer(normed, stream, jnp.stack([shard, core]), all_gates, halves)
    return mixed.astype(jnp.bfloat16)


def solution(mesh):
    in_specs = (
        P("seq", "exp"),
        P("seq", "exp"),
        P("seq", "exp"),
        P(("seq", "exp"), None),
        P(),
        P("exp", None),
        P(),
        P(("seq", "exp"), None),
        P(("seq", "exp"), None),
        P("seq", None, "exp"),
        P("seq", None, "exp"),
        P("seq", "exp", None),
    )
    out_specs = P(("seq", "exp"), None)
    return jax.shard_map(shards, mesh=mesh, in_specs=in_specs, out_specs=out_specs, check_vma=False)
```
